512 devices in a mesh: dp: 16 (over x_lo, y, core), tensor: 32 (over x_hi, z).
Axes of the slice: x: 4 (x_hi: 2, x_lo: 2; x = x_hi * 2 + x_lo), y: 4, z: 16, core: 2. Of those that a mesh axis runs over, the one named last changes fastest.
Arguments:
- queries: bfloat16 [256, 128, 4096], P('dp', None, 'tensor'), may hold values from -6 to 6
- keys_values: bfloat16 [256, 128, 1024], P('dp', 'tensor'), may hold values from -6 to 6
- grad_out: bfloat16 [256, 128, 4096], P('dp', None, 'tensor'), may hold values from -6 to 6
- send_tiles: int32 [16, 16, 2], P('dp'), may hold values from 0 to 15, as said below
- recv_slot: int32 [16, 16], replicated, may hold values from 0 to 31, as said below
- tile_seq: int32 [16, 16], P('dp'), may hold values from 0 to 5, never falling along the last dimension, each value on 1 to 8 neighbouring positions
Outputs:
- grad_queries: bfloat16 [256, 128, 4096], P('dp', None, 'tensor')
- grad_keys_values: bfloat16 [256, 128, 1024], P('dp', 'tensor')
The draws below stay inside these ranges and needn't reach their ends.
Inputs may be any that keep to these rules, and one draw needn't show every extreme that they name: Every tile of shard s is named by exactly one used slot send_tiles[s, d, c]; slots that no recv_slot entry names hold 0. Which slots are used from shard s to replica d depends only on (s - d) mod 16; used slots of one pair run from c = 0 upward, and some pair uses all 2. recv_slot is consistent with send_tiles: entry s * 2 + c names shard s's slot c towards replica d; each replica's row names distinct slots, and 2 is reached.
All inputs are finite; a program needn't handle non-finite values.
Results may differ from the reference program's by a relative error of at most 0.0072.
Values may be sent and summed in bfloat16 or wider, within the bound.
No kernel may reach another device: no remote copies, remote signals or barrier semaphores. Data moves between devices by JAX's collectives and lax.ppermute only.
A program may use at most 64 MiB of HBM per device.

```python
import math
import jax
import jax.numpy as jnp
import numpy as np
from jax import lax

HD = 128
H = 32
KV = 4
TILE = 128
TILES = 16
CAP = 2
ALL_TILES = 256
N_DP = 16


def place_first(order, wanted, slot):
    where_now = jnp.argmax(order == wanted).astype(jnp.int32)
    current = order[slot]
    return order.at[where_now].set(current).at[slot].set(wanted)


def route_pattern(key):
    key_cut, key_perm = jax.random.split(key)
    coins = jax.random.randint(key_cut, (TILES,), 0, 2, dtype=jnp.int32)
    places = jnp.arange(TILES, dtype=jnp.int32)

    def advance(state, inputs):
        run_length, part_total = state
        place, coin = inputs
        remaining = TILES - place
        forced = run_length == CAP
        allowed = part_total + (remaining + CAP - 1) // CAP <= N_DP
        cut = (place >= CAP) & (forced | (coin == 1) & allowed)
        part_index = jnp.where(cut, part_total, part_total - 1)
        run_next = jnp.where(cut, 1, run_length + 1).astype(jnp.int32)
        total_next = (part_total + cut.astype(jnp.int32)).astype(jnp.int32)
        return ((run_next, total_next), (part_index.astype(jnp.int32), (run_next - 1).astype(jnp.int32)))
    start_state = (jnp.int32(0), jnp.int32(1))
    final_state, outputs = lax.scan(advance, start_state, (places, coins))
    part_of, rank_of = outputs
    order = jax.random.permutation(key_perm, N_DP).astype(jnp.int32)
    order = place_first(order, jnp.int32(N_DP // 2), 0)
    if N_DP > 2:
        order = place_first(order, jnp.int32(1), 1)
    return (order[part_of], rank_of)


def draw_queries(key, part):
    key = jax.random.fold_in(key, 11)
    values = jax.random.normal(key, (N_DP * TILES, TILE, H * HD), jnp.float32)
    return jnp.clip(values, -6.0, 6.0).astype(jnp.bfloat16)


def draw_keys_values(key, part):
    key = jax.random.fold_in(key, 13)
    values = jax.random.normal(key, (N_DP * TILES, TILE, 2 * KV * HD), jnp.float32)
    return jnp.clip(values, -6.0, 6.0).astype(jnp.bfloat16)


def draw_send_tiles(key, part):
    offset_of, rank_of = route_pattern(key)
    shard_ids = jnp.arange(N_DP, dtype=jnp.int32)
    shard_gap = (shard_ids[:, None] - shard_ids[None, :]) % N_DP
    slot_ids = jnp.arange(CAP, dtype=jnp.int32)
    matched = (offset_of[None, None, None, :] == shard_gap[:, :, None, None]) & (rank_of[None, None, None, :] == slot_ids[None, None, :, None])
    return jnp.sum(jnp.where(matched, jnp.arange(TILES, dtype=jnp.int32), 0), axis=3).astype(jnp.int32)


def draw_recv_slot(key, part):
    offset_of, rank_of = route_pattern(key)
    replica_ids = jnp.arange(N_DP, dtype=jnp.int32)
    source_ids = (replica_ids[:, None] + offset_of[None, :]) % N_DP
    return (source_ids * CAP + rank_of[None, :]).astype(jnp.int32)


def steps_of(own_key, dims, cuts, least, high):
    loudness = 1.0
    for position, parts in cuts:
        heights = jax.random.uniform(jax.random.fold_in(jax.random.fold_in(own_key, 6), position), (parts,), jnp.float32, least / len(cuts), high / len(cuts))
        loudness = loudness * jnp.repeat(jnp.exp(heights), dims[position] // parts).reshape((-1,) + (1,) * (len(dims) - 1 - position))
    return loudness


def split_up(amount, total, most, lean):
    weights = [(1 << 20) // math.isqrt(grade ** lean) + 1 for grade in range(2, amount + 1)]
    rest, holding = total - most - (amount - 1), [1] * (amount - 1)
    while rest > 0:
        candidates = [i for i in range(amount - 1) if holding[i] < most]
        whole, budget = sum([weights[i] for i in candidates]), rest
        for i in candidates:
            addition = min(most - holding[i], max(1, budget * weights[i] // whole), rest)
            holding[i] = holding[i] + addition
            rest = rest - addition
    return np.array([most] + holding)


def uneven_parts(own_key, amount, total, most, slope):
    if amount == 2:
        one = jax.random.randint(own_key, (), max(1, total - most), min(most, total - 1) + 1)
        return jnp.stack([one, total - one])
    sizes = jnp.asarray(split_up(amount, total, most, slope), jnp.int32)
    twos = (amount - 1) // 2
    giver, taker = sizes[1:1 + 2 * twos:2], sizes[2:2 + 2 * twos:2]
    room = jnp.minimum(giver - 1, most - taker)
    passed = jax.random.randint(jax.random.fold_in(own_key, 1), (twos,), 0, 1 << 20) % (room + 1)
    sizes = sizes.at[1:1 + 2 * twos:2].set(giver - passed).at[2:2 + 2 * twos:2].set(taker + passed)
    return sizes[jax.random.permutation(jax.random.fold_in(own_key, 2), amount)]


def noise(stream_key, dims, scale, limit, cuts=(), held_as=jnp.bfloat16):
    array = jax.random.normal(stream_key, dims, jnp.float32) * scale
    if len(cuts) > 0:
        array = steps_of(stream_key, dims, cuts, -0.22, 0.18) * array
    return jnp.clip(array, min=-limit, max=limit).astype(held_as)


def setup_inputs(seed: int = 0) -> dict:
    seeds = jax.random.split(jax.random.key(seed), 7)
    return {
        "queries": draw_queries(jax.random.fold_in(seeds[6], 71), 0),
        "keys_values": draw_keys_values(jax.random.fold_in(seeds[6], 71), 0),
        "grad_out": noise(seeds[2], (ALL_TILES, TILE, H * HD), 1.0, 6.0, ((0, 16), (2, 32))),
        "send_tiles": draw_send_tiles(jax.random.fold_in(seeds[6], 71), 0),
        "recv_slot": draw_recv_slot(jax.random.fold_in(seeds[6], 71), 0),
        "tile_seq": jax.vmap(lambda own: jnp.searchsorted(jnp.cumsum(uneven_parts(own, TILES // 4 + 2, TILES, TILES // 2, 2)), jnp.arange(TILES), side="right"))(jax.random.split(seeds[5], N_DP)).reshape((N_DP, TILES)).astype(jnp.int32),
    }


def head_backward(query_head, grad_head, key_head, value_head, allowed):
    scaling = HD ** -0.5
    scores = jnp.dot(query_head, key_head.T, preferred_element_type=jnp.float32) * scaling
    scores = jnp.where(allowed, scores, -jnp.inf)
    row_peak = jnp.max(scores, axis=-1, keepdims=True)
    weights = jnp.exp(scores - row_peak)
    attn_probs = weights / jnp.sum(weights, axis=-1, keepdims=True)
    probs_low = attn_probs.astype(jnp.bfloat16)
    grad_probs = jnp.dot(grad_head, value_head.T, preferred_element_type=jnp.float32)
    row_delta = jnp.sum(attn_probs * grad_probs, axis=-1, keepdims=True)
    grad_scores = (attn_probs * (grad_probs - row_delta)).astype(jnp.bfloat16)
    grad_query = (jnp.dot(grad_scores, key_head, preferred_element_type=jnp.float32) * scaling).astype(jnp.bfloat16)
    grad_key = jnp.dot(grad_scores.T, query_head, preferred_element_type=jnp.float32) * scaling
    grad_value = jnp.dot(probs_low.T, grad_head, preferred_element_type=jnp.float32)
    return grad_query, grad_key, grad_value


def replica_backward(inputs):
    query_rows, grad_rows, kv_rows, seq_ids = inputs
    row_count = query_rows.shape[0]
    group_size = H // KV
    seq_rows = jnp.repeat(seq_ids, TILE)
    positions = jnp.arange(row_count)
    allowed = (seq_rows[:, None] == seq_rows[None, :]) & (positions[None, :] <= positions[:, None])
    query_groups = query_rows.reshape(row_count, KV, group_size, HD).transpose(1, 2, 0, 3)
    grad_groups = grad_rows.reshape(row_count, KV, group_size, HD).transpose(1, 2, 0, 3)
    kv_split = kv_rows.reshape(row_count, 2, KV, HD).transpose(1, 2, 0, 3)

    def per_group(group_inputs):
        query_group, grad_group, key_head, value_head = group_inputs

        def per_head(totals, head_inputs):
            query_head, grad_head = head_inputs
            grad_query, grad_key, grad_value = head_backward(query_head, grad_head, key_head, value_head, allowed)
            return (totals[0] + grad_key, totals[1] + grad_value), grad_query

        zeros = jnp.zeros((row_count, HD), jnp.float32)
        sums, grad_queries = lax.scan(per_head, (zeros, zeros), (query_group, grad_group))
        return grad_queries, sums[0].astype(jnp.bfloat16), sums[1].astype(jnp.bfloat16)

    grad_queries, grad_keys, grad_values = lax.map(per_group, (query_groups, grad_groups, kv_split[0], kv_split[1]))
    grad_q = grad_queries.transpose(2, 0, 1, 3).reshape(row_count, H * HD)
    grad_kv = jnp.stack([grad_keys, grad_values]).transpose(2, 0, 1, 3).reshape(row_count, 2 * KV * HD)
    return grad_q, grad_kv


def reference(queries, keys_values, grad_out, send_tiles, recv_slot, tile_seq):
    source = (recv_slot // CAP).astype(jnp.int32)
    slot_of = (recv_slot % CAP).astype(jnp.int32)
    replica = jnp.arange(N_DP, dtype=jnp.int32)[:, None]
    source_tile = send_tiles[source, replica, slot_of]
    tile_order = (source * TILES + source_tile).astype(jnp.int32).reshape(-1)

    def to_replicas(values):
        return values[tile_order].reshape(N_DP, TILES * TILE, values.shape[-1])

    grad_q, grad_kv = lax.map(replica_backward, (to_replicas(queries), to_replicas(grad_out), to_replicas(keys_values), tile_seq))
    grad_queries = jnp.zeros_like(queries).at[tile_order].set(grad_q.reshape(N_DP * TILES, TILE, H * HD))
    grad_keys_values = jnp.zeros_like(keys_values).at[tile_order].set(grad_kv.reshape(N_DP * TILES, TILE, 2 * KV * HD))
    return grad_queries, grad_keys_values
```

```python
import functools

import jax
import jax.numpy as jnp
from jax import lax
from jax.experimental import pallas as pl
from jax.experimental.pallas import tpu as pltpu
from jax.sharding import Mesh
from jax.sharding import PartitionSpec as P

HD = 128
KV = 4
PAIR = 2
SCALING = HD ** (-0.5)
LOG2E = 1.4426950408889634
FAR = ("xh", "zh", "zm")


def matmul(a, b, contract):
    return lax.dot_general(a, b, (contract, ((), ())), preferred_element_type=jnp.float32)


def pack_kernel(index_ref, q_ref, g_ref, out_ref):
    def body(slot, _):
        tile = index_ref[slot]
        out_ref[slot, 0] = q_ref[tile]
        out_ref[slot, 1] = g_ref[tile]
        return 0

    lax.fori_loop(0, out_ref.shape[0], body, 0)


def pack(index, queries, grad_out):
    slots = index.shape[0]
    return pl.pallas_call(
        pack_kernel,
        out_shape=jax.ShapeDtypeStruct((slots, 2) + queries.shape[1:], queries.dtype),
        in_specs=[
            pl.BlockSpec(memory_space=pltpu.SMEM),
            pl.BlockSpec(memory_space=pltpu.VMEM),
            pl.BlockSpec(memory_space=pltpu.VMEM),
        ],
        out_specs=pl.BlockSpec(memory_space=pltpu.VMEM),
        compiler_params=pltpu.CompilerParams(vmem_limit_bytes=24 * 2**20),
        name="pack_rows",
    )(index, queries, grad_out)


def attention_kernel(
    recv_ref, start_ref, place_ref, qg_ref, kv0, kv1, kv2, kv3, dq_ref, dkv0, dkv1, dkv2, dkv3,
    k_all, kt_all, v_all, dk_all, dv_all, scores, dprobs, dqt,
):
    blocks = k_all.shape[0]
    width = k_all.shape[1]
    tile_rows = width // PAIR
    part = width // 4
    factor = SCALING * LOG2E

    def stage(block, _):
        for place, ref in enumerate((kv0, kv1, kv2, kv3)):
            rows = slice(place * part, (place + 1) * part)
            key = ref[:, 0, block].astype(jnp.float32).reshape(part, HD)
            value = ref[:, 1, block].astype(jnp.float32).reshape(part, HD)
            k_all[block, rows] = key.astype(jnp.bfloat16)
            v_all[block, rows] = value.astype(jnp.bfloat16)
        kt_all[block] = k_all[block].astype(jnp.float32).T.astype(jnp.bfloat16)
        return 0

    lax.fori_loop(0, blocks, stage, 0)

    row = lax.broadcasted_iota(jnp.int32, (width, 1), 0)
    key_offset = (
        ((row >> 2) & 1) * tile_rows
        + ((row >> 3) & 7) * 16
        + ((place_ref[0] - (row >> 6)) & 3) * 4
        + (row & 3)
    )
    lane = lax.broadcasted_iota(jnp.int32, (1, width), 1)

    def query_block(block, _):
        first = recv_ref[PAIR * block]
        second = recv_ref[PAIR * block + 1]
        query = jnp.concatenate([qg_ref[first, 0], qg_ref[second, 0]], axis=0)
        grad = jnp.concatenate([qg_ref[first, 1], qg_ref[second, 1]], axis=0)
        start_low = start_ref[PAIR * block]
        start_high = start_ref[PAIR * block + 1]
        lowest = start_low // PAIR
        row_start = jnp.where(lane < tile_rows, start_low, start_high) * tile_rows

        def products(other, masked_by_order, peak):
            score = matmul(k_all[other], query, ((1,), (1,)))
            key_pos = key_offset + other * width
            allowed = key_pos >= row_start
            if masked_by_order:
                allowed = allowed & (key_offset <= lane)
            score = jnp.where(allowed, score, -jnp.inf)
            scores[other] = score
            dprobs[other] = matmul(v_all[other], grad, ((1,), (1,)))
            return jnp.maximum(peak, jnp.max(score, axis=0, keepdims=True))

        peak = products(block, True, jnp.full((1, width), -jnp.inf, jnp.float32))
        peak = lax.fori_loop(lowest, block, lambda other, m: products(other, False, m), peak)
        shift = peak * factor

        def sums(other, totals):
            weights = jnp.exp2(scores[other] * factor - shift)
            scores[other] = weights
            return (
                totals[0] + jnp.sum(weights, axis=0, keepdims=True),
                totals[1] + jnp.sum(weights * dprobs[other], axis=0, keepdims=True),
            )

        zeros = jnp.zeros((1, width), jnp.float32)
        total, weighted = lax.fori_loop(lowest, block + 1, sums, (zeros, zeros))
        inverse = 1.0 / total
        delta = weighted * inverse

        def terms(other):
            probs = scores[other] * inverse
            dscores = (probs * (dprobs[other] - delta)).astype(jnp.bfloat16)
            grad_value = matmul(probs.astype(jnp.bfloat16), grad, ((1,), (0,)))
            grad_key = matmul(dscores, query, ((1,), (0,)))
            grad_query = matmul(kt_all[other], dscores, ((1,), (0,)))
            return grad_key, grad_value, grad_query

        grad_key, grad_value, grad_query = terms(block)
        dk_all[block] = grad_key
        dv_all[block] = grad_value
        dqt[...] = grad_query

        def earlier(other, _):
            grad_key, grad_value, grad_query = terms(other)
            dk_all[other] += grad_key
            dv_all[other] += grad_value
            dqt[...] += grad_query
            return 0

        lax.fori_loop(lowest, block, earlier, 0)
        result = (dqt[...] * SCALING).T.astype(jnp.bfloat16)
        dq_ref[first] = result[:tile_rows]
        dq_ref[second] = result[tile_rows:]
        return 0

    lax.fori_loop(0, blocks, query_block, 0)

    def unstage(block, _):
        for place, ref in enumerate((dkv0, dkv1, dkv2, dkv3)):
            rows = slice(place * part, (place + 1) * part)
            shape = (ref.shape[0],) + ref.shape[3:]
            ref[:, 0, block] = (dk_all[block, rows] * SCALING).reshape(shape).astype(jnp.bfloat16)
            ref[:, 1, block] = dv_all[block, rows].reshape(shape).astype(jnp.bfloat16)
        return 0

    lax.fori_loop(0, blocks, unstage, 0)


def attention(my_recv, start, place, qg, kv_parts):
    slots, _, tile_rows, _ = qg.shape
    blocks = my_recv.shape[0] // PAIR
    width = PAIR * tile_rows
    vmem = pl.BlockSpec(memory_space=pltpu.VMEM)
    smem = pl.BlockSpec(memory_space=pltpu.SMEM)
    part = jax.ShapeDtypeStruct(kv_parts[0].shape, jnp.bfloat16)
    return pl.pallas_call(
        attention_kernel,
        out_shape=(jax.ShapeDtypeStruct((slots, tile_rows, HD), jnp.bfloat16),) + (part,) * 4,
        in_specs=[smem, smem, smem] + [vmem] * 5,
        out_specs=(vmem,) * 5,
        scratch_shapes=[
            pltpu.VMEM((blocks, width, HD), jnp.bfloat16),
            pltpu.VMEM((blocks, HD, width), jnp.bfloat16),
            pltpu.VMEM((blocks, width, HD), jnp.bfloat16),
            pltpu.VMEM((blocks, width, HD), jnp.float32),
            pltpu.VMEM((blocks, width, HD), jnp.float32),
            pltpu.VMEM((blocks, width, width), jnp.float32),
            pltpu.VMEM((blocks, width, width), jnp.float32),
            pltpu.VMEM((HD, width), jnp.float32),
        ],
        compiler_params=pltpu.CompilerParams(vmem_limit_bytes=40 * 2**20),
        cost_estimate=pl.CostEstimate(
            flops=2 * 10**9, bytes_accessed=6 * 2**20, transcendentals=2 * 10**6
        ),
        name="attention_backward",
    )(my_recv, start, place, qg, *kv_parts)


def near_shift(values, step):
    size = lax.axis_size("zl")
    return lax.ppermute(values, "zl", [(source, (source + step) % size) for source in range(size)])


def on_device(queries, keys_values, grad_out, send_tiles, recv_slot, tile_seq):
    n_replicas = lax.axis_size("dp")
    replica = lax.axis_index("dp")
    tile_count, tile_rows, row_width = queries.shape
    sliver = keys_values.shape[1]
    slot_cap = send_tiles.shape[2]
    slots = n_replicas * slot_cap
    pairs = tile_count // PAIR
    my_send = send_tiles[0]
    outgoing = my_send.reshape(-1)

    kv_packed = keys_values[outgoing].reshape(n_replicas, slot_cap, sliver, 2 * KV * HD)
    kv_arrived = lax.all_to_all(kv_packed, "dp", split_axis=0, concat_axis=0, tiled=True)
    qg_packed = pack(outgoing, queries, grad_out)
    qg_arrived = lax.all_to_all(
        qg_packed.reshape(n_replicas, slot_cap, 2, tile_rows, row_width),
        "dp", split_axis=0, concat_axis=0, tiled=True,
    ).reshape(slots, 2, tile_rows, row_width)

    my_recv = lax.dynamic_index_in_dim(recv_slot, replica, 0, keepdims=False)
    kv_here = kv_arrived.reshape(slots, sliver, 2 * KV * HD)[my_recv]
    by_head = kv_here.reshape(pairs, PAIR * sliver, 2, KV, HD).transpose(3, 2, 0, 1, 4)
    far_out = jnp.broadcast_to(by_head[:, None], (KV, 2) + by_head.shape[1:]).reshape(
        (2 * KV,) + by_head.shape[1:]
    )
    far_in = lax.all_to_all(far_out, FAR, split_axis=0, concat_axis=0, tiled=True)
    kv_parts = [far_in] + [near_shift(far_in, step) for step in range(1, 4)]

    seq = tile_seq[0]
    start = jnp.sum((seq[None, :] < seq[:, None]).astype(jnp.int32), axis=1)
    place = lax.axis_index("zl").astype(jnp.int32).reshape(1)
    query_back, *dkv_parts = attention(my_recv, start, place, qg_arrived, kv_parts)
    query_returned = lax.all_to_all(
        query_back.reshape(n_replicas, slot_cap, tile_rows, row_width),
        "dp", split_axis=0, concat_axis=0, tiled=True,
    )

    near = [dkv_parts[0]] + [near_shift(dkv_parts[step], -step) for step in range(1, 4)]
    near_sum = sum(term.astype(jnp.float32) for term in near).astype(jnp.bfloat16)
    near_sum, query_returned = lax.optimization_barrier((near_sum, query_returned))
    far = lax.all_to_all(near_sum, FAR, split_axis=0, concat_axis=0, tiled=True)
    far_sum = jnp.sum(
        far.reshape((KV, 2) + far.shape[1:]).astype(jnp.float32), axis=1
    ).astype(jnp.bfloat16)
    kv_grad_here = far_sum.transpose(2, 3, 1, 0, 4).reshape(tile_count, sliver, 2 * KV * HD)

    flat_slots = jnp.arange(slots)
    slot_hits = my_recv[:, None] == flat_slots[None, :]
    back_index = jnp.sum(jnp.where(slot_hits, jnp.arange(tile_count)[:, None], 0), axis=0)
    kv_returned = lax.all_to_all(
        kv_grad_here[back_index].reshape(n_replicas, slot_cap, sliver, 2 * KV * HD),
        "dp", split_axis=0, concat_axis=0, tiled=True,
    )
    own_slots = replica * slot_cap + jnp.arange(slot_cap)
    slot_used = jnp.any(recv_slot[:, None, :] == own_slots[None, :, None], axis=2)
    matched = slot_used[:, :, None] & (my_send[:, :, None] == jnp.arange(tile_count)[None, None, :])
    anchor = jnp.sum(
        jnp.where(matched, flat_slots.reshape(n_replicas, slot_cap)[:, :, None], 0), axis=(0, 1)
    )
    grad_queries = query_returned.reshape(slots, tile_rows, row_width)[anchor]
    grad_keys_values = kv_returned.reshape(slots, sliver, 2 * KV * HD)[anchor]
    return (grad_queries, grad_keys_values)


def solution(mesh):
    names = ("dp",) + FAR + ("zl",)
    fine = Mesh(mesh.devices.reshape(mesh.devices.shape[0], 2, 2, 2, 4), names)
    tensor = FAR + ("zl",)
    in_specs = (
        P("dp", None, tensor),
        P("dp", tensor, None),
        P("dp", None, tensor),
        P("dp", None, None),
        P(),
        P("dp", None),
    )
    out_specs = (P("dp", None, tensor), P("dp", tensor, None))
    return jax.shard_map(
        on_device, mesh=fine, in_specs=in_specs, out_specs=out_specs, check_vma=False
    )
```

```python
import functools

import jax
import jax.numpy as jnp
from jax import lax
from jax.experimental import pallas as pl
from jax.experimental.pallas import tpu as pltpu
from jax.sharding import Mesh
from jax.sharding import PartitionSpec as P

HD = 128
KV = 4
PAIR = 2
SCALING = HD ** (-0.5)
LOG2E = 1.4426950408889634
PLANE = ("dp", "xh")
COLUMN = ("zh", "zm", "zl")
LINE = ("zm", "zl")


def matmul(a, b, contract):
    return lax.dot_general(a, b, (contract, ((), ())), preferred_element_type=jnp.float32)


def pack_kernel(index_ref, q_ref, g_ref, out_ref):
    def body(slot, _):
        tile = index_ref[slot & 1, slot >> 1]
        out_ref[slot, 0] = q_ref[tile]
        out_ref[slot, 1] = g_ref[tile]
        return 0

    lax.fori_loop(0, out_ref.shape[0], body, 0)


def pack(index, queries, grad_out):
    slots = index.size
    return pl.pallas_call(
        pack_kernel,
        out_shape=jax.ShapeDtypeStruct((slots, 2) + queries.shape[1:], queries.dtype),
        in_specs=[
            pl.BlockSpec(memory_space=pltpu.SMEM),
            pl.BlockSpec(memory_space=pltpu.VMEM),
            pl.BlockSpec(memory_space=pltpu.VMEM),
        ],
        out_specs=pl.BlockSpec(memory_space=pltpu.VMEM),
        compiler_params=pltpu.CompilerParams(vmem_limit_bytes=24 * 2**20),
        name="pack_rows",
    )(index, queries, grad_out)


def attention_kernel(
    recv_ref, start_ref, place_ref, qg_ref, kv_ref, dq_ref, dkv_ref,
    k_all, kt_all, v_all, dk_all, dv_all, scores, dprobs, dqt,
):
    blocks = k_all.shape[0]
    width = k_all.shape[1]
    tile_rows = width // PAIR
    factor = SCALING * LOG2E

    def stage(block, _):
        key = kv_ref[:, :, :, 0, block].astype(jnp.float32).reshape(width, HD)
        value = kv_ref[:, :, :, 1, block].astype(jnp.float32).reshape(width, HD)
        k_all[block] = key.astype(jnp.bfloat16)
        v_all[block] = value.astype(jnp.bfloat16)
        kt_all[block] = key.T.astype(jnp.bfloat16)
        return 0

    lax.fori_loop(0, blocks, stage, 0)

    row = lax.broadcasted_iota(jnp.int32, (width, 1), 0)
    source = ((place_ref[0] & 8) | (row >> 5)) ^ (((row >> 4) & 1) * 15)
    key_offset = (
        ((row >> 2) & 1) * tile_rows + ((row >> 3) & 1) * 64 + source * 4 + (row & 3)
    )
    lane = lax.broadcasted_iota(jnp.int32, (1, width), 1)

    def query_block(block, _):
        first = recv_ref[PAIR * block]
        second = recv_ref[PAIR * block + 1]
        query = jnp.concatenate([qg_ref[first, 0], qg_ref[second, 0]], axis=0)
        grad = jnp.concatenate([qg_ref[first, 1], qg_ref[second, 1]], axis=0)
        start_low = start_ref[PAIR * block]
        start_high = start_ref[PAIR * block + 1]
        lowest = start_low // PAIR
        row_start = jnp.where(lane < tile_rows, start_low, start_high) * tile_rows

        def products(other, masked_by_order, peak):
            score = matmul(k_all[other], query, ((1,), (1,)))
            key_pos = key_offset + other * width
            allowed = key_pos >= row_start
            if masked_by_order:
                allowed = allowed & (key_offset <= lane)
            score = jnp.where(allowed, score, -jnp.inf)
            scores[other] = score
            dprobs[other] = matmul(v_all[other], grad, ((1,), (1,)))
            return jnp.maximum(peak, jnp.max(score, axis=0, keepdims=True))

        peak = products(block, True, jnp.full((1, width), -jnp.inf, jnp.float32))
        peak = lax.fori_loop(lowest, block, lambda other, m: products(other, False, m), peak)
        shift = peak * factor

        def sums(other, totals):
            weights = jnp.exp2(scores[other] * factor - shift)
            scores[other] = weights
            return (
                totals[0] + jnp.sum(weights, axis=0, keepdims=True),
                totals[1] + jnp.sum(weights * dprobs[other], axis=0, keepdims=True),
            )

        zeros = jnp.zeros((1, width), jnp.float32)
        total, weighted = lax.fori_loop(lowest, block + 1, sums, (zeros, zeros))
        inverse = 1.0 / total
        delta = weighted * inverse

        def terms(other):
            probs = scores[other] * inverse
            dscores = (probs * (dprobs[other] - delta)).astype(jnp.bfloat16)
            grad_value = matmul(probs.astype(jnp.bfloat16), grad, ((1,), (0,)))
            grad_key = matmul(dscores, query, ((1,), (0,)))
            grad_query = matmul(kt_all[other], dscores, ((1,), (0,)))
            return grad_key, grad_value, grad_query

        grad_key, grad_value, grad_query = terms(block)
        dk_all[block] = grad_key
        dv_all[block] = grad_value
        dqt[...] = grad_query

        def earlier(other, _):
            grad_key, grad_value, grad_query = terms(other)
            dk_all[other] += grad_key
            dv_all[other] += grad_value
            dqt[...] += grad_query
            return 0

        lax.fori_loop(lowest, block, earlier, 0)
        result = (dqt[...] * SCALING).T.astype(jnp.bfloat16)
        dq_ref[first] = result[:tile_rows]
        dq_ref[second] = result[tile_rows:]
        return 0

    lax.fori_loop(0, blocks, query_block, 0)

    def unstage(block, _):
        shape = kv_ref.shape[:3] + kv_ref.shape[5:]
        dkv_ref[:, :, :, 0, block] = (dk_all[block] * SCALING).reshape(shape).astype(jnp.bfloat16)
        dkv_ref[:, :, :, 1, block] = dv_all[block].reshape(shape).astype(jnp.bfloat16)
        return 0

    lax.fori_loop(0, blocks, unstage, 0)


def attention(my_recv, start, place, qg, kv):
    slots, _, tile_rows, _ = qg.shape
    blocks = my_recv.shape[0] // PAIR
    width = PAIR * tile_rows
    vmem = pl.BlockSpec(memory_space=pltpu.VMEM)
    smem = pl.BlockSpec(memory_space=pltpu.SMEM)
    return pl.pallas_call(
        attention_kernel,
        out_shape=(
            jax.ShapeDtypeStruct((slots, tile_rows, HD), jnp.bfloat16),
            jax.ShapeDtypeStruct(kv.shape, jnp.bfloat16),
        ),
        in_specs=[smem, smem, smem, vmem, vmem],
        out_specs=(vmem, vmem),
        scratch_shapes=[
            pltpu.VMEM((blocks, width, HD), jnp.bfloat16),
            pltpu.VMEM((blocks, HD, width), jnp.bfloat16),
            pltpu.VMEM((blocks, width, HD), jnp.bfloat16),
            pltpu.VMEM((blocks, width, HD), jnp.float32),
            pltpu.VMEM((blocks, width, HD), jnp.float32),
            pltpu.VMEM((blocks, width, width), jnp.float32),
            pltpu.VMEM((blocks, width, width), jnp.float32),
            pltpu.VMEM((HD, width), jnp.float32),
        ],
        compiler_params=pltpu.CompilerParams(vmem_limit_bytes=24 * 2**20),
        cost_estimate=pl.CostEstimate(
            flops=2 * 10**9, bytes_accessed=6 * 2**20, transcendentals=2 * 10**6
        ),
        name="attention_backward",
    )(my_recv, start, place, qg, kv)


def kv_pack_kernel(index_ref, kv_ref, out_ref):
    def body(slot, _):
        tile = index_ref[slot & 1, slot >> 1]
        piece = kv_ref[tile].reshape((2, 2, 2) + kv_ref.shape[2:])
        for half in range(2):
            out_ref[slot >> 1, half, slot & 1] = piece[:, half]
        return 0

    lax.fori_loop(0, 2 * index_ref.shape[1], body, 0, unroll=4)


def kv_unpack_kernel(recv_ref, place_ref, kv_ref, own_ref, other_ref):
    head = place_ref[0] >> 3

    def body(pair, _):
        low = recv_ref[PAIR * pair]
        high = recv_ref[PAIR * pair + 1]
        for half in range(2):
            for kind in range(2):
                for ref, which in ((own_ref, head), (other_ref, 1 - head)):
                    rows = [
                        kv_ref[slot >> 1, half, slot & 1, kind, which].astype(jnp.float32)
                        for slot in (low, high)
                    ]
                    ref[half, kind, pair] = jnp.concatenate(rows, axis=0).astype(jnp.bfloat16)
        return 0

    lax.fori_loop(0, recv_ref.shape[0] // PAIR, body, 0)


def kv_back_kernel(recv_ref, place_ref, own_ref, other_ref, out_ref):
    head = place_ref[0] >> 3
    sliver = out_ref.shape[-2]

    def body(pair, _):
        slots = (recv_ref[PAIR * pair], recv_ref[PAIR * pair + 1])
        for half in range(2):
            for kind in range(2):
                for ref, which in ((own_ref, head), (other_ref, 1 - head)):
                    total = ref[half, kind, pair].astype(jnp.float32)
                    for order, slot in enumerate(slots):
                        rows = total[order * sliver : (order + 1) * sliver]
                        out_ref[slot >> 1, half, slot & 1, kind, which] = rows.astype(jnp.bfloat16)
        return 0

    lax.fori_loop(0, recv_ref.shape[0] // PAIR, body, 0)


def kv_final_kernel(anchor_ref, kv_ref, out_ref):
    def body(tile, _):
        slot = anchor_ref[tile]
        piece = kv_ref[slot >> 1, :, slot & 1]
        for half in range(2):
            for kind in range(2):
                for head in range(2):
                    out_ref[tile, kind * 4 + half * 2 + head] = piece[half, kind, head]
        return 0

    lax.fori_loop(0, anchor_ref.shape[0], body, 0)


def local_call(kernel, name, scalars, arrays, out_shape):
    vmem = pl.BlockSpec(memory_space=pltpu.VMEM)
    smem = pl.BlockSpec(memory_space=pltpu.SMEM)
    return pl.pallas_call(
        kernel,
        out_shape=out_shape,
        in_specs=[smem] * len(scalars) + [vmem] * len(arrays),
        out_specs=jax.tree.map(lambda _: vmem, out_shape),
        compiler_params=pltpu.CompilerParams(vmem_limit_bytes=16 * 2**20),
        name=name,
    )(*scalars, *arrays)


def mirror(values):
    return lax.ppermute(values, COLUMN, [(source, 15 - source) for source in range(16)])


def on_device(queries, keys_values, grad_out, send_tiles, recv_slot, tile_seq):
    n_replicas = lax.axis_size("dp")
    replica = lax.axis_index("dp")
    tile_count, tile_rows, row_width = queries.shape
    sliver = keys_values.shape[1]
    slot_cap = send_tiles.shape[2]
    slots = n_replicas * slot_cap
    pairs = tile_count // PAIR
    my_send = send_tiles[0]
    outgoing = my_send.T
    my_recv = lax.dynamic_index_in_dim(recv_slot, replica, 0, keepdims=False)
    place = lax.axis_index(COLUMN).astype(jnp.int32).reshape(1)
    traveling = jax.ShapeDtypeStruct(
        (n_replicas, 2, slot_cap, 2, 2, sliver, HD), keys_values.dtype
    )
    half_shape = jax.ShapeDtypeStruct((2, 2, pairs, PAIR * sliver, HD), keys_values.dtype)

    def over_plane(values):
        return lax.all_to_all(
            values.reshape((2 * n_replicas,) + values.shape[2:]),
            PLANE, split_axis=0, concat_axis=0, tiled=True,
        ).reshape(values.shape)

    kv_blocks = keys_values.reshape(tile_count, sliver, 2 * KV, HD).transpose(0, 2, 1, 3)
    kv_arrived = over_plane(
        local_call(kv_pack_kernel, "kv_pack", [outgoing], [kv_blocks], traveling)
    )
    own, other = local_call(
        kv_unpack_kernel, "kv_unpack", [my_recv, place], [kv_arrived], (half_shape, half_shape)
    )
    qg_packed = pack(outgoing, queries, grad_out)
    mirrored = mirror(other)
    qg_packed, mirrored = lax.optimization_barrier((qg_packed, mirrored))
    qg_arrived = lax.all_to_all(
        qg_packed.reshape(n_replicas, slot_cap, 2, tile_rows, row_width),
        "dp", split_axis=0, concat_axis=0, tiled=True,
    ).reshape(slots, 2, tile_rows, row_width)
    kv_all = lax.all_gather(jnp.stack([own, mirrored]), LINE)

    seq = tile_seq[0]
    start = jnp.sum((seq[None, :] < seq[:, None]).astype(jnp.int32), axis=1)
    query_back, dkv = attention(my_recv, start, place, qg_arrived, kv_all)
    query_returned = lax.all_to_all(
        query_back.reshape(n_replicas, slot_cap, tile_rows, row_width),
        "dp", split_axis=0, concat_axis=0, tiled=True,
    )

    summed = lax.psum_scatter(dkv, LINE, scatter_dimension=0)
    summed, query_returned = lax.optimization_barrier((summed, query_returned))
    swapped = [summed[0], mirror(summed[1])]
    kv_returned = over_plane(
        local_call(kv_back_kernel, "kv_back", [my_recv, place], swapped, traveling)
    )

    flat_slots = jnp.arange(slots)
    own_slots = replica * slot_cap + jnp.arange(slot_cap)
    slot_used = jnp.any(recv_slot[:, None, :] == own_slots[None, :, None], axis=2)
    matched = slot_used[:, :, None] & (my_send[:, :, None] == jnp.arange(tile_count)[None, None, :])
    anchor = jnp.sum(
        jnp.where(matched, flat_slots.reshape(n_replicas, slot_cap)[:, :, None], 0), axis=(0, 1)
    )
    grad_queries = query_returned.reshape(slots, tile_rows, row_width)[anchor]
    kv_final = local_call(
        kv_final_kernel, "kv_final", [anchor], [kv_returned],
        jax.ShapeDtypeStruct(kv_blocks.shape, keys_values.dtype),
    )
    grad_keys_values = kv_final.transpose(0, 2, 1, 3).reshape(keys_values.shape)
    return (grad_queries, grad_keys_values)


def solution(mesh):
    names = PLANE + COLUMN
    fine = Mesh(mesh.devices.reshape(mesh.devices.shape[0], 2, 2, 2, 4), names)
    tensor = ("xh",) + COLUMN
    in_specs = (
        P("dp", None, tensor),
        P("dp", tensor, None),
        P("dp", None, tensor),
        P("dp", None, None),
        P(),
        P("dp", None),
    )
    out_specs = (P("dp", None, tensor), P("dp", tensor, None))
    return jax.shard_map(
        on_device, mesh=fine, in_specs=in_specs, out_specs=out_specs, check_vma=False
    )
```

```python
import functools

import jax
import jax.numpy as jnp
from jax import lax
from jax.experimental import pallas as pl
from jax.experimental.pallas import tpu as pltpu
from jax.sharding import Mesh
from jax.sharding import PartitionSpec as P

HD = 128
KV = 4
PAIR = 2
SCALING = HD ** (-0.5)
LOG2E = 1.4426950408889634
PLANE = ("dp", "xh")
COLUMN = ("zh", "zm", "zl")
RING = 8
FOLD = (0, 2, 4, 6, 7, 5, 3, 1)


def matmul(a, b, contract):
    return lax.dot_general(a, b, (contract, ((), ())), preferred_element_type=jnp.float32)


def pack_kernel(index_ref, q_ref, g_ref, out_ref):
    def body(slot, _):
        tile = index_ref[slot & 1, slot >> 1]
        out_ref[slot, 0] = q_ref[tile]
        out_ref[slot, 1] = g_ref[tile]
        return 0

    lax.fori_loop(0, out_ref.shape[0], body, 0)


def pack(index, queries, grad_out):
    slots = index.size
    return pl.pallas_call(
        pack_kernel,
        out_shape=jax.ShapeDtypeStruct((slots, 2) + queries.shape[1:], queries.dtype),
        in_specs=[
            pl.BlockSpec(memory_space=pltpu.SMEM),
            pl.BlockSpec(memory_space=pltpu.VMEM),
            pl.BlockSpec(memory_space=pltpu.VMEM),
        ],
        out_specs=pl.BlockSpec(memory_space=pltpu.VMEM),
        compiler_params=pltpu.CompilerParams(vmem_limit_bytes=24 * 2**20),
        name="pack_rows",
    )(index, queries, grad_out)


def attention_kernel(
    recv_ref, start_ref, place_ref, qg_ref, *refs
):
    kv_refs, dq_ref, dkv_refs = refs[:RING], refs[RING], refs[RING + 1 : 2 * RING + 1]
    k_all, kt_all, v_all, dk_all, dv_all, scores, dprobs, dqt = refs[2 * RING + 1 :]
    blocks = k_all.shape[0]
    width = k_all.shape[1]
    tile_rows = width // PAIR
    part = width // RING
    factor = SCALING * LOG2E

    def stage(block, _):
        for slot, ref in enumerate(kv_refs):
            rows = slice(slot * part, (slot + 1) * part)
            key = ref[:, :, 0, block].astype(jnp.float32).reshape(part, HD)
            value = ref[:, :, 1, block].astype(jnp.float32).reshape(part, HD)
            k_all[block, rows] = key.astype(jnp.bfloat16)
            v_all[block, rows] = value.astype(jnp.bfloat16)
        kt_all[block] = k_all[block].astype(jnp.float32).T.astype(jnp.bfloat16)
        return 0

    lax.fori_loop(0, blocks, stage, 0)

    row = lax.broadcasted_iota(jnp.int32, (width, 1), 0)
    slot = row >> 5
    step = (slot + 1) >> 1
    ahead = jnp.where((slot & 1) == 1, -step, step)
    member = place_ref[0] & (RING - 1)
    index = (jnp.where((member & 1) == 1, 15 - member, member) >> 1) + ahead & (RING - 1)
    column = jnp.where(index < RING // 2, 2 * index, 15 - 2 * index)
    source = ((place_ref[0] & 8) | column) ^ (((row >> 4) & 1) * 15)
    key_offset = (
        ((row >> 2) & 1) * tile_rows + ((row >> 3) & 1) * 64 + source * 4 + (row & 3)
    )
    lane = lax.broadcasted_iota(jnp.int32, (1, width), 1)

    def query_block(block, _):
        first = recv_ref[PAIR * block]
        second = recv_ref[PAIR * block + 1]
        query = jnp.concatenate([qg_ref[first, 0], qg_ref[second, 0]], axis=0)
        grad = jnp.concatenate([qg_ref[first, 1], qg_ref[second, 1]], axis=0)
        start_low = start_ref[PAIR * block]
        start_high = start_ref[PAIR * block + 1]
        lowest = start_low // PAIR
        row_start = jnp.where(lane < tile_rows, start_low, start_high) * tile_rows

        def products(other, masked_by_order, peak):
            score = matmul(k_all[other], query, ((1,), (1,)))
            key_pos = key_offset + other * width
            allowed = key_pos >= row_start
            if masked_by_order:
                allowed = allowed & (key_offset <= lane)
            score = jnp.where(allowed, score, -jnp.inf)
            scores[other] = score
            dprobs[other] = matmul(v_all[other], grad, ((1,), (1,)))
            return jnp.maximum(peak, jnp.max(score, axis=0, keepdims=True))

        peak = products(block, True, jnp.full((1, width), -jnp.inf, jnp.float32))
        peak = lax.fori_loop(lowest, block, lambda other, m: products(other, False, m), peak)
        shift = peak * factor

        def sums(other, totals):
            weights = jnp.exp2(scores[other] * factor - shift)
            scores[other] = weights
            return (
                totals[0] + jnp.sum(weights, axis=0, keepdims=True),
                totals[1] + jnp.sum(weights * dprobs[other], axis=0, keepdims=True),
            )

        zeros = jnp.zeros((1, width), jnp.float32)
        total, weighted = lax.fori_loop(lowest, block + 1, sums, (zeros, zeros))
        inverse = 1.0 / total
        delta = weighted * inverse

        def terms(other):
            probs = scores[other] * inverse
            dscores = (probs * (dprobs[other] - delta)).astype(jnp.bfloat16)
            grad_value = matmul(probs.astype(jnp.bfloat16), grad, ((1,), (0,)))
            grad_key = matmul(dscores, query, ((1,), (0,)))
            grad_query = matmul(kt_all[other], dscores, ((1,), (0,)))
            return grad_key, grad_value, grad_query

        grad_key, grad_value, grad_query = terms(block)
        dk_all[block] = grad_key
        dv_all[block] = grad_value
        dqt[...] = grad_query

        def earlier(other, _):
            grad_key, grad_value, grad_query = terms(other)
            dk_all[other] += grad_key
            dv_all[other] += grad_value
            dqt[...] += grad_query
            return 0

        lax.fori_loop(lowest, block, earlier, 0)
        result = (dqt[...] * SCALING).T.astype(jnp.bfloat16)
        dq_ref[first] = result[:tile_rows]
        dq_ref[second] = result[tile_rows:]
        return 0

    lax.fori_loop(0, blocks, query_block, 0)

    def unstage(block, _):
        for slot, ref in enumerate(dkv_refs):
            rows = slice(slot * part, (slot + 1) * part)
            shape = ref.shape[:2] + ref.shape[4:]
            ref[:, :, 0, block] = (dk_all[block, rows] * SCALING).reshape(shape).astype(jnp.bfloat16)
            ref[:, :, 1, block] = dv_all[block, rows].reshape(shape).astype(jnp.bfloat16)
        return 0

    lax.fori_loop(0, blocks, unstage, 0)


def attention(my_recv, start, place, qg, chunks):
    slots, _, tile_rows, _ = qg.shape
    blocks = my_recv.shape[0] // PAIR
    width = PAIR * tile_rows
    vmem = pl.BlockSpec(memory_space=pltpu.VMEM)
    smem = pl.BlockSpec(memory_space=pltpu.SMEM)
    return pl.pallas_call(
        attention_kernel,
        out_shape=(jax.ShapeDtypeStruct((slots, tile_rows, HD), jnp.bfloat16),)
        + (jax.ShapeDtypeStruct(chunks[0].shape, jnp.bfloat16),) * RING,
        in_specs=[smem] * 3 + [vmem] * (1 + RING),
        out_specs=(vmem,) * (1 + RING),
        scratch_shapes=[
            pltpu.VMEM((blocks, width, HD), jnp.bfloat16),
            pltpu.VMEM((blocks, HD, width), jnp.bfloat16),
            pltpu.VMEM((blocks, width, HD), jnp.bfloat16),
            pltpu.VMEM((blocks, width, HD), jnp.float32),
            pltpu.VMEM((blocks, width, HD), jnp.float32),
            pltpu.VMEM((blocks, width, width), jnp.float32),
            pltpu.VMEM((blocks, width, width), jnp.float32),
            pltpu.VMEM((HD, width), jnp.float32),
        ],
        compiler_params=pltpu.CompilerParams(vmem_limit_bytes=24 * 2**20),
        cost_estimate=pl.CostEstimate(
            flops=2 * 10**9, bytes_accessed=6 * 2**20, transcendentals=2 * 10**6
        ),
        name="attention_backward",
    )(my_recv, start, place, qg, *chunks)


def kv_pack_kernel(index_ref, kv_ref, out_ref):
    def body(slot, _):
        tile = index_ref[slot & 1, slot >> 1]
        piece = kv_ref[tile].reshape((2, 2, 2) + kv_ref.shape[2:])
        for half in range(2):
            out_ref[slot >> 1, half, slot & 1] = piece[:, half]
        return 0

    lax.fori_loop(0, 2 * index_ref.shape[1], body, 0, unroll=4)


def kv_unpack_kernel(recv_ref, place_ref, kv_ref, own_ref, other_ref):
    head = place_ref[0] >> 3

    def body(pair, _):
        low = recv_ref[PAIR * pair]
        high = recv_ref[PAIR * pair + 1]
        for half in range(2):
            for kind in range(2):
                for ref, which in ((own_ref, head), (other_ref, 1 - head)):
                    rows = [
                        kv_ref[slot >> 1, half, slot & 1, kind, which].astype(jnp.float32)
                        for slot in (low, high)
                    ]
                    ref[half, kind, pair] = jnp.concatenate(rows, axis=0).astype(jnp.bfloat16)
        return 0

    lax.fori_loop(0, recv_ref.shape[0] // PAIR, body, 0)


def kv_back_kernel(recv_ref, place_ref, own_ref, other_ref, out_ref):
    head = place_ref[0] >> 3
    sliver = out_ref.shape[-2]

    def body(pair, _):
        slots = (recv_ref[PAIR * pair], recv_ref[PAIR * pair + 1])
        for half in range(2):
            for kind in range(2):
                for ref, which in ((own_ref, head), (other_ref, 1 - head)):
                    total = ref[half, kind, pair].astype(jnp.float32)
                    for order, slot in enumerate(slots):
                        rows = total[order * sliver : (order + 1) * sliver]
                        out_ref[slot >> 1, half, slot & 1, kind, which] = rows.astype(jnp.bfloat16)
        return 0

    lax.fori_loop(0, recv_ref.shape[0] // PAIR, body, 0)


def kv_final_kernel(anchor_ref, kv_ref, out_ref):
    def body(tile, _):
        slot = anchor_ref[tile]
        piece = kv_ref[slot >> 1, :, slot & 1]
        for half in range(2):
            for kind in range(2):
                for head in range(2):
                    out_ref[tile, kind * 4 + half * 2 + head] = piece[half, kind, head]
        return 0

    lax.fori_loop(0, anchor_ref.shape[0], body, 0)


def local_call(kernel, name, scalars, arrays, out_shape):
    vmem = pl.BlockSpec(memory_space=pltpu.VMEM)
    smem = pl.BlockSpec(memory_space=pltpu.SMEM)
    return pl.pallas_call(
        kernel,
        out_shape=out_shape,
        in_specs=[smem] * len(scalars) + [vmem] * len(arrays),
        out_specs=jax.tree.map(lambda _: vmem, out_shape),
        compiler_params=pltpu.CompilerParams(vmem_limit_bytes=16 * 2**20),
        name=name,
    )(*scalars, *arrays)


def mirror(values):
    return lax.ppermute(values, COLUMN, [(source, 15 - source) for source in range(16)])


def turn(values, step):
    pairs = [
        (base + FOLD[index], base + FOLD[(index + step) % RING])
        for base in (0, RING)
        for index in range(RING)
    ]
    return lax.ppermute(values, COLUMN, pairs)


def ring_gather(mine):
    chunks = [mine]
    before = after = mine
    for step in range(1, RING // 2 + 1):
        before = turn(before, 1)
        chunks.append(before)
        if step < RING // 2:
            after = turn(after, -1)
            chunks.append(after)
    return chunks


def ring_reduce(terms):
    def plus(arrived, term):
        return (arrived.astype(jnp.float32) + term.astype(jnp.float32)).astype(term.dtype)

    half = RING // 2
    onward = turn(terms[RING - 1], 1)
    first = onward
    back = turn(terms[2 * half - 3], -1)
    for step in range(half - 1, 0, -1):
        onward = turn(plus(onward, terms[2 * step]), 1)
        if step > 1:
            back = turn(plus(back, terms[2 * step - 3]), -1)
    total = onward.astype(jnp.float32) + back.astype(jnp.float32) + terms[0].astype(jnp.float32)
    return total.astype(terms[0].dtype), first


def on_device(queries, keys_values, grad_out, send_tiles, recv_slot, tile_seq):
    n_replicas = lax.axis_size("dp")
    replica = lax.axis_index("dp")
    tile_count, tile_rows, row_width = queries.shape
    sliver = keys_values.shape[1]
    slot_cap = send_tiles.shape[2]
    slots = n_replicas * slot_cap
    pairs = tile_count // PAIR
    my_send = send_tiles[0]
    outgoing = my_send.T
    my_recv = lax.dynamic_index_in_dim(recv_slot, replica, 0, keepdims=False)
    place = lax.axis_index(COLUMN).astype(jnp.int32).reshape(1)
    traveling = jax.ShapeDtypeStruct(
        (n_replicas, 2, slot_cap, 2, 2, sliver, HD), keys_values.dtype
    )
    half_shape = jax.ShapeDtypeStruct((2, 2, pairs, PAIR * sliver, HD), keys_values.dtype)

    def over_plane(values):
        return lax.all_to_all(
            values.reshape((2 * n_replicas,) + values.shape[2:]),
            PLANE, split_axis=0, concat_axis=0, tiled=True,
        ).reshape(values.shape)

    kv_blocks = keys_values.reshape(tile_count, sliver, 2 * KV, HD).transpose(0, 2, 1, 3)
    kv_arrived = over_plane(
        local_call(kv_pack_kernel, "kv_pack", [outgoing], [kv_blocks], traveling)
    )
    own, other = local_call(
        kv_unpack_kernel, "kv_unpack", [my_recv, place], [kv_arrived], (half_shape, half_shape)
    )
    qg_packed = pack(outgoing, queries, grad_out)
    mirrored = mirror(other)
    qg_packed, mirrored = lax.optimization_barrier((qg_packed, mirrored))
    qg_arrived = lax.all_to_all(
        qg_packed.reshape(n_replicas, slot_cap, 2, tile_rows, row_width),
        "dp", split_axis=0, concat_axis=0, tiled=True,
    ).reshape(slots, 2, tile_rows, row_width)
    chunks = ring_gather(jnp.stack([own, mirrored]))

    seq = tile_seq[0]
    start = jnp.sum((seq[None, :] < seq[:, None]).astype(jnp.int32), axis=1)
    query_back, *terms = attention(my_recv, start, place, qg_arrived, chunks)
    summed, first = ring_reduce(terms)
    query_back, _ = lax.optimization_barrier((query_back, first))
    query_returned = lax.all_to_all(
        query_back.reshape(n_replicas, slot_cap, tile_rows, row_width),
        "dp", split_axis=0, concat_axis=0, tiled=True,
    )
    summed, query_returned = lax.optimization_barrier((summed, query_returned))
    swapped = [summed[0], mirror(summed[1])]
    kv_returned = over_plane(
        local_call(kv_back_kernel, "kv_back", [my_recv, place], swapped, traveling)
    )

    flat_slots = jnp.arange(slots)
    own_slots = replica * slot_cap + jnp.arange(slot_cap)
    slot_used = jnp.any(recv_slot[:, None, :] == own_slots[None, :, None], axis=2)
    matched = slot_used[:, :, None] & (my_send[:, :, None] == jnp.arange(tile_count)[None, None, :])
    anchor = jnp.sum(
        jnp.where(matched, flat_slots.reshape(n_replicas, slot_cap)[:, :, None], 0), axis=(0, 1)
    )
    grad_queries = query_returned.reshape(slots, tile_rows, row_width)[anchor]
    kv_final = local_call(
        kv_final_kernel, "kv_final", [anchor], [kv_returned],
        jax.ShapeDtypeStruct(kv_blocks.shape, keys_values.dtype),
    )
    grad_keys_values = kv_final.transpose(0, 2, 1, 3).reshape(keys_values.shape)
    return (grad_queries, grad_keys_values)


def solution(mesh):
    names = PLANE + COLUMN
    fine = Mesh(mesh.devices.reshape(mesh.devices.shape[0], 2, 2, 2, 4), names)
    tensor = ("xh",) + COLUMN
    in_specs = (
        P("dp", None, tensor),
        P("dp", tensor, None),
        P("dp", None, tensor),
        P("dp", None, None),
        P(),
        P("dp", None),
    )
    out_specs = (P("dp", None, tensor), P("dp", tensor, None))
    return jax.shard_map(
        on_device, mesh=fine, in_specs=in_specs, out_specs=out_specs, check_vma=False
    )
```

```python
import functools

import jax
import jax.numpy as jnp
from jax import lax
from jax.experimental import pallas as pl
from jax.experimental.pallas import tpu as pltpu
from jax.sharding import Mesh
from jax.sharding import PartitionSpec as P

HD = 128
KV = 4
PAIR = 2
SCALING = HD ** (-0.5)
LOG2E = 1.4426950408889634
PLANE = ("dp", "xh")
COLUMN = ("zh", "zm", "zl")
NEAR = 4


def matmul(a, b, contract):
    return lax.dot_general(a, b, (contract, ((), ())), preferred_element_type=jnp.float32)


def pack_kernel(index_ref, q_ref, g_ref, out_ref):
    def body(slot, _):
        tile = index_ref[slot & 1, slot >> 1]
        out_ref[slot, 0] = q_ref[tile]
        out_ref[slot, 1] = g_ref[tile]
        return 0

    lax.fori_loop(0, out_ref.shape[0], body, 0)


def pack(index, queries, grad_out):
    slots = index.size
    return pl.pallas_call(
        pack_kernel,
        out_shape=jax.ShapeDtypeStruct((slots, 2) + queries.shape[1:], queries.dtype),
        in_specs=[
            pl.BlockSpec(memory_space=pltpu.SMEM),
            pl.BlockSpec(memory_space=pltpu.VMEM),
            pl.BlockSpec(memory_space=pltpu.VMEM),
        ],
        out_specs=pl.BlockSpec(memory_space=pltpu.VMEM),
        compiler_params=pltpu.CompilerParams(vmem_limit_bytes=24 * 2**20),
        name="pack_rows",
    )(index, queries, grad_out)


def attention_kernel(
    recv_ref, start_ref, place_ref, qg_ref, *refs
):
    kv_refs, dq_ref, dkv_refs = refs[:NEAR], refs[NEAR], refs[NEAR + 1 : 2 * NEAR + 1]
    k_all, kt_all, v_all, dk_all, dv_all, scores, dprobs, dqt, parts, arrived = refs[2 * NEAR + 1 :]
    copies = [
        pltpu.make_async_copy(ref, parts.at[slot], arrived.at[slot])
        for slot, ref in enumerate(kv_refs)
    ]
    for copy in copies:
        copy.start()
    blocks = k_all.shape[0]
    width = k_all.shape[1]
    tile_rows = width // PAIR
    part = width // NEAR
    factor = SCALING * LOG2E

    def stage(block, _):
        for slot in range(NEAR):
            rows = slice(slot * part, (slot + 1) * part)
            key = parts[slot, :, :, 0, block].astype(jnp.float32).reshape(part, HD)
            value = parts[slot, :, :, 1, block].astype(jnp.float32).reshape(part, HD)
            k_all[block, rows] = key.astype(jnp.bfloat16)
            v_all[block, rows] = value.astype(jnp.bfloat16)
        kt_all[block] = k_all[block].astype(jnp.float32).T.astype(jnp.bfloat16)
        return 0

    for copy in copies:
        copy.wait()
    lax.fori_loop(0, blocks, stage, 0)

    row = lax.broadcasted_iota(jnp.int32, (width, 1), 0)
    holder = (place_ref[0] & 12) | ((place_ref[0] - (row >> 6)) & 3)
    origin = (row >> 4) & 3
    hop = 4 - 8 * (holder & 1)
    source = jnp.where(
        origin == 0,
        holder,
        jnp.where(
            origin == 1,
            (holder - hop) & 15,
            jnp.where(origin == 2, (holder + hop) & 15, holder ^ 11),
        ),
    )
    key_offset = (
        ((row >> 2) & 1) * tile_rows + ((row >> 3) & 1) * 64 + source * 4 + (row & 3)
    )
    lane = lax.broadcasted_iota(jnp.int32, (1, width), 1)

    def query_block(block, _):
        first = recv_ref[PAIR * block]
        second = recv_ref[PAIR * block + 1]
        query = jnp.concatenate([qg_ref[first, 0], qg_ref[second, 0]], axis=0)
        grad = jnp.concatenate([qg_ref[first, 1], qg_ref[second, 1]], axis=0)
        start_low = start_ref[PAIR * block]
        start_high = start_ref[PAIR * block + 1]
        lowest = start_low // PAIR
        row_start = jnp.where(lane < tile_rows, start_low, start_high) * tile_rows

        def products(other, masked_by_order, peak):
            score = matmul(k_all[other], query, ((1,), (1,)))
            key_pos = key_offset + other * width
            allowed = key_pos >= row_start
            if masked_by_order:
                allowed = allowed & (key_offset <= lane)
            score = jnp.where(allowed, score, -jnp.inf)
            scores[other] = score
            dprobs[other] = matmul(v_all[other], grad, ((1,), (1,)))
            return jnp.maximum(peak, jnp.max(score, axis=0, keepdims=True))

        peak = products(block, True, jnp.full((1, width), -jnp.inf, jnp.float32))
        peak = lax.fori_loop(lowest, block, lambda other, m: products(other, False, m), peak)
        shift = peak * factor

        def sums(other, totals):
            weights = jnp.exp2(scores[other] * factor - shift)
            scores[other] = weights
            return (
                totals[0] + jnp.sum(weights, axis=0, keepdims=True),
                totals[1] + jnp.sum(weights * dprobs[other], axis=0, keepdims=True),
            )

        zeros = jnp.zeros((1, width), jnp.float32)
        total, weighted = lax.fori_loop(lowest, block + 1, sums, (zeros, zeros))
        inverse = 1.0 / total
        delta = weighted * inverse

        def terms(other):
            probs = scores[other] * inverse
            dscores = (probs * (dprobs[other] - delta)).astype(jnp.bfloat16)
            grad_value = matmul(probs.astype(jnp.bfloat16), grad, ((1,), (0,)))
            grad_key = matmul(dscores, query, ((1,), (0,)))
            grad_query = matmul(kt_all[other], dscores, ((1,), (0,)))
            return grad_key, grad_value, grad_query

        grad_key, grad_value, grad_query = terms(block)
        dk_all[block] = grad_key
        dv_all[block] = grad_value
        dqt[...] = grad_query

        def earlier(other, _):
            grad_key, grad_value, grad_query = terms(other)
            dk_all[other] += grad_key
            dv_all[other] += grad_value
            dqt[...] += grad_query
            return 0

        lax.fori_loop(lowest, block, earlier, 0)
        result = (dqt[...] * SCALING).T.astype(jnp.bfloat16)
        dq_ref[first] = result[:tile_rows]
        dq_ref[second] = result[tile_rows:]
        return 0

    lax.fori_loop(0, blocks, query_block, 0)

    def unstage(block, _):
        for slot, ref in enumerate(dkv_refs):
            rows = slice(slot * part, (slot + 1) * part)
            shape = ref.shape[:2] + ref.shape[4:]
            ref[:, :, 0, block] = (dk_all[block, rows] * SCALING).reshape(shape).astype(jnp.bfloat16)
            ref[:, :, 1, block] = dv_all[block, rows].reshape(shape).astype(jnp.bfloat16)
        return 0

    lax.fori_loop(0, blocks, unstage, 0)


def attention(my_recv, start, place, qg, chunks):
    slots, _, tile_rows, _ = qg.shape
    blocks = my_recv.shape[0] // PAIR
    width = PAIR * tile_rows
    vmem = pl.BlockSpec(memory_space=pltpu.VMEM)
    smem = pl.BlockSpec(memory_space=pltpu.SMEM)
    return pl.pallas_call(
        attention_kernel,
        out_shape=(jax.ShapeDtypeStruct((slots, tile_rows, HD), jnp.bfloat16),)
        + (jax.ShapeDtypeStruct(chunks[0].shape, jnp.bfloat16),) * NEAR,
        in_specs=[smem] * 3 + [vmem] + [pl.BlockSpec(memory_space=pl.ANY)] * NEAR,
        out_specs=(vmem,) * (1 + NEAR),
        scratch_shapes=[
            pltpu.VMEM((blocks, width, HD), jnp.bfloat16),
            pltpu.VMEM((blocks, HD, width), jnp.bfloat16),
            pltpu.VMEM((blocks, width, HD), jnp.bfloat16),
            pltpu.VMEM((blocks, width, HD), jnp.float32),
            pltpu.VMEM((blocks, width, HD), jnp.float32),
            pltpu.VMEM((blocks, width, width), jnp.float32),
            pltpu.VMEM((blocks, width, width), jnp.float32),
            pltpu.VMEM((HD, width), jnp.float32),
            pltpu.VMEM((NEAR,) + chunks[0].shape, jnp.bfloat16),
            pltpu.SemaphoreType.DMA((NEAR,)),
        ],
        compiler_params=pltpu.CompilerParams(vmem_limit_bytes=24 * 2**20),
        cost_estimate=pl.CostEstimate(
            flops=2 * 10**9, bytes_accessed=6 * 2**20, transcendentals=2 * 10**6
        ),
        name="attention_backward",
    )(my_recv, start, place, qg, *chunks)


def kv_pack_kernel(index_ref, kv_ref, out_ref):
    def body(slot, _):
        tile = index_ref[slot & 1, slot >> 1]
        piece = kv_ref[tile].reshape((2, 2, 2) + kv_ref.shape[2:])
        for half in range(2):
            out_ref[slot >> 1, half, slot & 1] = piece[:, half]
        return 0

    lax.fori_loop(0, 2 * index_ref.shape[1], body, 0, unroll=4)


def plus_stays(place):
    return ((place & 1) == 0) == ((place & 4) == 0)


def kv_unpack_kernel(recv_ref, place_ref, kv_ref, own_ref, other_ref, plus_ref, minus_ref):
    head = place_ref[0] >> 3
    plus_head = jnp.where(plus_stays(place_ref[0]), head, 1 - head)

    def body(pair, _):
        low = recv_ref[PAIR * pair]
        high = recv_ref[PAIR * pair + 1]
        for half in range(2):
            for kind in range(2):
                for ref, which in (
                    (own_ref, head),
                    (other_ref, 1 - head),
                    (plus_ref, plus_head),
                    (minus_ref, 1 - plus_head),
                ):
                    rows = [
                        kv_ref[slot >> 1, half, slot & 1, kind, which].astype(jnp.float32)
                        for slot in (low, high)
                    ]
                    ref[half, kind, pair] = jnp.concatenate(rows, axis=0).astype(jnp.bfloat16)
        return 0

    lax.fori_loop(0, recv_ref.shape[0] // PAIR, body, 0)


def kv_back_kernel(recv_ref, place_ref, own_ref, from_plus, from_minus, other_ref, out_ref):
    head = place_ref[0] >> 3
    stays = plus_stays(place_ref[0])
    sliver = out_ref.shape[-2]

    def body(pair, _):
        slots = (recv_ref[PAIR * pair], recv_ref[PAIR * pair + 1])
        for half in range(2):
            for kind in range(2):
                plus = from_plus[half, kind, pair].astype(jnp.float32)
                minus = from_minus[half, kind, pair].astype(jnp.float32)
                for ref, far, which in (
                    (own_ref, jnp.where(stays, plus, minus), head),
                    (other_ref, jnp.where(stays, minus, plus), 1 - head),
                ):
                    total = ref[half, kind, pair].astype(jnp.float32) + far
                    for order, slot in enumerate(slots):
                        rows = total[order * sliver : (order + 1) * sliver]
                        out_ref[slot >> 1, half, slot & 1, kind, which] = rows.astype(jnp.bfloat16)
        return 0

    lax.fori_loop(0, recv_ref.shape[0] // PAIR, body, 0)


def kv_final_kernel(anchor_ref, kv_ref, out_ref):
    def body(tile, _):
        slot = anchor_ref[tile]
        piece = kv_ref[slot >> 1, :, slot & 1]
        for half in range(2):
            for kind in range(2):
                for head in range(2):
                    out_ref[tile, kind * 4 + half * 2 + head] = piece[half, kind, head]
        return 0

    lax.fori_loop(0, anchor_ref.shape[0], body, 0)


def local_call(kernel, name, scalars, arrays, out_shape):
    vmem = pl.BlockSpec(memory_space=pltpu.VMEM)
    smem = pl.BlockSpec(memory_space=pltpu.SMEM)
    return pl.pallas_call(
        kernel,
        out_shape=out_shape,
        in_specs=[smem] * len(scalars) + [vmem] * len(arrays),
        out_specs=jax.tree.map(lambda _: vmem, out_shape),
        compiler_params=pltpu.CompilerParams(vmem_limit_bytes=16 * 2**20),
        name=name,
    )(*scalars, *arrays)


def plus_four(values):
    pairs = [(place, (place + 4 - 8 * (place & 1)) & 15) for place in range(16)]
    return lax.ppermute(values, COLUMN, pairs)


def minus_four(values):
    pairs = [(place, (place - 4 + 8 * (place & 1)) & 15) for place in range(16)]
    return lax.ppermute(values, COLUMN, pairs)


def across(values):
    return lax.ppermute(values, COLUMN, [(place, place ^ 11) for place in range(16)])


def near_shift(values, step):
    pairs = [(place, (place & 12) | ((place + step) & 3)) for place in range(16)]
    return lax.ppermute(values, COLUMN, pairs)


def on_device(queries, keys_values, grad_out, send_tiles, recv_slot, tile_seq):
    n_replicas = lax.axis_size("dp")
    replica = lax.axis_index("dp")
    tile_count, tile_rows, row_width = queries.shape
    sliver = keys_values.shape[1]
    slot_cap = send_tiles.shape[2]
    slots = n_replicas * slot_cap
    pairs = tile_count // PAIR
    my_send = send_tiles[0]
    outgoing = my_send.T
    my_recv = lax.dynamic_index_in_dim(recv_slot, replica, 0, keepdims=False)
    place = lax.axis_index(COLUMN).astype(jnp.int32).reshape(1)
    traveling = jax.ShapeDtypeStruct(
        (n_replicas, 2, slot_cap, 2, 2, sliver, HD), keys_values.dtype
    )
    half_shape = jax.ShapeDtypeStruct((2, 2, pairs, PAIR * sliver, HD), keys_values.dtype)

    def over_plane(values):
        return lax.all_to_all(
            values.reshape((2 * n_replicas,) + values.shape[2:]),
            PLANE, split_axis=0, concat_axis=0, tiled=True,
        ).reshape(values.shape)

    kv_blocks = keys_values.reshape(tile_count, sliver, 2 * KV, HD).transpose(0, 2, 1, 3)
    kv_arrived = over_plane(
        local_call(kv_pack_kernel, "kv_pack", [outgoing], [kv_blocks], traveling)
    )
    own, other, plus, minus = local_call(
        kv_unpack_kernel, "kv_unpack", [my_recv, place], [kv_arrived], (half_shape,) * 4
    )
    qg_packed = pack(outgoing, queries, grad_out)
    far_plus, far_minus, far_across = plus_four(plus), minus_four(minus), across(other)
    qg_packed, far_plus = lax.optimization_barrier((qg_packed, far_plus))
    qg_arrived = lax.all_to_all(
        qg_packed.reshape(n_replicas, slot_cap, 2, tile_rows, row_width),
        "dp", split_axis=0, concat_axis=0, tiled=True,
    ).reshape(slots, 2, tile_rows, row_width)
    mine = jnp.stack([own, far_plus, far_minus, far_across])
    chunks = [mine] + [near_shift(mine, step) for step in range(1, NEAR)]

    seq = tile_seq[0]
    start = jnp.sum((seq[None, :] < seq[:, None]).astype(jnp.int32), axis=1)
    query_back, *terms = attention(my_recv, start, place, qg_arrived, chunks)
    near = [terms[0]] + [near_shift(terms[step], -step) for step in range(1, NEAR)]
    near[1], query_back = lax.optimization_barrier((near[1], query_back))
    query_returned = lax.all_to_all(
        query_back.reshape(n_replicas, slot_cap, tile_rows, row_width),
        "dp", split_axis=0, concat_axis=0, tiled=True,
    )
    sums = [
        sum(term[origin].astype(jnp.float32) for term in near).astype(jnp.bfloat16)
        for origin in range(4)
    ]
    swapped = [sums[0], minus_four(sums[1]), plus_four(sums[2]), across(sums[3])]
    swapped, query_returned = lax.optimization_barrier((swapped, query_returned))
    kv_returned = over_plane(
        local_call(kv_back_kernel, "kv_back", [my_recv, place], swapped, traveling)
    )

    flat_slots = jnp.arange(slots)
    own_slots = replica * slot_cap + jnp.arange(slot_cap)
    slot_used = jnp.any(recv_slot[:, None, :] == own_slots[None, :, None], axis=2)
    matched = slot_used[:, :, None] & (my_send[:, :, None] == jnp.arange(tile_count)[None, None, :])
    anchor = jnp.sum(
        jnp.where(matched, flat_slots.reshape(n_replicas, slot_cap)[:, :, None], 0), axis=(0, 1)
    )
    grad_queries = query_returned.reshape(slots, tile_rows, row_width)[anchor]
    kv_final = local_call(
        kv_final_kernel, "kv_final", [anchor], [kv_returned],
        jax.ShapeDtypeStruct(kv_blocks.shape, keys_values.dtype),
    )
    grad_keys_values = kv_final.transpose(0, 2, 1, 3).reshape(keys_values.shape)
    return (grad_queries, grad_keys_values)


def solution(mesh):
    names = PLANE + COLUMN
    fine = Mesh(mesh.devices.reshape(mesh.devices.shape[0], 2, 2, 2, 4), names)
    tensor = ("xh",) + COLUMN
    in_specs = (
        P("dp", None, tensor),
        P("dp", tensor, None),
        P("dp", None, tensor),
        P("dp", None, None),
        P(),
        P("dp", None),
    )
    out_specs = (P("dp", None, tensor), P("dp", tensor, None))
    return jax.shard_map(
        on_device, mesh=fine, in_specs=in_specs, out_specs=out_specs, check_vma=False
    )
```

```python
import functools

import jax
import jax.numpy as jnp
from jax import lax
from jax.experimental import pallas as pl
from jax.experimental.pallas import tpu as pltpu
from jax.sharding import Mesh
from jax.sharding import PartitionSpec as P

HD = 128
KV = 4
PAIR = 2
SCALING = HD ** (-0.5)
LOG2E = 1.4426950408889634
PLANE = ("dp", "xh")
NEAR = 4


def matmul(a, b, contract):
    return lax.dot_general(a, b, (contract, ((), ())), preferred_element_type=jnp.float32)


def pack_kernel(index_ref, q_ref, g_ref, out_ref):
    def body(slot, _):
        tile = index_ref[slot & 1, slot >> 1]
        out_ref[slot, 0] = q_ref[tile]
        out_ref[slot, 1] = g_ref[tile]
        return 0

    lax.fori_loop(0, out_ref.shape[0], body, 0)


def pack(index, queries, grad_out):
    slots = index.size
    return pl.pallas_call(
        pack_kernel,
        out_shape=jax.ShapeDtypeStruct((slots, 2) + queries.shape[1:], queries.dtype),
        in_specs=[
            pl.BlockSpec(memory_space=pltpu.SMEM),
            pl.BlockSpec(memory_space=pltpu.VMEM),
            pl.BlockSpec(memory_space=pltpu.VMEM),
        ],
        out_specs=pl.BlockSpec(memory_space=pltpu.VMEM),
        compiler_params=pltpu.CompilerParams(vmem_limit_bytes=24 * 2**20),
        name="pack_rows",
    )(index, queries, grad_out)


def attention_kernel(
    recv_ref, start_ref, place_ref, qg_ref, kv0, kv1, kv2, kv3, dq_ref, dkv0, dkv1, dkv2, dkv3,
    qg_all, k_all, kt_all, v_all, dk_all, dv_all, weights_all, dprobs_all, peaks, dqt, arrived,
):
    blocks = k_all.shape[0]
    width = k_all.shape[1]
    tile_rows = width // PAIR
    part = width // NEAR
    factor = SCALING * LOG2E

    def tile_copy(tile, kind):
        return pltpu.make_async_copy(
            qg_ref.at[recv_ref[tile], kind], qg_all.at[kind, tile], arrived.at[kind, tile]
        )

    def fetch(tile, _):
        tile_copy(tile, 0).start()
        tile_copy(tile, 1).start()
        return 0

    lax.fori_loop(0, PAIR * blocks, fetch, 0)

    def stage(block, _):
        for slot, ref in enumerate((kv0, kv1, kv2, kv3)):
            rows = slice(slot * part, (slot + 1) * part)
            key = ref[:, :, 0, block].astype(jnp.float32).reshape(part, HD)
            value = ref[:, :, 1, block].astype(jnp.float32).reshape(part, HD)
            k_all[block, rows] = key.astype(jnp.bfloat16)
            v_all[block, rows] = value.astype(jnp.bfloat16)
        kt_all[block] = k_all[block].astype(jnp.float32).T.astype(jnp.bfloat16)
        return 0

    lax.fori_loop(0, blocks, stage, 0)

    row = lax.broadcasted_iota(jnp.int32, (width, 1), 0)
    holder = (place_ref[0] & 12) | ((place_ref[0] - (row >> 6)) & 3)
    group = jnp.where(holder < 8, holder, 3 - holder) & 3
    origin = (row >> 4) & 3
    source = origin * 4 + jnp.where(origin < 2, group, 3 - group)
    key_offset = (
        ((row >> 2) & 1) * tile_rows + ((row >> 3) & 1) * 64 + source * 4 + (row & 3)
    )
    lane = lax.broadcasted_iota(jnp.int32, (1, width), 1)

    def query_block(block, _):
        for tile in (PAIR * block, PAIR * block + 1):
            tile_copy(tile, 0).wait()
            tile_copy(tile, 1).wait()
        tiles = pl.ds(PAIR * block, PAIR)
        query = qg_all[0, tiles].reshape(width, HD)
        grad = qg_all[1, tiles].reshape(width, HD)
        start_low = start_ref[PAIR * block]
        start_high = start_ref[PAIR * block + 1]
        lowest = start_low // PAIR
        row_start = jnp.where(lane < tile_rows, start_low, start_high) * tile_rows

        def products(other, masked_by_order):
            score = matmul(k_all[other], query, ((1,), (1,)))
            dprobs = matmul(v_all[other], grad, ((1,), (1,)))
            allowed = key_offset >= row_start - other * width
            if masked_by_order:
                allowed = allowed & (key_offset <= lane)
            score = jnp.where(allowed, score, -jnp.inf)
            peak = jnp.maximum(jnp.max(score, axis=0, keepdims=True), -1e30)
            weights = jnp.exp2(score * factor - peak * factor)
            weights_all[other] = weights
            dprobs_all[other] = dprobs
            peaks[other] = jnp.broadcast_to(peak, peaks.shape[1:])
            total = jnp.sum(weights, axis=0, keepdims=True)
            weighted = jnp.sum(weights * dprobs, axis=0, keepdims=True)
            return peak, total, weighted

        def merge(other, state):
            peak, total, weighted = state
            new_peak, new_total, new_weighted = products(other, False)
            top = jnp.maximum(peak, new_peak)
            old, new = jnp.exp2((peak - top) * factor), jnp.exp2((new_peak - top) * factor)
            return top, total * old + new_total * new, weighted * old + new_weighted * new

        peak, total, weighted = lax.fori_loop(lowest, block, merge, products(block, True))
        inverse = 1.0 / total
        delta = weighted * inverse

        def terms(other):
            scale = jnp.exp2((peaks[other][:1] - peak) * factor) * inverse
            probs = weights_all[other] * scale
            dscores = (probs * (dprobs_all[other] - delta)).astype(jnp.bfloat16)
            grad_value = matmul(probs.astype(jnp.bfloat16), grad, ((1,), (0,)))
            grad_key = matmul(dscores, query, ((1,), (0,)))
            grad_query = matmul(kt_all[other], dscores, ((1,), (0,)))
            return grad_key, grad_value, grad_query

        grad_key, grad_value, grad_query = terms(block)
        dk_all[block] = grad_key
        dv_all[block] = grad_value
        dqt[...] = grad_query

        def earlier(other, _):
            grad_key, grad_value, grad_query = terms(other)
            dk_all[other] += grad_key
            dv_all[other] += grad_value
            dqt[...] += grad_query
            return 0

        lax.fori_loop(lowest, block, earlier, 0)
        result = (dqt[...] * SCALING).T.astype(jnp.bfloat16)
        dq_ref[recv_ref[PAIR * block]] = result[:tile_rows]
        dq_ref[recv_ref[PAIR * block + 1]] = result[tile_rows:]
        return 0

    lax.fori_loop(0, blocks, query_block, 0)

    def unstage(block, _):
        for slot, ref in enumerate((dkv0, dkv1, dkv2, dkv3)):
            rows = slice(slot * part, (slot + 1) * part)
            shape = ref.shape[:2] + ref.shape[4:]
            ref[:, :, 0, block] = (dk_all[block, rows] * SCALING).reshape(shape).astype(jnp.bfloat16)
            ref[:, :, 1, block] = dv_all[block, rows].reshape(shape).astype(jnp.bfloat16)
        return 0

    lax.fori_loop(0, blocks, unstage, 0)


def attention(my_recv, start, place, qg, chunks):
    slots, _, tile_rows, _ = qg.shape
    blocks = my_recv.shape[0] // PAIR
    width = PAIR * tile_rows
    vmem = pl.BlockSpec(memory_space=pltpu.VMEM)
    smem = pl.BlockSpec(memory_space=pltpu.SMEM)
    return pl.pallas_call(
        attention_kernel,
        out_shape=(jax.ShapeDtypeStruct((slots, tile_rows, HD), jnp.bfloat16),)
        + (jax.ShapeDtypeStruct(chunks[0].shape, jnp.bfloat16),) * NEAR,
        in_specs=[smem] * 3 + [pl.BlockSpec(memory_space=pl.ANY)] + [vmem] * NEAR,
        out_specs=(vmem,) * (1 + NEAR),
        scratch_shapes=[
            pltpu.VMEM((2, PAIR * blocks, tile_rows, HD), jnp.bfloat16),
            pltpu.VMEM((blocks, width, HD), jnp.bfloat16),
            pltpu.VMEM((blocks, HD, width), jnp.bfloat16),
            pltpu.VMEM((blocks, width, HD), jnp.bfloat16),
            pltpu.VMEM((blocks, width, HD), jnp.float32),
            pltpu.VMEM((blocks, width, HD), jnp.float32),
            pltpu.VMEM((blocks, width, width), jnp.float32),
            pltpu.VMEM((blocks, width, width), jnp.float32),
            pltpu.VMEM((blocks, 8, width), jnp.float32),
            pltpu.VMEM((HD, width), jnp.float32),
            pltpu.SemaphoreType.DMA((2, PAIR * blocks)),
        ],
        compiler_params=pltpu.CompilerParams(vmem_limit_bytes=24 * 2**20),
        cost_estimate=pl.CostEstimate(
            flops=2 * 10**9, bytes_accessed=6 * 2**20, transcendentals=2 * 10**6
        ),
        name="attention_backward",
    )(my_recv, start, place, qg, *chunks)


def kv_pack_kernel(index_ref, kv_ref, out_ref):
    def body(slot, _):
        tile = index_ref[slot & 1, slot >> 1]
        piece = kv_ref[tile].reshape((2, 2, 2) + kv_ref.shape[2:])
        for half in range(2):
            out_ref[slot >> 1, half, slot & 1] = piece[:, half]
        return 0

    lax.fori_loop(0, 2 * index_ref.shape[1], body, 0, unroll=4)


def kv_unpack_kernel(recv_ref, kv_ref, out_ref):
    def body(pair, _):
        slots = (recv_ref[PAIR * pair], recv_ref[PAIR * pair + 1])
        for half in range(2):
            for kind in range(2):
                for head in range(2):
                    rows = [
                        kv_ref[slot >> 1, half, slot & 1, kind, head].astype(jnp.float32)
                        for slot in slots
                    ]
                    both = jnp.concatenate(rows, axis=0).astype(jnp.bfloat16)
                    out_ref[2 * head, half, kind, pair] = both
                    out_ref[2 * head + 1, half, kind, pair] = both
        return 0

    lax.fori_loop(0, recv_ref.shape[0] // PAIR, body, 0)


def kv_back_kernel(recv_ref, terms_ref, out_ref):
    sliver = out_ref.shape[-2]

    def body(pair, _):
        slots = (recv_ref[PAIR * pair], recv_ref[PAIR * pair + 1])
        for half in range(2):
            for kind in range(2):
                for head in range(2):
                    total = terms_ref[2 * head, half, kind, pair].astype(jnp.float32)
                    total += terms_ref[2 * head + 1, half, kind, pair].astype(jnp.float32)
                    for order, slot in enumerate(slots):
                        rows = total[order * sliver : (order + 1) * sliver]
                        out_ref[slot >> 1, half, slot & 1, kind, head] = rows.astype(jnp.bfloat16)
        return 0

    lax.fori_loop(0, recv_ref.shape[0] // PAIR, body, 0)


def kv_final_kernel(anchor_ref, kv_ref, out_ref):
    def body(tile, _):
        slot = anchor_ref[tile]
        piece = kv_ref[slot >> 1, :, slot & 1]
        for half in range(2):
            for kind in range(2):
                for head in range(2):
                    out_ref[tile, kind * 4 + half * 2 + head] = piece[half, kind, head]
        return 0

    lax.fori_loop(0, anchor_ref.shape[0], body, 0)


def local_call(kernel, name, scalars, arrays, out_shape):
    vmem = pl.BlockSpec(memory_space=pltpu.VMEM)
    smem = pl.BlockSpec(memory_space=pltpu.SMEM)
    return pl.pallas_call(
        kernel,
        out_shape=out_shape,
        in_specs=[smem] * len(scalars) + [vmem] * len(arrays),
        out_specs=jax.tree.map(lambda _: vmem, out_shape),
        compiler_params=pltpu.CompilerParams(vmem_limit_bytes=16 * 2**20),
        name=name,
    )(*scalars, *arrays)


def between_cubes(values):
    groups = [[base, base + 4, 11 - base, 15 - base] for base in range(4)]
    return lax.all_to_all(
        values, "z", split_axis=0, concat_axis=0, axis_index_groups=groups, tiled=True
    )


def near_shift(values, step):
    pairs = [(place, (place & 12) | ((place + step) & 3)) for place in range(16)]
    return lax.ppermute(values, "z", pairs)


def on_device(queries, keys_values, grad_out, send_tiles, recv_slot, tile_seq):
    n_replicas = lax.axis_size("dp")
    replica = lax.axis_index("dp")
    tile_count, tile_rows, row_width = queries.shape
    sliver = keys_values.shape[1]
    slot_cap = send_tiles.shape[2]
    slots = n_replicas * slot_cap
    pairs = tile_count // PAIR
    my_send = send_tiles[0]
    outgoing = my_send.T
    my_recv = lax.dynamic_index_in_dim(recv_slot, replica, 0, keepdims=False)
    place = lax.axis_index("z").astype(jnp.int32).reshape(1)
    traveling = jax.ShapeDtypeStruct(
        (n_replicas, 2, slot_cap, 2, 2, sliver, HD), keys_values.dtype
    )
    far_shape = jax.ShapeDtypeStruct((4, 2, 2, pairs, PAIR * sliver, HD), keys_values.dtype)

    def over_plane(values):
        return lax.all_to_all(
            values.reshape((2 * n_replicas,) + values.shape[2:]),
            PLANE, split_axis=0, concat_axis=0, tiled=True,
        ).reshape(values.shape)

    kv_blocks = keys_values.reshape(tile_count, sliver, 2 * KV, HD).transpose(0, 2, 1, 3)
    kv_arrived = over_plane(
        local_call(kv_pack_kernel, "kv_pack", [outgoing], [kv_blocks], traveling)
    )
    mine = between_cubes(
        local_call(kv_unpack_kernel, "kv_unpack", [my_recv], [kv_arrived], far_shape)
    )
    qg_packed = pack(outgoing, queries, grad_out)
    qg_arrived = lax.all_to_all(
        qg_packed.reshape(n_replicas, slot_cap, 2, tile_rows, row_width),
        "dp", split_axis=0, concat_axis=0, tiled=True,
    ).reshape(slots, 2, tile_rows, row_width)
    chunks = [mine] + [near_shift(mine, step) for step in range(1, NEAR)]

    seq = tile_seq[0]
    start = jnp.sum((seq[None, :] < seq[:, None]).astype(jnp.int32), axis=1)
    query_back, *terms = attention(my_recv, start, place, qg_arrived, chunks)
    near = [terms[0]] + [near_shift(terms[step], -step) for step in range(1, NEAR)]
    query_returned = lax.all_to_all(
        query_back.reshape(n_replicas, slot_cap, tile_rows, row_width),
        "dp", split_axis=0, concat_axis=0, tiled=True,
    )
    near_sum = sum(term.astype(jnp.float32) for term in near).astype(jnp.bfloat16)
    near_sum, query_returned = lax.optimization_barrier((near_sum, query_returned))
    far = between_cubes(near_sum)
    kv_returned = over_plane(
        local_call(kv_back_kernel, "kv_back", [my_recv], [far], traveling)
    )

    flat_slots = jnp.arange(slots)
    own_slots = replica * slot_cap + jnp.arange(slot_cap)
    slot_used = jnp.any(recv_slot[:, None, :] == own_slots[None, :, None], axis=2)
    matched = slot_used[:, :, None] & (my_send[:, :, None] == jnp.arange(tile_count)[None, None, :])
    anchor = jnp.sum(
        jnp.where(matched, flat_slots.reshape(n_replicas, slot_cap)[:, :, None], 0), axis=(0, 1)
    )
    grad_queries = query_returned.reshape(slots, tile_rows, row_width)[anchor]
    kv_final = local_call(
        kv_final_kernel, "kv_final", [anchor], [kv_returned],
        jax.ShapeDtypeStruct(kv_blocks.shape, keys_values.dtype),
    )
    grad_keys_values = kv_final.transpose(0, 2, 1, 3).reshape(keys_values.shape)
    return (grad_queries, grad_keys_values)


def solution(mesh):
    fine = Mesh(mesh.devices.reshape(mesh.devices.shape[0], 2, 16), ("dp", "xh", "z"))
    tensor = ("xh", "z")
    in_specs = (
        P("dp", None, tensor),
        P("dp", tensor, None),
        P("dp", None, tensor),
        P("dp", None, None),
        P(),
        P("dp", None),
    )
    out_specs = (P("dp", None, tensor), P("dp", tensor, None))
    return jax.shard_map(
        on_device, mesh=fine, in_specs=in_specs, out_specs=out_specs, check_vma=False
    )
```

```python
import functools

import jax
import jax.numpy as jnp
from jax import lax
from jax.experimental import pallas as pl
from jax.experimental.pallas import tpu as pltpu
from jax.sharding import Mesh
from jax.sharding import PartitionSpec as P

HD = 128
KV = 4
PAIR = 2
SCALING = HD ** (-0.5)
LOG2E = 1.4426950408889634
PLANE = ("dp", "xh")
FAR = (4, 15, 11)
NEAR = 4


def matmul(a, b, contract):
    return lax.dot_general(a, b, (contract, ((), ())), preferred_element_type=jnp.float32)


def pack_kernel(index_ref, q_ref, g_ref, out_ref):
    def body(slot, _):
        tile = index_ref[slot & 1, slot >> 1]
        out_ref[slot, 0] = q_ref[tile]
        out_ref[slot, 1] = g_ref[tile]
        return 0

    lax.fori_loop(0, out_ref.shape[0], body, 0)


def pack(index, queries, grad_out):
    slots = index.size
    return pl.pallas_call(
        pack_kernel,
        out_shape=jax.ShapeDtypeStruct((slots, 2) + queries.shape[1:], queries.dtype),
        in_specs=[
            pl.BlockSpec(memory_space=pltpu.SMEM),
            pl.BlockSpec(memory_space=pltpu.VMEM),
            pl.BlockSpec(memory_space=pltpu.VMEM),
        ],
        out_specs=pl.BlockSpec(memory_space=pltpu.VMEM),
        compiler_params=pltpu.CompilerParams(vmem_limit_bytes=24 * 2**20),
        name="pack_rows",
    )(index, queries, grad_out)


def attention_kernel(
    recv_ref, start_ref, place_ref, qg_ref, *refs
):
    kv_refs, dq_ref, dkv_refs = refs[: 2 * NEAR], refs[2 * NEAR], refs[2 * NEAR + 1 : 4 * NEAR + 1]
    k_all, kt_all, v_all, dk_all, dv_all, scores, dprobs, dqt = refs[4 * NEAR + 1 :]
    blocks = k_all.shape[0]
    width = k_all.shape[1]
    tile_rows = width // PAIR
    part = width // NEAR
    own_part = part // 4
    factor = SCALING * LOG2E

    def rows_of(slot):
        begin = (slot % NEAR) * part
        if slot < NEAR:
            return slice(begin, begin + own_part)
        return slice(begin + own_part, begin + part)

    def stage(block, _):
        for slot, ref in enumerate(kv_refs):
            rows = rows_of(slot)
            count = rows.stop - rows.start
            key = ref[:, :, 0, block].astype(jnp.float32).reshape(count, HD)
            value = ref[:, :, 1, block].astype(jnp.float32).reshape(count, HD)
            k_all[block, rows] = key.astype(jnp.bfloat16)
            v_all[block, rows] = value.astype(jnp.bfloat16)
        kt_all[block] = k_all[block].astype(jnp.float32).T.astype(jnp.bfloat16)
        return 0

    lax.fori_loop(0, blocks, stage, 0)

    row = lax.broadcasted_iota(jnp.int32, (width, 1), 0)
    holder = (place_ref[0] & 12) | ((place_ref[0] - (row >> 6)) & 3)
    source = holder ^ (((row >> 4) & 1) * 4) ^ (((row >> 5) & 1) * 15)
    key_offset = (
        ((row >> 2) & 1) * tile_rows + ((row >> 3) & 1) * 64 + source * 4 + (row & 3)
    )
    lane = lax.broadcasted_iota(jnp.int32, (1, width), 1)

    def query_block(block, _):
        first = recv_ref[PAIR * block]
        second = recv_ref[PAIR * block + 1]
        query = jnp.concatenate([qg_ref[first, 0], qg_ref[second, 0]], axis=0)
        grad = jnp.concatenate([qg_ref[first, 1], qg_ref[second, 1]], axis=0)
        start_low = start_ref[PAIR * block]
        start_high = start_ref[PAIR * block + 1]
        lowest = start_low // PAIR
        row_start = jnp.where(lane < tile_rows, start_low, start_high) * tile_rows

        def products(other, masked_by_order, peak):
            score = matmul(k_all[other], query, ((1,), (1,)))
            key_pos = key_offset + other * width
            allowed = key_pos >= row_start
            if masked_by_order:
                allowed = allowed & (key_offset <= lane)
            score = jnp.where(allowed, score, -jnp.inf)
            scores[other] = score
            dprobs[other] = matmul(v_all[other], grad, ((1,), (1,)))
            return jnp.maximum(peak, jnp.max(score, axis=0, keepdims=True))

        peak = products(block, True, jnp.full((1, width), -jnp.inf, jnp.float32))
        peak = lax.fori_loop(lowest, block, lambda other, m: products(other, False, m), peak)
        shift = peak * factor

        def sums(other, totals):
            weights = jnp.exp2(scores[other] * factor - shift)
            scores[other] = weights
            return (
                totals[0] + jnp.sum(weights, axis=0, keepdims=True),
                totals[1] + jnp.sum(weights * dprobs[other], axis=0, keepdims=True),
            )

        zeros = jnp.zeros((1, width), jnp.float32)
        total, weighted = lax.fori_loop(lowest, block + 1, sums, (zeros, zeros))
        inverse = 1.0 / total
        delta = weighted * inverse

        def terms(other):
            probs = scores[other] * inverse
            dscores = (probs * (dprobs[other] - delta)).astype(jnp.bfloat16)
            grad_value = matmul(probs.astype(jnp.bfloat16), grad, ((1,), (0,)))
            grad_key = matmul(dscores, query, ((1,), (0,)))
            grad_query = matmul(kt_all[other], dscores, ((1,), (0,)))
            return grad_key, grad_value, grad_query

        grad_key, grad_value, grad_query = terms(block)
        dk_all[block] = grad_key
        dv_all[block] = grad_value
        dqt[...] = grad_query

        def earlier(other, _):
            grad_key, grad_value, grad_query = terms(other)
            dk_all[other] += grad_key
            dv_all[other] += grad_value
            dqt[...] += grad_query
            return 0

        lax.fori_loop(lowest, block, earlier, 0)
        result = (dqt[...] * SCALING).T.astype(jnp.bfloat16)
        dq_ref[first] = result[:tile_rows]
        dq_ref[second] = result[tile_rows:]
        return 0

    lax.fori_loop(0, blocks, query_block, 0)

    def unstage(block, _):
        for slot, ref in enumerate(dkv_refs):
            rows = rows_of(slot)
            shape = ref.shape[:2] + ref.shape[4:]
            ref[:, :, 0, block] = (dk_all[block, rows] * SCALING).reshape(shape).astype(jnp.bfloat16)
            ref[:, :, 1, block] = dv_all[block, rows].reshape(shape).astype(jnp.bfloat16)
        return 0

    lax.fori_loop(0, blocks, unstage, 0)


def attention(my_recv, start, place, qg, chunks):
    slots, _, tile_rows, _ = qg.shape
    blocks = my_recv.shape[0] // PAIR
    width = PAIR * tile_rows
    vmem = pl.BlockSpec(memory_space=pltpu.VMEM)
    smem = pl.BlockSpec(memory_space=pltpu.SMEM)
    return pl.pallas_call(
        attention_kernel,
        out_shape=(jax.ShapeDtypeStruct((slots, tile_rows, HD), jnp.bfloat16),)
        + tuple(jax.ShapeDtypeStruct(chunk.shape, jnp.bfloat16) for chunk in chunks),
        in_specs=[smem] * 3 + [vmem] * (1 + 2 * NEAR),
        out_specs=(vmem,) * (1 + 2 * NEAR),
        scratch_shapes=[
            pltpu.VMEM((blocks, width, HD), jnp.bfloat16),
            pltpu.VMEM((blocks, HD, width), jnp.bfloat16),
            pltpu.VMEM((blocks, width, HD), jnp.bfloat16),
            pltpu.VMEM((blocks, width, HD), jnp.float32),
            pltpu.VMEM((blocks, width, HD), jnp.float32),
            pltpu.VMEM((blocks, width, width), jnp.float32),
            pltpu.VMEM((blocks, width, width), jnp.float32),
            pltpu.VMEM((HD, width), jnp.float32),
        ],
        compiler_params=pltpu.CompilerParams(vmem_limit_bytes=24 * 2**20),
        cost_estimate=pl.CostEstimate(
            flops=2 * 10**9, bytes_accessed=6 * 2**20, transcendentals=2 * 10**6
        ),
        name="attention_backward",
    )(my_recv, start, place, qg, *chunks)


def kv_pack_kernel(index_ref, kv_ref, out_ref):
    def body(slot, _):
        tile = index_ref[slot & 1, slot >> 1]
        piece = kv_ref[tile].reshape((2, 2, 2) + kv_ref.shape[2:])
        for half in range(2):
            out_ref[slot >> 1, half, slot & 1] = piece[:, half]
        return 0

    lax.fori_loop(0, 2 * index_ref.shape[1], body, 0, unroll=4)


def kv_unpack_kernel(recv_ref, place_ref, kv_ref, own_ref, other_ref):
    head = place_ref[0] >> 3

    def body(pair, _):
        low = recv_ref[PAIR * pair]
        high = recv_ref[PAIR * pair + 1]
        for half in range(2):
            for kind in range(2):
                for ref, which in ((own_ref, head), (other_ref, 1 - head)):
                    rows = [
                        kv_ref[slot >> 1, half, slot & 1, kind, which].astype(jnp.float32)
                        for slot in (low, high)
                    ]
                    ref[half, kind, pair] = jnp.concatenate(rows, axis=0).astype(jnp.bfloat16)
        return 0

    lax.fori_loop(0, recv_ref.shape[0] // PAIR, body, 0)


def kv_back_kernel(recv_ref, place_ref, p0, p1, p2, p3, out_ref):
    head = place_ref[0] >> 3
    sliver = out_ref.shape[-2]

    def body(pair, _):
        slots = (recv_ref[PAIR * pair], recv_ref[PAIR * pair + 1])
        for half in range(2):
            for kind in range(2):
                for a, b, which in ((p0, p1, head), (p2, p3, 1 - head)):
                    total = a[half, kind, pair].astype(jnp.float32) + b[half, kind, pair].astype(jnp.float32)
                    for order, slot in enumerate(slots):
                        rows = total[order * sliver : (order + 1) * sliver]
                        out_ref[slot >> 1, half, slot & 1, kind, which] = rows.astype(jnp.bfloat16)
        return 0

    lax.fori_loop(0, recv_ref.shape[0] // PAIR, body, 0)


def kv_final_kernel(anchor_ref, kv_ref, out_ref):
    def body(tile, _):
        slot = anchor_ref[tile]
        piece = kv_ref[slot >> 1, :, slot & 1]
        for half in range(2):
            for kind in range(2):
                for head in range(2):
                    out_ref[tile, kind * 4 + half * 2 + head] = piece[half, kind, head]
        return 0

    lax.fori_loop(0, anchor_ref.shape[0], body, 0)


def local_call(kernel, name, scalars, arrays, out_shape):
    vmem = pl.BlockSpec(memory_space=pltpu.VMEM)
    smem = pl.BlockSpec(memory_space=pltpu.SMEM)
    return pl.pallas_call(
        kernel,
        out_shape=out_shape,
        in_specs=[smem] * len(scalars) + [vmem] * len(arrays),
        out_specs=jax.tree.map(lambda _: vmem, out_shape),
        compiler_params=pltpu.CompilerParams(vmem_limit_bytes=16 * 2**20),
        name=name,
    )(*scalars, *arrays)


def far_swap(values, flip):
    return lax.ppermute(values, "z", [(place, place ^ flip) for place in range(16)])


def near_shift(values, step):
    pairs = [(place, (place & 12) | ((place + step) & 3)) for place in range(16)]
    return lax.ppermute(values, "z", pairs)


def near_gather(values):
    return [values] + [near_shift(values, step) for step in range(1, NEAR)]


def near_terms(terms):
    return [terms[0]] + [near_shift(terms[step], -step) for step in range(1, NEAR)]


def total(terms, index):
    return sum(term[index].astype(jnp.float32) for term in terms).astype(jnp.bfloat16)


def on_device(queries, keys_values, grad_out, send_tiles, recv_slot, tile_seq):
    n_replicas = lax.axis_size("dp")
    replica = lax.axis_index("dp")
    tile_count, tile_rows, row_width = queries.shape
    sliver = keys_values.shape[1]
    slot_cap = send_tiles.shape[2]
    slots = n_replicas * slot_cap
    pairs = tile_count // PAIR
    my_send = send_tiles[0]
    outgoing = my_send.T
    my_recv = lax.dynamic_index_in_dim(recv_slot, replica, 0, keepdims=False)
    place = lax.axis_index("z").astype(jnp.int32).reshape(1)
    traveling = jax.ShapeDtypeStruct(
        (n_replicas, 2, slot_cap, 2, 2, sliver, HD), keys_values.dtype
    )
    half_shape = jax.ShapeDtypeStruct((2, 2, pairs, PAIR * sliver, HD), keys_values.dtype)

    def over_plane(values):
        return lax.all_to_all(
            values.reshape((2 * n_replicas,) + values.shape[2:]),
            PLANE, split_axis=0, concat_axis=0, tiled=True,
        ).reshape(values.shape)

    kv_blocks = keys_values.reshape(tile_count, sliver, 2 * KV, HD).transpose(0, 2, 1, 3)
    kv_arrived = over_plane(
        local_call(kv_pack_kernel, "kv_pack", [outgoing], [kv_blocks], traveling)
    )
    own, other = local_call(
        kv_unpack_kernel, "kv_unpack", [my_recv, place], [kv_arrived], (half_shape, half_shape)
    )
    qg_packed = pack(outgoing, queries, grad_out)
    qg_arrived = lax.all_to_all(
        qg_packed.reshape(n_replicas, slot_cap, 2, tile_rows, row_width),
        "dp", split_axis=0, concat_axis=0, tiled=True,
    ).reshape(slots, 2, tile_rows, row_width)
    far = jnp.stack([far_swap(own, FAR[0]), far_swap(other, FAR[1]), far_swap(other, FAR[2])])
    own_chunks = near_gather(own[None])
    far, own_chunks, qg_arrived = lax.optimization_barrier((far, own_chunks, qg_arrived))
    chunks = own_chunks + near_gather(far)

    seq = tile_seq[0]
    start = jnp.sum((seq[None, :] < seq[:, None]).astype(jnp.int32), axis=1)
    query_back, *terms = attention(my_recv, start, place, qg_arrived, chunks)
    query_returned = lax.all_to_all(
        query_back.reshape(n_replicas, slot_cap, tile_rows, row_width),
        "dp", split_axis=0, concat_axis=0, tiled=True,
    )
    far_terms = near_terms(terms[NEAR:])
    back = [far_swap(total(far_terms, index), flip) for index, flip in enumerate(FAR)]
    own_sum = total(near_terms(terms[:NEAR]), 0)
    swapped, query_returned = lax.optimization_barrier(([own_sum] + back, query_returned))
    kv_returned = over_plane(
        local_call(kv_back_kernel, "kv_back", [my_recv, place], swapped, traveling)
    )

    flat_slots = jnp.arange(slots)
    own_slots = replica * slot_cap + jnp.arange(slot_cap)
    slot_used = jnp.any(recv_slot[:, None, :] == own_slots[None, :, None], axis=2)
    matched = slot_used[:, :, None] & (my_send[:, :, None] == jnp.arange(tile_count)[None, None, :])
    anchor = jnp.sum(
        jnp.where(matched, flat_slots.reshape(n_replicas, slot_cap)[:, :, None], 0), axis=(0, 1)
    )
    grad_queries = query_returned.reshape(slots, tile_rows, row_width)[anchor]
    kv_final = local_call(
        kv_final_kernel, "kv_final", [anchor], [kv_returned],
        jax.ShapeDtypeStruct(kv_blocks.shape, keys_values.dtype),
    )
    grad_keys_values = kv_final.transpose(0, 2, 1, 3).reshape(keys_values.shape)
    return (grad_queries, grad_keys_values)


def solution(mesh):
    fine = Mesh(mesh.devices.reshape(mesh.devices.shape[0], 2, 16), ("dp", "xh", "z"))
    tensor = ("xh", "z")
    in_specs = (
        P("dp", None, tensor),
        P("dp", tensor, None),
        P("dp", None, tensor),
        P("dp", None, None),
        P(),
        P("dp", None),
    )
    out_specs = (P("dp", None, tensor), P("dp", tensor, None))
    return jax.shard_map(
        on_device, mesh=fine, in_specs=in_specs, out_specs=out_specs, check_vma=False
    )
```

```python
import functools

import jax
import jax.numpy as jnp
from jax import lax
from jax.experimental import pallas as pl
from jax.experimental.pallas import tpu as pltpu
from jax.sharding import Mesh
from jax.sharding import PartitionSpec as P

HD = 128
KV = 4
PAIR = 2
SCALING = HD ** (-0.5)
LOG2E = 1.4426950408889634
PLANE = ("dp", "xh")
FAR = (4, 15, 11)
NEAR = 4


def matmul(a, b, contract):
    return lax.dot_general(a, b, (contract, ((), ())), preferred_element_type=jnp.float32)


def pack_kernel(index_ref, q_ref, g_ref, out_ref):
    def body(slot, _):
        tile = index_ref[slot & 1, slot >> 1]
        out_ref[slot, 0] = q_ref[tile]
        out_ref[slot, 1] = g_ref[tile]
        return 0

    lax.fori_loop(0, out_ref.shape[0], body, 0)


def pack(index, queries, grad_out):
    slots = index.size
    return pl.pallas_call(
        pack_kernel,
        out_shape=jax.ShapeDtypeStruct((slots, 2) + queries.shape[1:], queries.dtype),
        in_specs=[
            pl.BlockSpec(memory_space=pltpu.SMEM),
            pl.BlockSpec(memory_space=pltpu.VMEM),
            pl.BlockSpec(memory_space=pltpu.VMEM),
        ],
        out_specs=pl.BlockSpec(memory_space=pltpu.VMEM),
        compiler_params=pltpu.CompilerParams(vmem_limit_bytes=24 * 2**20),
        name="pack_rows",
    )(index, queries, grad_out)


def attention_kernel(
    recv_ref, start_ref, place_ref, qg_ref, *refs
):
    kv_refs, dq_ref, dkv_refs = refs[: 2 * NEAR], refs[2 * NEAR], refs[2 * NEAR + 1 : 4 * NEAR + 1]
    k_all, kt_all, v_all, dk_all, dv_all, scores, dprobs, dqt = refs[4 * NEAR + 1 :]
    blocks = k_all.shape[0]
    width = k_all.shape[1]
    tile_rows = width // PAIR
    part = width // NEAR
    own_part = part // 4
    factor = SCALING * LOG2E

    def rows_of(slot):
        begin = (slot % NEAR) * part
        if slot < NEAR:
            return slice(begin, begin + own_part)
        return slice(begin + own_part, begin + part)

    def stage(block, _):
        for slot, ref in enumerate(kv_refs):
            rows = rows_of(slot)
            count = rows.stop - rows.start
            key = ref[:, :, 0, block].astype(jnp.float32).reshape(count, HD)
            value = ref[:, :, 1, block].astype(jnp.float32).reshape(count, HD)
            k_all[block, rows] = key.astype(jnp.bfloat16)
            v_all[block, rows] = value.astype(jnp.bfloat16)
        kt_all[block] = k_all[block].astype(jnp.float32).T.astype(jnp.bfloat16)
        return 0

    lax.fori_loop(0, blocks, stage, 0)

    row = lax.broadcasted_iota(jnp.int32, (width, 1), 0)
    holder = (place_ref[0] & 12) | ((place_ref[0] - (row >> 6)) & 3)
    source = holder ^ (((row >> 4) & 1) * 4) ^ (((row >> 5) & 1) * 15)
    key_offset = (
        ((row >> 2) & 1) * tile_rows + ((row >> 3) & 1) * 64 + source * 4 + (row & 3)
    )
    lane = lax.broadcasted_iota(jnp.int32, (1, width), 1)

    def query_block(block, _):
        first = recv_ref[PAIR * block]
        second = recv_ref[PAIR * block + 1]
        query = jnp.concatenate([qg_ref[first, 0], qg_ref[second, 0]], axis=0)
        grad = jnp.concatenate([qg_ref[first, 1], qg_ref[second, 1]], axis=0)
        start_low = start_ref[PAIR * block]
        start_high = start_ref[PAIR * block + 1]
        lowest = start_low // PAIR
        row_start = jnp.where(lane < tile_rows, start_low, start_high) * tile_rows

        def products(other, masked_by_order, peak):
            score = matmul(k_all[other], query, ((1,), (1,)))
            key_pos = key_offset + other * width
            allowed = key_pos >= row_start
            if masked_by_order:
                allowed = allowed & (key_offset <= lane)
            score = jnp.where(allowed, score, -jnp.inf)
            scores[other] = score
            dprobs[other] = matmul(v_all[other], grad, ((1,), (1,)))
            return jnp.maximum(peak, jnp.max(score, axis=0, keepdims=True))

        peak = products(block, True, jnp.full((1, width), -jnp.inf, jnp.float32))
        peak = lax.fori_loop(lowest, block, lambda other, m: products(other, False, m), peak)
        shift = peak * factor

        def sums(other, totals):
            weights = jnp.exp2(scores[other] * factor - shift)
            scores[other] = weights
            return (
                totals[0] + jnp.sum(weights, axis=0, keepdims=True),
                totals[1] + jnp.sum(weights * dprobs[other], axis=0, keepdims=True),
            )

        zeros = jnp.zeros((1, width), jnp.float32)
        total, weighted = lax.fori_loop(lowest, block + 1, sums, (zeros, zeros))
        inverse = 1.0 / total
        delta = weighted * inverse

        def terms(other):
            probs = scores[other] * inverse
            dscores = (probs * (dprobs[other] - delta)).astype(jnp.bfloat16)
            grad_value = matmul(probs.astype(jnp.bfloat16), grad, ((1,), (0,)))
            grad_key = matmul(dscores, query, ((1,), (0,)))
            grad_query = matmul(kt_all[other], dscores, ((1,), (0,)))
            return grad_key, grad_value, grad_query

        grad_key, grad_value, grad_query = terms(block)
        dk_all[block] = grad_key
        dv_all[block] = grad_value
        dqt[...] = grad_query

        def earlier(other, _):
            grad_key, grad_value, grad_query = terms(other)
            dk_all[other] += grad_key
            dv_all[other] += grad_value
            dqt[...] += grad_query
            return 0

        lax.fori_loop(lowest, block, earlier, 0)
        result = (dqt[...] * SCALING).T.astype(jnp.bfloat16)
        dq_ref[first] = result[:tile_rows]
        dq_ref[second] = result[tile_rows:]
        return 0

    lax.fori_loop(0, blocks, query_block, 0)

    def unstage(block, _):
        for slot, ref in enumerate(dkv_refs):
            rows = rows_of(slot)
            shape = ref.shape[:2] + ref.shape[4:]
            ref[:, :, 0, block] = (dk_all[block, rows] * SCALING).reshape(shape).astype(jnp.bfloat16)
            ref[:, :, 1, block] = dv_all[block, rows].reshape(shape).astype(jnp.bfloat16)
        return 0

    lax.fori_loop(0, blocks, unstage, 0)


def attention(my_recv, start, place, qg, chunks):
    slots, _, tile_rows, _ = qg.shape
    blocks = my_recv.shape[0] // PAIR
    width = PAIR * tile_rows
    vmem = pl.BlockSpec(memory_space=pltpu.VMEM)
    smem = pl.BlockSpec(memory_space=pltpu.SMEM)
    return pl.pallas_call(
        attention_kernel,
        out_shape=(jax.ShapeDtypeStruct((slots, tile_rows, HD), jnp.bfloat16),)
        + tuple(jax.ShapeDtypeStruct(chunk.shape, jnp.bfloat16) for chunk in chunks),
        in_specs=[smem] * 3 + [vmem] * (1 + 2 * NEAR),
        out_specs=(vmem,) * (1 + 2 * NEAR),
        scratch_shapes=[
            pltpu.VMEM((blocks, width, HD), jnp.bfloat16),
            pltpu.VMEM((blocks, HD, width), jnp.bfloat16),
            pltpu.VMEM((blocks, width, HD), jnp.bfloat16),
            pltpu.VMEM((blocks, width, HD), jnp.float32),
            pltpu.VMEM((blocks, width, HD), jnp.float32),
            pltpu.VMEM((blocks, width, width), jnp.float32),
            pltpu.VMEM((blocks, width, width), jnp.float32),
            pltpu.VMEM((HD, width), jnp.float32),
        ],
        compiler_params=pltpu.CompilerParams(vmem_limit_bytes=24 * 2**20),
        cost_estimate=pl.CostEstimate(
            flops=2 * 10**9, bytes_accessed=6 * 2**20, transcendentals=2 * 10**6
        ),
        name="attention_backward",
    )(my_recv, start, place, qg, *chunks)


def kv_pack_kernel(index_ref, kv_ref, out_ref):
    def body(slot, _):
        tile = index_ref[slot & 1, slot >> 1]
        piece = kv_ref[tile].reshape((2, 2, 2) + kv_ref.shape[2:])
        for half in range(2):
            out_ref[slot >> 1, half, slot & 1] = piece[:, half]
        return 0

    lax.fori_loop(0, 2 * index_ref.shape[1], body, 0, unroll=4)


def kv_unpack_kernel(recv_ref, place_ref, kv_ref, own_ref, other_ref):
    head = place_ref[0] >> 3

    def body(pair, _):
        low = recv_ref[PAIR * pair]
        high = recv_ref[PAIR * pair + 1]
        for half in range(2):
            for kind in range(2):
                for ref, which in ((own_ref, head), (other_ref, 1 - head)):
                    rows = [
                        kv_ref[slot >> 1, half, slot & 1, kind, which].astype(jnp.float32)
                        for slot in (low, high)
                    ]
                    ref[half, kind, pair] = jnp.concatenate(rows, axis=0).astype(jnp.bfloat16)
        return 0

    lax.fori_loop(0, recv_ref.shape[0] // PAIR, body, 0)


def kv_back_kernel(recv_ref, place_ref, p0, p1, p2, p3, out_ref):
    head = place_ref[0] >> 3
    sliver = out_ref.shape[-2]

    def body(pair, _):
        slots = (recv_ref[PAIR * pair], recv_ref[PAIR * pair + 1])
        for half in range(2):
            for kind in range(2):
                for a, b, which in ((p0, p1, head), (p2, p3, 1 - head)):
                    total = a[half, kind, pair].astype(jnp.float32) + b[half, kind, pair].astype(jnp.float32)
                    for order, slot in enumerate(slots):
                        rows = total[order * sliver : (order + 1) * sliver]
                        out_ref[slot >> 1, half, slot & 1, kind, which] = rows.astype(jnp.bfloat16)
        return 0

    lax.fori_loop(0, recv_ref.shape[0] // PAIR, body, 0)


def kv_final_kernel(anchor_ref, kv_ref, out_ref):
    def body(tile, _):
        slot = anchor_ref[tile]
        piece = kv_ref[slot >> 1, :, slot & 1]
        for half in range(2):
            for kind in range(2):
                for head in range(2):
                    out_ref[tile, kind * 4 + half * 2 + head] = piece[half, kind, head]
        return 0

    lax.fori_loop(0, anchor_ref.shape[0], body, 0)


def local_call(kernel, name, scalars, arrays, out_shape):
    vmem = pl.BlockSpec(memory_space=pltpu.VMEM)
    smem = pl.BlockSpec(memory_space=pltpu.SMEM)
    return pl.pallas_call(
        kernel,
        out_shape=out_shape,
        in_specs=[smem] * len(scalars) + [vmem] * len(arrays),
        out_specs=jax.tree.map(lambda _: vmem, out_shape),
        compiler_params=pltpu.CompilerParams(vmem_limit_bytes=16 * 2**20),
        name=name,
    )(*scalars, *arrays)


def far_swap(values, flip):
    return lax.ppermute(values, "z", [(place, place ^ flip) for place in range(16)])


def near_shift(values, step):
    pairs = [(place, (place & 12) | ((place + step) & 3)) for place in range(16)]
    return lax.ppermute(values, "z", pairs)


def near_gather(values):
    return [values] + [near_shift(values, step) for step in range(1, NEAR)]


def near_terms(terms):
    return [terms[0]] + [near_shift(terms[step], -step) for step in range(1, NEAR)]


def total(terms, index):
    return sum(term[index].astype(jnp.float32) for term in terms).astype(jnp.bfloat16)


def on_device(queries, keys_values, grad_out, send_tiles, recv_slot, tile_seq):
    n_replicas = lax.axis_size("dp")
    replica = lax.axis_index("dp")
    tile_count, tile_rows, row_width = queries.shape
    sliver = keys_values.shape[1]
    slot_cap = send_tiles.shape[2]
    slots = n_replicas * slot_cap
    pairs = tile_count // PAIR
    my_send = send_tiles[0]
    outgoing = my_send.T
    my_recv = lax.dynamic_index_in_dim(recv_slot, replica, 0, keepdims=False)
    place = lax.axis_index("z").astype(jnp.int32).reshape(1)
    traveling = jax.ShapeDtypeStruct(
        (n_replicas, 2, slot_cap, 2, 2, sliver, HD), keys_values.dtype
    )
    half_shape = jax.ShapeDtypeStruct((2, 2, pairs, PAIR * sliver, HD), keys_values.dtype)

    def over_plane(values):
        return lax.all_to_all(
            values.reshape((2 * n_replicas,) + values.shape[2:]),
            PLANE, split_axis=0, concat_axis=0, tiled=True,
        ).reshape(values.shape)

    kv_blocks = keys_values.reshape(tile_count, sliver, 2 * KV, HD).transpose(0, 2, 1, 3)
    kv_arrived = over_plane(
        local_call(kv_pack_kernel, "kv_pack", [outgoing], [kv_blocks], traveling)
    )
    own, other = local_call(
        kv_unpack_kernel, "kv_unpack", [my_recv, place], [kv_arrived], (half_shape, half_shape)
    )
    qg_packed = pack(outgoing, queries, grad_out)
    qg_arrived = lax.all_to_all(
        qg_packed.reshape(n_replicas, slot_cap, 2, tile_rows, row_width),
        "dp", split_axis=0, concat_axis=0, tiled=True,
    ).reshape(slots, 2, tile_rows, row_width)
    far = jnp.stack([far_swap(own, FAR[0]), far_swap(other, FAR[1]), far_swap(other, FAR[2])])
    own_chunks = near_gather(own[None])
    far, own_chunks, qg_arrived = lax.optimization_barrier((far, own_chunks, qg_arrived))
    chunks = own_chunks + near_gather(far)

    seq = tile_seq[0]
    start = jnp.sum((seq[None, :] < seq[:, None]).astype(jnp.int32), axis=1)
    query_back, *terms = attention(my_recv, start, place, qg_arrived, chunks)
    query_returned = lax.all_to_all(
        query_back.reshape(n_replicas, slot_cap, tile_rows, row_width),
        "dp", split_axis=0, concat_axis=0, tiled=True,
    )
    far_terms = near_terms(terms[NEAR:])
    own_terms, far_terms = lax.optimization_barrier((terms[:NEAR], far_terms))
    back = [far_swap(total(far_terms, index), flip) for index, flip in enumerate(FAR)]
    own_sum = total(near_terms(own_terms), 0)
    swapped, query_returned = lax.optimization_barrier(([own_sum] + back, query_returned))
    kv_returned = over_plane(
        local_call(kv_back_kernel, "kv_back", [my_recv, place], swapped, traveling)
    )

    flat_slots = jnp.arange(slots)
    own_slots = replica * slot_cap + jnp.arange(slot_cap)
    slot_used = jnp.any(recv_slot[:, None, :] == own_slots[None, :, None], axis=2)
    matched = slot_used[:, :, None] & (my_send[:, :, None] == jnp.arange(tile_count)[None, None, :])
    anchor = jnp.sum(
        jnp.where(matched, flat_slots.reshape(n_replicas, slot_cap)[:, :, None], 0), axis=(0, 1)
    )
    grad_queries = query_returned.reshape(slots, tile_rows, row_width)[anchor]
    kv_final = local_call(
        kv_final_kernel, "kv_final", [anchor], [kv_returned],
        jax.ShapeDtypeStruct(kv_blocks.shape, keys_values.dtype),
    )
    grad_keys_values = kv_final.transpose(0, 2, 1, 3).reshape(keys_values.shape)
    return (grad_queries, grad_keys_values)


def solution(mesh):
    fine = Mesh(mesh.devices.reshape(mesh.devices.shape[0], 2, 16), ("dp", "xh", "z"))
    tensor = ("xh", "z")
    in_specs = (
        P("dp", None, tensor),
        P("dp", tensor, None),
        P("dp", None, tensor),
        P("dp", None, None),
        P(),
        P("dp", None),
    )
    out_specs = (P("dp", None, tensor), P("dp", tensor, None))
    return jax.shard_map(
        on_device, mesh=fine, in_specs=in_specs, out_specs=out_specs, check_vma=False
    )
```

```python
import functools

import jax
import jax.numpy as jnp
from jax import lax
from jax.experimental import pallas as pl
from jax.experimental.pallas import tpu as pltpu
from jax.sharding import Mesh
from jax.sharding import PartitionSpec as P

HD = 128
KV = 4
PAIR = 2
SCALING = HD ** (-0.5)
LOG2E = 1.4426950408889634
PLANE = ("dp", "xh")
MIRROR = 15
ACROSS = 4
NEAR = 4


def matmul(a, b, contract):
    return lax.dot_general(a, b, (contract, ((), ())), preferred_element_type=jnp.float32)


def pack_kernel(index_ref, q_ref, g_ref, out_ref):
    def body(slot, _):
        tile = index_ref[slot & 1, slot >> 1]
        out_ref[slot, 0] = q_ref[tile]
        out_ref[slot, 1] = g_ref[tile]
        return 0

    lax.fori_loop(0, out_ref.shape[0], body, 0)


def pack(index, queries, grad_out):
    slots = index.size
    return pl.pallas_call(
        pack_kernel,
        out_shape=jax.ShapeDtypeStruct((slots, 2) + queries.shape[1:], queries.dtype),
        in_specs=[
            pl.BlockSpec(memory_space=pltpu.SMEM),
            pl.BlockSpec(memory_space=pltpu.VMEM),
            pl.BlockSpec(memory_space=pltpu.VMEM),
        ],
        out_specs=pl.BlockSpec(memory_space=pltpu.VMEM),
        compiler_params=pltpu.CompilerParams(vmem_limit_bytes=24 * 2**20),
        name="pack_rows",
    )(index, queries, grad_out)


def attention_kernel(
    recv_ref, start_ref, place_ref, qg_ref, *refs
):
    kv_refs, dq_ref, dkv_refs = refs[: 2 * NEAR], refs[2 * NEAR], refs[2 * NEAR + 1 : 4 * NEAR + 1]
    k_all, kt_all, v_all, dk_all, dv_all, scores, dprobs, dqt = refs[4 * NEAR + 1 :]
    blocks = k_all.shape[0]
    width = k_all.shape[1]
    tile_rows = width // PAIR
    part = width // NEAR
    factor = SCALING * LOG2E

    def rows_of(slot, first_part):
        begin = (slot % NEAR) * part
        if slot < NEAR:
            return slice(begin, begin + first_part)
        return slice(begin + first_part, begin + part)

    def stage(block, _):
        for slot, ref in enumerate(kv_refs):
            rows = rows_of(slot, part // 4)
            count = rows.stop - rows.start
            key = ref[:, :, 0, block].astype(jnp.float32).reshape(count, HD)
            value = ref[:, :, 1, block].astype(jnp.float32).reshape(count, HD)
            k_all[block, rows] = key.astype(jnp.bfloat16)
            v_all[block, rows] = value.astype(jnp.bfloat16)
        kt_all[block] = k_all[block].astype(jnp.float32).T.astype(jnp.bfloat16)
        return 0

    lax.fori_loop(0, blocks, stage, 0)

    row = lax.broadcasted_iota(jnp.int32, (width, 1), 0)
    holder = (place_ref[0] & 12) | ((place_ref[0] - (row >> 6)) & 3)
    source = holder ^ (((row >> 4) & 1) * MIRROR) ^ (((row >> 5) & 1) * ACROSS)
    key_offset = (
        ((row >> 2) & 1) * tile_rows + ((row >> 3) & 1) * 64 + source * 4 + (row & 3)
    )
    lane = lax.broadcasted_iota(jnp.int32, (1, width), 1)

    def query_block(block, _):
        first = recv_ref[PAIR * block]
        second = recv_ref[PAIR * block + 1]
        query = jnp.concatenate([qg_ref[first, 0], qg_ref[second, 0]], axis=0)
        grad = jnp.concatenate([qg_ref[first, 1], qg_ref[second, 1]], axis=0)
        start_low = start_ref[PAIR * block]
        start_high = start_ref[PAIR * block + 1]
        lowest = start_low // PAIR
        row_start = jnp.where(lane < tile_rows, start_low, start_high) * tile_rows

        def products(other, masked_by_order, peak):
            score = matmul(k_all[other], query, ((1,), (1,)))
            key_pos = key_offset + other * width
            allowed = key_pos >= row_start
            if masked_by_order:
                allowed = allowed & (key_offset <= lane)
            score = jnp.where(allowed, score, -jnp.inf)
            scores[other] = score
            dprobs[other] = matmul(v_all[other], grad, ((1,), (1,)))
            return jnp.maximum(peak, jnp.max(score, axis=0, keepdims=True))

        peak = products(block, True, jnp.full((1, width), -jnp.inf, jnp.float32))
        peak = lax.fori_loop(lowest, block, lambda other, m: products(other, False, m), peak)
        shift = peak * factor

        def sums(other, totals):
            weights = jnp.exp2(scores[other] * factor - shift)
            scores[other] = weights
            return (
                totals[0] + jnp.sum(weights, axis=0, keepdims=True),
                totals[1] + jnp.sum(weights * dprobs[other], axis=0, keepdims=True),
            )

        zeros = jnp.zeros((1, width), jnp.float32)
        total, weighted = lax.fori_loop(lowest, block + 1, sums, (zeros, zeros))
        inverse = 1.0 / total
        delta = weighted * inverse

        def terms(other):
            probs = scores[other] * inverse
            dscores = (probs * (dprobs[other] - delta)).astype(jnp.bfloat16)
            grad_value = matmul(probs.astype(jnp.bfloat16), grad, ((1,), (0,)))
            grad_key = matmul(dscores, query, ((1,), (0,)))
            grad_query = matmul(kt_all[other], dscores, ((1,), (0,)))
            return grad_key, grad_value, grad_query

        grad_key, grad_value, grad_query = terms(block)
        dk_all[block] = grad_key
        dv_all[block] = grad_value
        dqt[...] = grad_query

        def earlier(other, _):
            grad_key, grad_value, grad_query = terms(other)
            dk_all[other] += grad_key
            dv_all[other] += grad_value
            dqt[...] += grad_query
            return 0

        lax.fori_loop(lowest, block, earlier, 0)
        result = (dqt[...] * SCALING).T.astype(jnp.bfloat16)
        dq_ref[first] = result[:tile_rows]
        dq_ref[second] = result[tile_rows:]
        return 0

    lax.fori_loop(0, blocks, query_block, 0)

    def unstage(block, _):
        for slot, ref in enumerate(dkv_refs):
            rows = rows_of(slot, part // 2)
            shape = ref.shape[:2] + ref.shape[4:]
            ref[:, :, 0, block] = (dk_all[block, rows] * SCALING).reshape(shape).astype(jnp.bfloat16)
            ref[:, :, 1, block] = dv_all[block, rows].reshape(shape).astype(jnp.bfloat16)
        return 0

    lax.fori_loop(0, blocks, unstage, 0)


def attention(my_recv, start, place, qg, chunks):
    slots, _, tile_rows, _ = qg.shape
    blocks = my_recv.shape[0] // PAIR
    width = PAIR * tile_rows
    vmem = pl.BlockSpec(memory_space=pltpu.VMEM)
    smem = pl.BlockSpec(memory_space=pltpu.SMEM)
    return pl.pallas_call(
        attention_kernel,
        out_shape=(jax.ShapeDtypeStruct((slots, tile_rows, HD), jnp.bfloat16),)
        + (jax.ShapeDtypeStruct((2,) + chunks[0].shape[1:], jnp.bfloat16),) * (2 * NEAR),
        in_specs=[smem] * 3 + [vmem] * (1 + 2 * NEAR),
        out_specs=(vmem,) * (1 + 2 * NEAR),
        scratch_shapes=[
            pltpu.VMEM((blocks, width, HD), jnp.bfloat16),
            pltpu.VMEM((blocks, HD, width), jnp.bfloat16),
            pltpu.VMEM((blocks, width, HD), jnp.bfloat16),
            pltpu.VMEM((blocks, width, HD), jnp.float32),
            pltpu.VMEM((blocks, width, HD), jnp.float32),
            pltpu.VMEM((blocks, width, width), jnp.float32),
            pltpu.VMEM((blocks, width, width), jnp.float32),
            pltpu.VMEM((HD, width), jnp.float32),
        ],
        compiler_params=pltpu.CompilerParams(vmem_limit_bytes=24 * 2**20),
        cost_estimate=pl.CostEstimate(
            flops=2 * 10**9, bytes_accessed=6 * 2**20, transcendentals=2 * 10**6
        ),
        name="attention_backward",
    )(my_recv, start, place, qg, *chunks)


def kv_pack_kernel(index_ref, kv_ref, out_ref):
    def body(slot, _):
        tile = index_ref[slot & 1, slot >> 1]
        piece = kv_ref[tile].reshape((2, 2, 2) + kv_ref.shape[2:])
        for half in range(2):
            out_ref[slot >> 1, half, slot & 1] = piece[:, half]
        return 0

    lax.fori_loop(0, 2 * index_ref.shape[1], body, 0, unroll=4)


def kv_unpack_kernel(recv_ref, place_ref, kv_ref, own_ref, other_ref):
    head = place_ref[0] >> 3

    def body(pair, _):
        low = recv_ref[PAIR * pair]
        high = recv_ref[PAIR * pair + 1]
        for half in range(2):
            for kind in range(2):
                for ref, which in ((own_ref, head), (other_ref, 1 - head)):
                    rows = [
                        kv_ref[slot >> 1, half, slot & 1, kind, which].astype(jnp.float32)
                        for slot in (low, high)
                    ]
                    ref[half, kind, pair] = jnp.concatenate(rows, axis=0).astype(jnp.bfloat16)
        return 0

    lax.fori_loop(0, recv_ref.shape[0] // PAIR, body, 0)


def kv_back_kernel(recv_ref, place_ref, own_ref, other_ref, out_ref):
    head = place_ref[0] >> 3
    sliver = out_ref.shape[-2]

    def body(pair, _):
        slots = (recv_ref[PAIR * pair], recv_ref[PAIR * pair + 1])
        for half in range(2):
            for kind in range(2):
                for ref, which in ((own_ref, head), (other_ref, 1 - head)):
                    total = ref[half, kind, pair].astype(jnp.float32)
                    for order, slot in enumerate(slots):
                        rows = total[order * sliver : (order + 1) * sliver]
                        out_ref[slot >> 1, half, slot & 1, kind, which] = rows.astype(jnp.bfloat16)
        return 0

    lax.fori_loop(0, recv_ref.shape[0] // PAIR, body, 0)


def kv_final_kernel(anchor_ref, kv_ref, out_ref):
    def body(tile, _):
        slot = anchor_ref[tile]
        piece = kv_ref[slot >> 1, :, slot & 1]
        for half in range(2):
            for kind in range(2):
                for head in range(2):
                    out_ref[tile, kind * 4 + half * 2 + head] = piece[half, kind, head]
        return 0

    lax.fori_loop(0, anchor_ref.shape[0], body, 0)


def local_call(kernel, name, scalars, arrays, out_shape):
    vmem = pl.BlockSpec(memory_space=pltpu.VMEM)
    smem = pl.BlockSpec(memory_space=pltpu.SMEM)
    return pl.pallas_call(
        kernel,
        out_shape=out_shape,
        in_specs=[smem] * len(scalars) + [vmem] * len(arrays),
        out_specs=jax.tree.map(lambda _: vmem, out_shape),
        compiler_params=pltpu.CompilerParams(vmem_limit_bytes=16 * 2**20),
        name=name,
    )(*scalars, *arrays)


def far_swap(values, flip):
    return lax.ppermute(values, "z", [(place, place ^ flip) for place in range(16)])


def near_shift(values, step):
    pairs = [(place, (place & 12) | ((place + step) & 3)) for place in range(16)]
    return lax.ppermute(values, "z", pairs)


def near_gather(values):
    return [values] + [near_shift(values, step) for step in range(1, NEAR)]


def near_terms(terms):
    return [terms[0]] + [near_shift(terms[step], -step) for step in range(1, NEAR)]


def total(terms):
    return sum(term.astype(jnp.float32) for term in terms)


def on_device(queries, keys_values, grad_out, send_tiles, recv_slot, tile_seq):
    n_replicas = lax.axis_size("dp")
    replica = lax.axis_index("dp")
    tile_count, tile_rows, row_width = queries.shape
    sliver = keys_values.shape[1]
    slot_cap = send_tiles.shape[2]
    slots = n_replicas * slot_cap
    pairs = tile_count // PAIR
    my_send = send_tiles[0]
    outgoing = my_send.T
    my_recv = lax.dynamic_index_in_dim(recv_slot, replica, 0, keepdims=False)
    place = lax.axis_index("z").astype(jnp.int32).reshape(1)
    traveling = jax.ShapeDtypeStruct(
        (n_replicas, 2, slot_cap, 2, 2, sliver, HD), keys_values.dtype
    )
    half_shape = jax.ShapeDtypeStruct((2, 2, pairs, PAIR * sliver, HD), keys_values.dtype)

    def over_plane(values):
        return lax.all_to_all(
            values.reshape((2 * n_replicas,) + values.shape[2:]),
            PLANE, split_axis=0, concat_axis=0, tiled=True,
        ).reshape(values.shape)

    kv_blocks = keys_values.reshape(tile_count, sliver, 2 * KV, HD).transpose(0, 2, 1, 3)
    kv_arrived = over_plane(
        local_call(kv_pack_kernel, "kv_pack", [outgoing], [kv_blocks], traveling)
    )
    own, other = local_call(
        kv_unpack_kernel, "kv_unpack", [my_recv, place], [kv_arrived], (half_shape, half_shape)
    )
    qg_packed = pack(outgoing, queries, grad_out)
    qg_arrived = lax.all_to_all(
        qg_packed.reshape(n_replicas, slot_cap, 2, tile_rows, row_width),
        "dp", split_axis=0, concat_axis=0, tiled=True,
    ).reshape(slots, 2, tile_rows, row_width)
    far = jnp.stack(
        [far_swap(other, MIRROR), far_swap(own, ACROSS), far_swap(other, MIRROR ^ ACROSS)]
    )
    own_chunks = near_gather(own[None])
    far, own_chunks, qg_arrived = lax.optimization_barrier((far, own_chunks, qg_arrived))
    chunks = own_chunks + near_gather(far)

    seq = tile_seq[0]
    start = jnp.sum((seq[None, :] < seq[:, None]).astype(jnp.int32), axis=1)
    query_back, *terms = attention(my_recv, start, place, qg_arrived, chunks)
    query_returned = lax.all_to_all(
        query_back.reshape(n_replicas, slot_cap, tile_rows, row_width),
        "dp", split_axis=0, concat_axis=0, tiled=True,
    )
    across_terms = near_terms(terms[NEAR:])
    own_terms, across_terms = lax.optimization_barrier((terms[:NEAR], across_terms))
    arrived = far_swap(total(across_terms).astype(jnp.bfloat16), ACROSS)
    base = lax.optimization_barrier(total([arrived, own_terms[0]]))
    summed = total([base] + near_terms(own_terms)[1:]).astype(jnp.bfloat16)
    swapped = [summed[0], far_swap(summed[1], MIRROR)]
    swapped, query_returned = lax.optimization_barrier((swapped, query_returned))
    kv_returned = over_plane(
        local_call(kv_back_kernel, "kv_back", [my_recv, place], swapped, traveling)
    )

    flat_slots = jnp.arange(slots)
    own_slots = replica * slot_cap + jnp.arange(slot_cap)
    slot_used = jnp.any(recv_slot[:, None, :] == own_slots[None, :, None], axis=2)
    matched = slot_used[:, :, None] & (my_send[:, :, None] == jnp.arange(tile_count)[None, None, :])
    anchor = jnp.sum(
        jnp.where(matched, flat_slots.reshape(n_replicas, slot_cap)[:, :, None], 0), axis=(0, 1)
    )
    grad_queries = query_returned.reshape(slots, tile_rows, row_width)[anchor]
    kv_final = local_call(
        kv_final_kernel, "kv_final", [anchor], [kv_returned],
        jax.ShapeDtypeStruct(kv_blocks.shape, keys_values.dtype),
    )
    grad_keys_values = kv_final.transpose(0, 2, 1, 3).reshape(keys_values.shape)
    return (grad_queries, grad_keys_values)


def solution(mesh):
    fine = Mesh(mesh.devices.reshape(mesh.devices.shape[0], 2, 16), ("dp", "xh", "z"))
    tensor = ("xh", "z")
    in_specs = (
        P("dp", None, tensor),
        P("dp", tensor, None),
        P("dp", None, tensor),
        P("dp", None, None),
        P(),
        P("dp", None),
    )
    out_specs = (P("dp", None, tensor), P("dp", tensor, None))
    return jax.shard_map(
        on_device, mesh=fine, in_specs=in_specs, out_specs=out_specs, check_vma=False
    )
```

```python
import functools

import jax
import jax.numpy as jnp
from jax import lax
from jax.experimental import pallas as pl
from jax.experimental.pallas import tpu as pltpu
from jax.sharding import Mesh
from jax.sharding import PartitionSpec as P

HD = 128
KV = 4
PAIR = 2
SCALING = HD ** (-0.5)
LOG2E = 1.4426950408889634
EVERYONE = ("dp", "xh", "z")
ACROSS = 4
NEAR = 4


def matmul(a, b, contract):
    return lax.dot_general(a, b, (contract, ((), ())), preferred_element_type=jnp.float32)


def pack_kernel(index_ref, q_ref, g_ref, out_ref):
    def body(slot, _):
        tile = index_ref[slot & 1, slot >> 1]
        out_ref[slot, 0] = q_ref[tile]
        out_ref[slot, 1] = g_ref[tile]
        return 0

    lax.fori_loop(0, out_ref.shape[0], body, 0)


def pack(index, queries, grad_out):
    slots = index.size
    return pl.pallas_call(
        pack_kernel,
        out_shape=jax.ShapeDtypeStruct((slots, 2) + queries.shape[1:], queries.dtype),
        in_specs=[
            pl.BlockSpec(memory_space=pltpu.SMEM),
            pl.BlockSpec(memory_space=pltpu.VMEM),
            pl.BlockSpec(memory_space=pltpu.VMEM),
        ],
        out_specs=pl.BlockSpec(memory_space=pltpu.VMEM),
        compiler_params=pltpu.CompilerParams(vmem_limit_bytes=24 * 2**20),
        name="pack_rows",
    )(index, queries, grad_out)


def attention_kernel(
    recv_ref, start_ref, place_ref, qg_ref, *refs
):
    kv_refs, dq_ref, dkv_refs = refs[: 2 * NEAR], refs[2 * NEAR], refs[2 * NEAR + 1 : 4 * NEAR + 1]
    k_all, kt_all, v_all, dk_all, dv_all, scores, dprobs, dqt = refs[4 * NEAR + 1 :]
    blocks = k_all.shape[0]
    width = k_all.shape[1]
    tile_rows = width // PAIR
    part = width // NEAR
    factor = SCALING * LOG2E

    def rows_of(slot):
        begin = (slot % NEAR) * part + (slot // NEAR) * (part // 2)
        return slice(begin, begin + part // 2)

    def stage(block, _):
        for slot, ref in enumerate(kv_refs):
            rows = rows_of(slot)
            count = rows.stop - rows.start
            key = ref[:, :, 0, block].astype(jnp.float32).reshape(count, HD)
            value = ref[:, :, 1, block].astype(jnp.float32).reshape(count, HD)
            k_all[block, rows] = key.astype(jnp.bfloat16)
            v_all[block, rows] = value.astype(jnp.bfloat16)
        kt_all[block] = k_all[block].astype(jnp.float32).T.astype(jnp.bfloat16)
        return 0

    lax.fori_loop(0, blocks, stage, 0)

    row = lax.broadcasted_iota(jnp.int32, (width, 1), 0)
    holder = (place_ref[0] & 12) | ((place_ref[0] - (row >> 6)) & 3)
    holder = holder ^ (((row >> 5) & 1) * ACROSS)
    lower = jnp.where(holder < 8, holder, 15 - holder)
    source = jnp.where(((row >> 4) & 1) == 0, lower, 15 - lower)
    key_offset = (
        ((row >> 2) & 1) * tile_rows + ((row >> 3) & 1) * 64 + source * 4 + (row & 3)
    )
    lane = lax.broadcasted_iota(jnp.int32, (1, width), 1)

    def query_block(block, _):
        first = recv_ref[PAIR * block]
        second = recv_ref[PAIR * block + 1]
        query = jnp.concatenate([qg_ref[first, 0], qg_ref[second, 0]], axis=0)
        grad = jnp.concatenate([qg_ref[first, 1], qg_ref[second, 1]], axis=0)
        start_low = start_ref[PAIR * block]
        start_high = start_ref[PAIR * block + 1]
        lowest = start_low // PAIR
        row_start = jnp.where(lane < tile_rows, start_low, start_high) * tile_rows

        def products(other, masked_by_order, peak):
            score = matmul(k_all[other], query, ((1,), (1,)))
            key_pos = key_offset + other * width
            allowed = key_pos >= row_start
            if masked_by_order:
                allowed = allowed & (key_offset <= lane)
            score = jnp.where(allowed, score, -jnp.inf)
            scores[other] = score
            dprobs[other] = matmul(v_all[other], grad, ((1,), (1,)))
            return jnp.maximum(peak, jnp.max(score, axis=0, keepdims=True))

        peak = products(block, True, jnp.full((1, width), -jnp.inf, jnp.float32))
        peak = lax.fori_loop(lowest, block, lambda other, m: products(other, False, m), peak)
        shift = peak * factor

        def sums(other, totals):
            weights = jnp.exp2(scores[other] * factor - shift)
            scores[other] = weights
            return (
                totals[0] + jnp.sum(weights, axis=0, keepdims=True),
                totals[1] + jnp.sum(weights * dprobs[other], axis=0, keepdims=True),
            )

        zeros = jnp.zeros((1, width), jnp.float32)
        total, weighted = lax.fori_loop(lowest, block + 1, sums, (zeros, zeros))
        inverse = 1.0 / total
        delta = weighted * inverse

        def terms(other):
            probs = scores[other] * inverse
            dscores = (probs * (dprobs[other] - delta)).astype(jnp.bfloat16)
            grad_value = matmul(probs.astype(jnp.bfloat16), grad, ((1,), (0,)))
            grad_key = matmul(dscores, query, ((1,), (0,)))
            grad_query = matmul(kt_all[other], dscores, ((1,), (0,)))
            return grad_key, grad_value, grad_query

        grad_key, grad_value, grad_query = terms(block)
        dk_all[block] = grad_key
        dv_all[block] = grad_value
        dqt[...] = grad_query

        def earlier(other, _):
            grad_key, grad_value, grad_query = terms(other)
            dk_all[other] += grad_key
            dv_all[other] += grad_value
            dqt[...] += grad_query
            return 0

        lax.fori_loop(lowest, block, earlier, 0)
        result = (dqt[...] * SCALING).T.astype(jnp.bfloat16)
        dq_ref[first] = result[:tile_rows]
        dq_ref[second] = result[tile_rows:]
        return 0

    lax.fori_loop(0, blocks, query_block, 0)

    def unstage(block, _):
        for slot, ref in enumerate(dkv_refs):
            rows = rows_of(slot)
            shape = ref.shape[:2] + ref.shape[4:]
            ref[:, :, 0, block] = (dk_all[block, rows] * SCALING).reshape(shape).astype(jnp.bfloat16)
            ref[:, :, 1, block] = dv_all[block, rows].reshape(shape).astype(jnp.bfloat16)
        return 0

    lax.fori_loop(0, blocks, unstage, 0)


def attention(my_recv, start, place, qg, chunks):
    slots, _, tile_rows, _ = qg.shape
    blocks = my_recv.shape[0] // PAIR
    width = PAIR * tile_rows
    vmem = pl.BlockSpec(memory_space=pltpu.VMEM)
    smem = pl.BlockSpec(memory_space=pltpu.SMEM)
    return pl.pallas_call(
        attention_kernel,
        out_shape=(jax.ShapeDtypeStruct((slots, tile_rows, HD), jnp.bfloat16),)
        + (jax.ShapeDtypeStruct(chunks[0].shape, jnp.bfloat16),) * (2 * NEAR),
        in_specs=[smem] * 3 + [vmem] * (1 + 2 * NEAR),
        out_specs=(vmem,) * (1 + 2 * NEAR),
        scratch_shapes=[
            pltpu.VMEM((blocks, width, HD), jnp.bfloat16),
            pltpu.VMEM((blocks, HD, width), jnp.bfloat16),
            pltpu.VMEM((blocks, width, HD), jnp.bfloat16),
            pltpu.VMEM((blocks, width, HD), jnp.float32),
            pltpu.VMEM((blocks, width, HD), jnp.float32),
            pltpu.VMEM((blocks, width, width), jnp.float32),
            pltpu.VMEM((blocks, width, width), jnp.float32),
            pltpu.VMEM((HD, width), jnp.float32),
        ],
        compiler_params=pltpu.CompilerParams(vmem_limit_bytes=24 * 2**20),
        cost_estimate=pl.CostEstimate(
            flops=2 * 10**9, bytes_accessed=6 * 2**20, transcendentals=2 * 10**6
        ),
        name="attention_backward",
    )(my_recv, start, place, qg, *chunks)


def kv_pack_kernel(index_ref, kv_ref, out_ref):
    def body(slot, _):
        tile = index_ref[slot & 1, slot >> 1]
        piece = kv_ref[tile].reshape((2, 2, 2) + kv_ref.shape[2:])
        for across in range(2):
            for half in range(2):
                out_ref[slot >> 1, across, half, slot & 1] = piece[:, across, half]
        return 0

    lax.fori_loop(0, 2 * index_ref.shape[1], body, 0, unroll=4)


def kv_unpack_kernel(recv_ref, kv_ref, out_ref):
    def body(pair, _):
        slots = (recv_ref[PAIR * pair], recv_ref[PAIR * pair + 1])
        for across in range(2):
            for half in range(2):
                rows = [
                    kv_ref[slot >> 1, across, half, slot & 1].astype(jnp.float32)
                    for slot in slots
                ]
                out_ref[half, across, :, pair] = jnp.concatenate(rows, axis=1).astype(jnp.bfloat16)
        return 0

    lax.fori_loop(0, recv_ref.shape[0] // PAIR, body, 0)


def kv_back_kernel(recv_ref, sum_ref, out_ref):
    sliver = out_ref.shape[-2]

    def body(pair, _):
        slots = (recv_ref[PAIR * pair], recv_ref[PAIR * pair + 1])
        for across in range(2):
            for half in range(2):
                both = sum_ref[half, across, :, pair].astype(jnp.float32)
                for order, slot in enumerate(slots):
                    rows = both[:, order * sliver : (order + 1) * sliver]
                    out_ref[slot >> 1, across, half, slot & 1] = rows.astype(jnp.bfloat16)
        return 0

    lax.fori_loop(0, recv_ref.shape[0] // PAIR, body, 0)


def kv_final_kernel(anchor_ref, kv_ref, out_ref):
    def body(tile, _):
        slot = anchor_ref[tile]
        for across in range(2):
            for half in range(2):
                piece = kv_ref[slot >> 1, across, half, slot & 1]
                for kind in range(2):
                    out_ref[tile, kind * 4 + across * 2 + half] = piece[kind]
        return 0

    lax.fori_loop(0, anchor_ref.shape[0], body, 0, unroll=4)


def local_call(kernel, name, scalars, arrays, out_shape):
    vmem = pl.BlockSpec(memory_space=pltpu.VMEM)
    smem = pl.BlockSpec(memory_space=pltpu.SMEM)
    return pl.pallas_call(
        kernel,
        out_shape=out_shape,
        in_specs=[smem] * len(scalars) + [vmem] * len(arrays),
        out_specs=jax.tree.map(lambda _: vmem, out_shape),
        compiler_params=pltpu.CompilerParams(vmem_limit_bytes=16 * 2**20),
        name=name,
    )(*scalars, *arrays)


def far_swap(values, flip):
    return lax.ppermute(values, "z", [(place, place ^ flip) for place in range(16)])


def near_shift(values, step):
    pairs = [(place, (place & 12) | ((place + step) & 3)) for place in range(16)]
    return lax.ppermute(values, "z", pairs)


def near_gather(values):
    return [values] + [near_shift(values, step) for step in range(1, NEAR)]


def near_terms(terms):
    return [terms[0]] + [near_shift(terms[step], -step) for step in range(1, NEAR)]


def total(terms):
    return sum(term.astype(jnp.float32) for term in terms)


def on_device(queries, keys_values, grad_out, send_tiles, recv_slot, tile_seq):
    n_replicas = lax.axis_size("dp")
    replica = lax.axis_index("dp")
    tile_count, tile_rows, row_width = queries.shape
    sliver = keys_values.shape[1]
    slot_cap = send_tiles.shape[2]
    slots = n_replicas * slot_cap
    pairs = tile_count // PAIR
    my_send = send_tiles[0]
    outgoing = my_send.T
    my_recv = lax.dynamic_index_in_dim(recv_slot, replica, 0, keepdims=False)
    place = lax.axis_index("z").astype(jnp.int32).reshape(1)
    traveling = jax.ShapeDtypeStruct(
        (n_replicas, 2, 2, slot_cap, 2, sliver, HD), keys_values.dtype
    )
    half_shape = jax.ShapeDtypeStruct((2, 2, 2, pairs, PAIR * sliver, HD), keys_values.dtype)
    half_groups = [
        [32 * rank + 16 * across + z for rank in range(n_replicas) for across in range(2) for z in pair]
        for pair in ((low, 15 - low) for low in range(8))
    ]

    def by_halves(values):
        return lax.all_to_all(
            values.reshape((4 * n_replicas,) + values.shape[3:]), EVERYONE,
            split_axis=0, concat_axis=0, axis_index_groups=half_groups, tiled=True,
        ).reshape(values.shape)

    kv_blocks = keys_values.reshape(tile_count, sliver, 2 * KV, HD).transpose(0, 2, 1, 3)
    kv_arrived = by_halves(
        local_call(kv_pack_kernel, "kv_pack", [outgoing], [kv_blocks], traveling)
    )
    mine = local_call(kv_unpack_kernel, "kv_unpack", [my_recv], [kv_arrived], half_shape)
    qg_packed = pack(outgoing, queries, grad_out)
    qg_arrived = lax.all_to_all(
        qg_packed.reshape(n_replicas, slot_cap, 2, tile_rows, row_width),
        "dp", split_axis=0, concat_axis=0, tiled=True,
    ).reshape(slots, 2, tile_rows, row_width)
    far = far_swap(mine, ACROSS)
    chunks = near_gather(mine)
    far, chunks, qg_arrived = lax.optimization_barrier((far, chunks, qg_arrived))
    chunks = chunks + near_gather(far)

    seq = tile_seq[0]
    start = jnp.sum((seq[None, :] < seq[:, None]).astype(jnp.int32), axis=1)
    query_back, *terms = attention(my_recv, start, place, qg_arrived, chunks)
    query_returned = lax.all_to_all(
        query_back.reshape(n_replicas, slot_cap, tile_rows, row_width),
        "dp", split_axis=0, concat_axis=0, tiled=True,
    )
    across_terms = near_terms(terms[NEAR:])
    own_terms, across_terms = lax.optimization_barrier((terms[:NEAR], across_terms))
    arrived = far_swap(total(across_terms).astype(jnp.bfloat16), ACROSS)
    base = lax.optimization_barrier(total([arrived, own_terms[0]]))
    summed = total([base] + near_terms(own_terms)[1:]).astype(jnp.bfloat16)
    summed, query_returned = lax.optimization_barrier((summed, query_returned))
    kv_returned = by_halves(
        local_call(kv_back_kernel, "kv_back", [my_recv], [summed], traveling)
    )

    flat_slots = jnp.arange(slots)
    own_slots = replica * slot_cap + jnp.arange(slot_cap)
    slot_used = jnp.any(recv_slot[:, None, :] == own_slots[None, :, None], axis=2)
    matched = slot_used[:, :, None] & (my_send[:, :, None] == jnp.arange(tile_count)[None, None, :])
    anchor = jnp.sum(
        jnp.where(matched, flat_slots.reshape(n_replicas, slot_cap)[:, :, None], 0), axis=(0, 1)
    )
    grad_queries = query_returned.reshape(slots, tile_rows, row_width)[anchor]
    kv_final = local_call(
        kv_final_kernel, "kv_final", [anchor], [kv_returned],
        jax.ShapeDtypeStruct(kv_blocks.shape, keys_values.dtype),
    )
    grad_keys_values = kv_final.transpose(0, 2, 1, 3).reshape(keys_values.shape)
    return (grad_queries, grad_keys_values)


def solution(mesh):
    fine = Mesh(mesh.devices.reshape(mesh.devices.shape[0], 2, 16), ("dp", "xh", "z"))
    tensor = ("xh", "z")
    in_specs = (
        P("dp", None, tensor),
        P("dp", tensor, None),
        P("dp", None, tensor),
        P("dp", None, None),
        P(),
        P("dp", None),
    )
    out_specs = (P("dp", None, tensor), P("dp", tensor, None))
    return jax.shard_map(
        on_device, mesh=fine, in_specs=in_specs, out_specs=out_specs, check_vma=False
    )
```

```python
import functools

import jax
import jax.numpy as jnp
from jax import lax
from jax.experimental import pallas as pl
from jax.experimental.pallas import tpu as pltpu
from jax.sharding import Mesh
from jax.sharding import PartitionSpec as P

HD = 128
KV = 4
PAIR = 2
SCALING = HD ** (-0.5)
LOG2E = 1.4426950408889634
PLANE = ("dp", "xh")
MIRROR = 15
ACROSS = 4
NEAR = 4


def matmul(a, b, contract):
    return lax.dot_general(a, b, (contract, ((), ())), preferred_element_type=jnp.float32)


def pack_kernel(index_ref, q_ref, g_ref, out_ref):
    def body(slot, _):
        tile = index_ref[slot & 1, slot >> 1]
        out_ref[slot, 0] = q_ref[tile]
        out_ref[slot, 1] = g_ref[tile]
        return 0

    lax.fori_loop(0, out_ref.shape[0], body, 0, unroll=2)


def pack(index, queries, grad_out):
    slots = index.size
    return pl.pallas_call(
        pack_kernel,
        out_shape=jax.ShapeDtypeStruct((slots, 2) + queries.shape[1:], queries.dtype),
        in_specs=[
            pl.BlockSpec(memory_space=pltpu.SMEM),
            pl.BlockSpec(memory_space=pltpu.VMEM),
            pl.BlockSpec(memory_space=pltpu.VMEM),
        ],
        out_specs=pl.BlockSpec(memory_space=pltpu.VMEM),
        compiler_params=pltpu.CompilerParams(vmem_limit_bytes=24 * 2**20),
        name="pack_rows",
    )(index, queries, grad_out)


def attention_kernel(
    recv_ref, start_ref, place_ref, qg_ref, *refs
):
    kv_refs, dq_ref, dkv_refs = refs[: 2 * NEAR], refs[2 * NEAR], refs[2 * NEAR + 1 : 4 * NEAR + 1]
    k_all, kt_all, v_all, dk_all, dv_all, *rest = refs[4 * NEAR + 1 :]
    scores, dprobs, diagonal_scores, diagonal_dprobs, stats, dqt = rest
    blocks = k_all.shape[0]
    width = k_all.shape[1]
    tile_rows = width // PAIR
    part = width // NEAR
    factor = SCALING * LOG2E

    def rows_of(slot, first_part):
        begin = (slot % NEAR) * part
        if slot < NEAR:
            return slice(begin, begin + first_part)
        return slice(begin + first_part, begin + part)

    def stage(block, _):
        for slot, ref in enumerate(kv_refs):
            rows = rows_of(slot, part // 4)
            count = rows.stop - rows.start
            key = ref[:, :, 0, block].astype(jnp.float32).reshape(count, HD)
            value = ref[:, :, 1, block].astype(jnp.float32).reshape(count, HD)
            k_all[block, rows] = key.astype(jnp.bfloat16)
            v_all[block, rows] = value.astype(jnp.bfloat16)
        kt_all[block] = k_all[block].astype(jnp.float32).T.astype(jnp.bfloat16)
        return 0

    lax.fori_loop(0, blocks, stage, 0, unroll=2)

    row = lax.broadcasted_iota(jnp.int32, (width, 1), 0)
    holder = (place_ref[0] & 12) | ((place_ref[0] - (row >> 6)) & 3)
    source = holder ^ (((row >> 4) & 1) * MIRROR) ^ (((row >> 5) & 1) * ACROSS)
    key_offset = (
        ((row >> 2) & 1) * tile_rows + ((row >> 3) & 1) * 64 + source * 4 + (row & 3)
    )
    lane = lax.broadcasted_iota(jnp.int32, (1, width), 1)

    def operands(block):
        first = recv_ref[PAIR * block]
        second = recv_ref[PAIR * block + 1]
        query = jnp.concatenate([qg_ref[first, 0], qg_ref[second, 0]], axis=0)
        grad = jnp.concatenate([qg_ref[first, 1], qg_ref[second, 1]], axis=0)
        return query, grad

    def first_row(block):
        low, high = start_ref[PAIR * block], start_ref[PAIR * block + 1]
        return jnp.where(lane < tile_rows, low, high) * tile_rows

    def terms(weights, dprob, key_t, query, grad, inverse, delta):
        probs = weights * inverse
        dscores = (probs * (dprob - delta)).astype(jnp.bfloat16)
        grad_value = matmul(probs.astype(jnp.bfloat16), grad, ((1,), (0,)))
        grad_key = matmul(dscores, query, ((1,), (0,)))
        grad_query = matmul(key_t, dscores, ((1,), (0,)))
        return grad_key, grad_value, grad_query

    def diagonal_products(block, _):
        query, grad = operands(block)
        score = matmul(k_all[block], query, ((1,), (1,)))
        allowed = (key_offset >= first_row(block) - block * width) & (key_offset <= lane)
        score = jnp.where(allowed, score, -jnp.inf)
        diagonal_scores[block] = score
        diagonal_dprobs[block] = matmul(v_all[block], grad, ((1,), (1,)))
        peak = jnp.max(score, axis=0, keepdims=True)
        stats[block, 0] = jnp.broadcast_to(peak, stats.shape[2:])
        dk_all[block] = jnp.zeros_like(dk_all[block])
        dv_all[block] = jnp.zeros_like(dv_all[block])
        dqt[block] = jnp.zeros_like(dqt[block])
        return 0

    lax.fori_loop(0, blocks, diagonal_products, 0, unroll=2)

    def query_block(block, _):
        query, grad = operands(block)
        row_start = first_row(block)
        lowest = start_ref[PAIR * block] // PAIR

        def products(other, peak):
            score = matmul(k_all[other], query, ((1,), (1,)))
            score = jnp.where(key_offset >= row_start - other * width, score, -jnp.inf)
            scores[other] = score
            dprobs[other] = matmul(v_all[other], grad, ((1,), (1,)))
            return jnp.maximum(peak, jnp.max(score, axis=0, keepdims=True))

        peak = lax.fori_loop(lowest, block, products, stats[block, 0][:1])
        shift = peak * factor

        def sums(other, totals):
            weights = jnp.exp2(scores[other] * factor - shift)
            scores[other] = weights
            return (
                totals[0] + jnp.sum(weights, axis=0, keepdims=True),
                totals[1] + jnp.sum(weights * dprobs[other], axis=0, keepdims=True),
            )

        weights = jnp.exp2(diagonal_scores[block] * factor - shift)
        diagonal_scores[block] = weights
        totals = (
            jnp.sum(weights, axis=0, keepdims=True),
            jnp.sum(weights * diagonal_dprobs[block], axis=0, keepdims=True),
        )
        total, weighted = lax.fori_loop(lowest, block, sums, totals)
        inverse = 1.0 / total
        delta = weighted * inverse
        stats[block, 0] = jnp.broadcast_to(inverse, stats.shape[2:])
        stats[block, 1] = jnp.broadcast_to(delta, stats.shape[2:])

        def earlier(other, _):
            grad_key, grad_value, grad_query = terms(
                scores[other], dprobs[other], kt_all[other], query, grad, inverse, delta
            )
            dk_all[other] += grad_key
            dv_all[other] += grad_value
            dqt[block] += grad_query
            return 0

        lax.fori_loop(lowest, block, earlier, 0)
        return 0

    lax.fori_loop(0, blocks, query_block, 0)

    def diagonal_terms(block, _):
        query, grad = operands(block)
        grad_key, grad_value, grad_query = terms(
            diagonal_scores[block], diagonal_dprobs[block], kt_all[block], query, grad,
            stats[block, 0][:1], stats[block, 1][:1],
        )
        dk_all[block] += grad_key
        dv_all[block] += grad_value
        result = ((dqt[block] + grad_query) * SCALING).T.astype(jnp.bfloat16)
        dq_ref[recv_ref[PAIR * block]] = result[:tile_rows]
        dq_ref[recv_ref[PAIR * block + 1]] = result[tile_rows:]
        return 0

    lax.fori_loop(0, blocks, diagonal_terms, 0, unroll=2)

    def unstage(block, _):
        for slot, ref in enumerate(dkv_refs):
            rows = rows_of(slot, part // 2)
            shape = ref.shape[:2] + ref.shape[4:]
            ref[:, :, 0, block] = (dk_all[block, rows] * SCALING).reshape(shape).astype(jnp.bfloat16)
            ref[:, :, 1, block] = dv_all[block, rows].reshape(shape).astype(jnp.bfloat16)
        return 0

    lax.fori_loop(0, blocks, unstage, 0, unroll=2)


def attention(my_recv, start, place, qg, chunks):
    slots, _, tile_rows, _ = qg.shape
    blocks = my_recv.shape[0] // PAIR
    width = PAIR * tile_rows
    vmem = pl.BlockSpec(memory_space=pltpu.VMEM)
    smem = pl.BlockSpec(memory_space=pltpu.SMEM)
    return pl.pallas_call(
        attention_kernel,
        out_shape=(jax.ShapeDtypeStruct((slots, tile_rows, HD), jnp.bfloat16),)
        + (jax.ShapeDtypeStruct((2,) + chunks[0].shape[1:], jnp.bfloat16),) * (2 * NEAR),
        in_specs=[smem] * 3 + [vmem] * (1 + 2 * NEAR),
        out_specs=(vmem,) * (1 + 2 * NEAR),
        scratch_shapes=[
            pltpu.VMEM((blocks, width, HD), jnp.bfloat16),
            pltpu.VMEM((blocks, HD, width), jnp.bfloat16),
            pltpu.VMEM((blocks, width, HD), jnp.bfloat16),
            pltpu.VMEM((blocks, width, HD), jnp.float32),
            pltpu.VMEM((blocks, width, HD), jnp.float32),
            pltpu.VMEM((blocks, width, width), jnp.float32),
            pltpu.VMEM((blocks, width, width), jnp.float32),
            pltpu.VMEM((blocks, width, width), jnp.float32),
            pltpu.VMEM((blocks, width, width), jnp.float32),
            pltpu.VMEM((blocks, 2, 8, width), jnp.float32),
            pltpu.VMEM((blocks, HD, width), jnp.float32),
        ],
        compiler_params=pltpu.CompilerParams(vmem_limit_bytes=24 * 2**20),
        cost_estimate=pl.CostEstimate(
            flops=2 * 10**9, bytes_accessed=6 * 2**20, transcendentals=2 * 10**6
        ),
        name="attention_backward",
    )(my_recv, start, place, qg, *chunks)


def kv_pack_kernel(index_ref, kv_ref, out_ref):
    def body(slot, _):
        tile = index_ref[slot & 1, slot >> 1]
        piece = kv_ref[tile].reshape((2, 2, 2) + kv_ref.shape[2:])
        for half in range(2):
            out_ref[slot >> 1, half, slot & 1] = piece[:, half]
        return 0

    lax.fori_loop(0, 2 * index_ref.shape[1], body, 0, unroll=4)


def kv_unpack_kernel(recv_ref, place_ref, kv_ref, own_ref, other_ref):
    head = place_ref[0] >> 3

    def body(pair, _):
        low = recv_ref[PAIR * pair]
        high = recv_ref[PAIR * pair + 1]
        for half in range(2):
            for kind in range(2):
                for ref, which in ((own_ref, head), (other_ref, 1 - head)):
                    rows = [
                        kv_ref[slot >> 1, half, slot & 1, kind, which].astype(jnp.float32)
                        for slot in (low, high)
                    ]
                    ref[half, kind, pair] = jnp.concatenate(rows, axis=0).astype(jnp.bfloat16)
        return 0

    lax.fori_loop(0, recv_ref.shape[0] // PAIR, body, 0, unroll=4)


def kv_back_kernel(recv_ref, place_ref, own_ref, other_ref, out_ref):
    head = place_ref[0] >> 3
    sliver = out_ref.shape[-2]

    def body(pair, _):
        slots = (recv_ref[PAIR * pair], recv_ref[PAIR * pair + 1])
        for half in range(2):
            for kind in range(2):
                for ref, which in ((own_ref, head), (other_ref, 1 - head)):
                    total = ref[half, kind, pair].astype(jnp.float32)
                    for order, slot in enumerate(slots):
                        rows = total[order * sliver : (order + 1) * sliver]
                        out_ref[slot >> 1, half, slot & 1, kind, which] = rows.astype(jnp.bfloat16)
        return 0

    lax.fori_loop(0, recv_ref.shape[0] // PAIR, body, 0, unroll=4)


def kv_final_kernel(anchor_ref, kv_ref, out_ref):
    def body(tile, _):
        slot = anchor_ref[tile]
        piece = kv_ref[slot >> 1, :, slot & 1]
        for half in range(2):
            for kind in range(2):
                for head in range(2):
                    out_ref[tile, kind * 4 + half * 2 + head] = piece[half, kind, head]
        return 0

    lax.fori_loop(0, anchor_ref.shape[0], body, 0, unroll=4)


def local_call(kernel, name, scalars, arrays, out_shape):
    vmem = pl.BlockSpec(memory_space=pltpu.VMEM)
    smem = pl.BlockSpec(memory_space=pltpu.SMEM)
    return pl.pallas_call(
        kernel,
        out_shape=out_shape,
        in_specs=[smem] * len(scalars) + [vmem] * len(arrays),
        out_specs=jax.tree.map(lambda _: vmem, out_shape),
        compiler_params=pltpu.CompilerParams(vmem_limit_bytes=16 * 2**20),
        name=name,
    )(*scalars, *arrays)


def far_swap(values, flip):
    return lax.ppermute(values, "z", [(place, place ^ flip) for place in range(16)])


def near_shift(values, step):
    pairs = [(place, (place & 12) | ((place + step) & 3)) for place in range(16)]
    return lax.ppermute(values, "z", pairs)


def near_gather(values):
    return [values] + [near_shift(values, step) for step in range(1, NEAR)]


def near_terms(terms):
    return [terms[0]] + [near_shift(terms[step], -step) for step in range(1, NEAR)]


def total(terms):
    return sum(term.astype(jnp.float32) for term in terms)


def on_device(queries, keys_values, grad_out, send_tiles, recv_slot, tile_seq):
    n_replicas = lax.axis_size("dp")
    replica = lax.axis_index("dp")
    tile_count, tile_rows, row_width = queries.shape
    sliver = keys_values.shape[1]
    slot_cap = send_tiles.shape[2]
    slots = n_replicas * slot_cap
    pairs = tile_count // PAIR
    my_send = send_tiles[0]
    outgoing = my_send.T
    my_recv = lax.dynamic_index_in_dim(recv_slot, replica, 0, keepdims=False)
    place = lax.axis_index("z").astype(jnp.int32).reshape(1)
    traveling = jax.ShapeDtypeStruct(
        (n_replicas, 2, slot_cap, 2, 2, sliver, HD), keys_values.dtype
    )
    half_shape = jax.ShapeDtypeStruct((2, 2, pairs, PAIR * sliver, HD), keys_values.dtype)

    def over_plane(values):
        return lax.all_to_all(
            values.reshape((2 * n_replicas,) + values.shape[2:]),
            PLANE, split_axis=0, concat_axis=0, tiled=True,
        ).reshape(values.shape)

    kv_blocks = keys_values.reshape(tile_count, sliver, 2 * KV, HD).transpose(0, 2, 1, 3)
    kv_arrived = over_plane(
        local_call(kv_pack_kernel, "kv_pack", [outgoing], [kv_blocks], traveling)
    )
    own, other = local_call(
        kv_unpack_kernel, "kv_unpack", [my_recv, place], [kv_arrived], (half_shape, half_shape)
    )
    qg_packed = pack(outgoing, queries, grad_out)
    qg_arrived = lax.all_to_all(
        qg_packed.reshape(n_replicas, slot_cap, 2, tile_rows, row_width),
        "dp", split_axis=0, concat_axis=0, tiled=True,
    ).reshape(slots, 2, tile_rows, row_width)
    far = jnp.stack(
        [far_swap(other, MIRROR), far_swap(own, ACROSS), far_swap(other, MIRROR ^ ACROSS)]
    )
    own_chunks = near_gather(own[None])
    far, own_chunks, qg_arrived = lax.optimization_barrier((far, own_chunks, qg_arrived))
    chunks = own_chunks + near_gather(far)

    seq = tile_seq[0]
    start = jnp.sum((seq[None, :] < seq[:, None]).astype(jnp.int32), axis=1)
    query_back, *terms = attention(my_recv, start, place, qg_arrived, chunks)
    query_returned = lax.all_to_all(
        query_back.reshape(n_replicas, slot_cap, tile_rows, row_width),
        "dp", split_axis=0, concat_axis=0, tiled=True,
    )
    across_terms = near_terms(terms[NEAR:])
    own_terms, across_terms = lax.optimization_barrier((terms[:NEAR], across_terms))
    arrived = far_swap(total(across_terms).astype(jnp.bfloat16), ACROSS)
    base = lax.optimization_barrier(total([arrived, own_terms[0]]))
    summed = total([base] + near_terms(own_terms)[1:]).astype(jnp.bfloat16)
    swapped = [summed[0], far_swap(summed[1], MIRROR)]
    swapped, query_returned = lax.optimization_barrier((swapped, query_returned))
    kv_returned = over_plane(
        local_call(kv_back_kernel, "kv_back", [my_recv, place], swapped, traveling)
    )

    flat_slots = jnp.arange(slots)
    own_slots = replica * slot_cap + jnp.arange(slot_cap)
    slot_used = jnp.any(recv_slot[:, None, :] == own_slots[None, :, None], axis=2)
    matched = slot_used[:, :, None] & (my_send[:, :, None] == jnp.arange(tile_count)[None, None, :])
    anchor = jnp.sum(
        jnp.where(matched, flat_slots.reshape(n_replicas, slot_cap)[:, :, None], 0), axis=(0, 1)
    )
    grad_queries = query_returned.reshape(slots, tile_rows, row_width)[anchor]
    kv_final = local_call(
        kv_final_kernel, "kv_final", [anchor], [kv_returned],
        jax.ShapeDtypeStruct(kv_blocks.shape, keys_values.dtype),
    )
    grad_keys_values = kv_final.transpose(0, 2, 1, 3).reshape(keys_values.shape)
    return (grad_queries, grad_keys_values)


def solution(mesh):
    fine = Mesh(mesh.devices.reshape(mesh.devices.shape[0], 2, 16), ("dp", "xh", "z"))
    tensor = ("xh", "z")
    in_specs = (
        P("dp", None, tensor),
        P("dp", tensor, None),
        P("dp", None, tensor),
        P("dp", None, None),
        P(),
        P("dp", None),
    )
    out_specs = (P("dp", None, tensor), P("dp", tensor, None))
    return jax.shard_map(
        on_device, mesh=fine, in_specs=in_specs, out_specs=out_specs, check_vma=False
    )
```

```python
import functools

import jax
import jax.numpy as jnp
from jax import lax
from jax.experimental import pallas as pl
from jax.experimental.pallas import tpu as pltpu
from jax.sharding import Mesh
from jax.sharding import PartitionSpec as P

HD = 128
KV = 4
PAIR = 2
SCALING = HD ** (-0.5)
LOG2E = 1.4426950408889634
PLANE = ("dp", "xh")
MIRROR = 15
ACROSS = 4
NEAR = 4


def matmul(a, b, contract):
    return lax.dot_general(a, b, (contract, ((), ())), preferred_element_type=jnp.float32)


def pack_kernel(index_ref, q_ref, g_ref, out_ref):
    def body(slot, _):
        tile = index_ref[slot & 1, slot >> 1]
        out_ref[slot, 0] = q_ref[tile]
        out_ref[slot, 1] = g_ref[tile]
        return 0

    lax.fori_loop(0, out_ref.shape[0], body, 0, unroll=2)


def pack(index, queries, grad_out):
    slots = index.size
    return pl.pallas_call(
        pack_kernel,
        out_shape=jax.ShapeDtypeStruct((slots, 2) + queries.shape[1:], queries.dtype),
        in_specs=[
            pl.BlockSpec(memory_space=pltpu.SMEM),
            pl.BlockSpec(memory_space=pltpu.VMEM),
            pl.BlockSpec(memory_space=pltpu.VMEM),
        ],
        out_specs=pl.BlockSpec(memory_space=pltpu.VMEM),
        compiler_params=pltpu.CompilerParams(vmem_limit_bytes=24 * 2**20),
        name="pack_rows",
    )(index, queries, grad_out)


def attention_kernel(
    recv_ref, start_ref, place_ref, qg_ref, *refs
):
    kv_refs, dq_ref, dkv_refs = refs[: 2 * NEAR], refs[2 * NEAR], refs[2 * NEAR + 1 : 5 * NEAR + 1]
    k_all, kt_all, v_all, dk_all, dv_all, *rest = refs[5 * NEAR + 1 :]
    scores, dprobs, diagonal_scores, diagonal_dprobs, stats, dqt = rest
    blocks = k_all.shape[0]
    width = k_all.shape[1]
    tile_rows = width // PAIR
    part = width // NEAR
    factor = SCALING * LOG2E

    def rows_of(slot, *bounds):
        begin = (slot % NEAR) * part
        return slice(begin + bounds[slot // NEAR], begin + bounds[slot // NEAR + 1])

    def stage(block, _):
        for slot, ref in enumerate(kv_refs):
            rows = rows_of(slot, 0, part // 4, part)
            count = rows.stop - rows.start
            key = ref[:, :, 0, block].astype(jnp.float32).reshape(count, HD)
            value = ref[:, :, 1, block].astype(jnp.float32).reshape(count, HD)
            k_all[block, rows] = key.astype(jnp.bfloat16)
            v_all[block, rows] = value.astype(jnp.bfloat16)
        kt_all[block] = k_all[block].astype(jnp.float32).T.astype(jnp.bfloat16)
        return 0

    lax.fori_loop(0, blocks, stage, 0, unroll=2)

    row = lax.broadcasted_iota(jnp.int32, (width, 1), 0)
    holder = (place_ref[0] & 12) | ((place_ref[0] - (row >> 6)) & 3)
    source = holder ^ (((row >> 4) & 1) * MIRROR) ^ (((row >> 5) & 1) * ACROSS)
    key_offset = (
        ((row >> 2) & 1) * tile_rows + ((row >> 3) & 1) * 64 + source * 4 + (row & 3)
    )
    lane = lax.broadcasted_iota(jnp.int32, (1, width), 1)

    def operands(block):
        first = recv_ref[PAIR * block]
        second = recv_ref[PAIR * block + 1]
        query = jnp.concatenate([qg_ref[first, 0], qg_ref[second, 0]], axis=0)
        grad = jnp.concatenate([qg_ref[first, 1], qg_ref[second, 1]], axis=0)
        return query, grad

    def first_row(block):
        low, high = start_ref[PAIR * block], start_ref[PAIR * block + 1]
        return jnp.where(lane < tile_rows, low, high) * tile_rows

    def terms(weights, dprob, key_t, query, grad, inverse, delta):
        probs = weights * inverse
        dscores = (probs * (dprob - delta)).astype(jnp.bfloat16)
        grad_value = matmul(probs.astype(jnp.bfloat16), grad, ((1,), (0,)))
        grad_key = matmul(dscores, query, ((1,), (0,)))
        grad_query = matmul(key_t, dscores, ((1,), (0,)))
        return grad_key, grad_value, grad_query

    def diagonal_products(block, _):
        query, grad = operands(block)
        score = matmul(k_all[block], query, ((1,), (1,)))
        allowed = (key_offset >= first_row(block) - block * width) & (key_offset <= lane)
        score = jnp.where(allowed, score, -jnp.inf)
        diagonal_scores[block] = score
        diagonal_dprobs[block] = matmul(v_all[block], grad, ((1,), (1,)))
        peak = jnp.max(score, axis=0, keepdims=True)
        stats[block, 0] = jnp.broadcast_to(peak, stats.shape[2:])
        dk_all[block] = jnp.zeros_like(dk_all[block])
        dv_all[block] = jnp.zeros_like(dv_all[block])
        dqt[block] = jnp.zeros_like(dqt[block])
        return 0

    lax.fori_loop(0, blocks, diagonal_products, 0, unroll=4)

    def query_block(block, _):
        query, grad = operands(block)
        row_start = first_row(block)
        lowest = start_ref[PAIR * block] // PAIR

        def products(other, peak):
            score = matmul(k_all[other], query, ((1,), (1,)))
            score = jnp.where(key_offset >= row_start - other * width, score, -jnp.inf)
            scores[other] = score
            dprobs[other] = matmul(v_all[other], grad, ((1,), (1,)))
            return jnp.maximum(peak, jnp.max(score, axis=0, keepdims=True))

        peak = lax.fori_loop(lowest, block, products, stats[block, 0][:1])
        shift = peak * factor

        def sums(other, totals):
            weights = jnp.exp2(scores[other] * factor - shift)
            scores[other] = weights
            return (
                totals[0] + jnp.sum(weights, axis=0, keepdims=True),
                totals[1] + jnp.sum(weights * dprobs[other], axis=0, keepdims=True),
            )

        weights = jnp.exp2(diagonal_scores[block] * factor - shift)
        diagonal_scores[block] = weights
        totals = (
            jnp.sum(weights, axis=0, keepdims=True),
            jnp.sum(weights * diagonal_dprobs[block], axis=0, keepdims=True),
        )
        total, weighted = lax.fori_loop(lowest, block, sums, totals)
        inverse = 1.0 / total
        delta = weighted * inverse
        stats[block, 0] = jnp.broadcast_to(inverse, stats.shape[2:])
        stats[block, 1] = jnp.broadcast_to(delta, stats.shape[2:])

        def earlier(other, _):
            grad_key, grad_value, grad_query = terms(
                scores[other], dprobs[other], kt_all[other], query, grad, inverse, delta
            )
            dk_all[other] += grad_key
            dv_all[other] += grad_value
            dqt[block] += grad_query
            return 0

        lax.fori_loop(lowest, block, earlier, 0)
        return 0

    lax.fori_loop(0, blocks, query_block, 0)

    def diagonal_terms(block, _):
        query, grad = operands(block)
        grad_key, grad_value, grad_query = terms(
            diagonal_scores[block], diagonal_dprobs[block], kt_all[block], query, grad,
            stats[block, 0][:1], stats[block, 1][:1],
        )
        dk_all[block] += grad_key
        dv_all[block] += grad_value
        result = ((dqt[block] + grad_query) * SCALING).T.astype(jnp.bfloat16)
        dq_ref[recv_ref[PAIR * block]] = result[:tile_rows]
        dq_ref[recv_ref[PAIR * block + 1]] = result[tile_rows:]
        return 0

    lax.fori_loop(0, blocks, diagonal_terms, 0, unroll=4)

    def unstage(block, _):
        for slot, ref in enumerate(dkv_refs):
            rows = rows_of(slot, 0, part // 4, part // 2, part)
            shape = ref.shape[:2] + ref.shape[4:]
            ref[:, :, 0, block] = (dk_all[block, rows] * SCALING).reshape(shape).astype(jnp.bfloat16)
            ref[:, :, 1, block] = dv_all[block, rows].reshape(shape).astype(jnp.bfloat16)
        return 0

    lax.fori_loop(0, blocks, unstage, 0, unroll=2)


def attention(my_recv, start, place, qg, chunks):
    slots, _, tile_rows, _ = qg.shape
    blocks = my_recv.shape[0] // PAIR
    width = PAIR * tile_rows
    vmem = pl.BlockSpec(memory_space=pltpu.VMEM)
    smem = pl.BlockSpec(memory_space=pltpu.SMEM)
    return pl.pallas_call(
        attention_kernel,
        out_shape=(jax.ShapeDtypeStruct((slots, tile_rows, HD), jnp.bfloat16),)
        + tuple(
            jax.ShapeDtypeStruct((count,) + chunks[0].shape[1:], jnp.bfloat16)
            for count in (1, 1, 2)
            for _ in range(NEAR)
        ),
        in_specs=[smem] * 3 + [vmem] * (1 + 2 * NEAR),
        out_specs=(vmem,) * (1 + 3 * NEAR),
        scratch_shapes=[
            pltpu.VMEM((blocks, width, HD), jnp.bfloat16),
            pltpu.VMEM((blocks, HD, width), jnp.bfloat16),
            pltpu.VMEM((blocks, width, HD), jnp.bfloat16),
            pltpu.VMEM((blocks, width, HD), jnp.float32),
            pltpu.VMEM((blocks, width, HD), jnp.float32),
            pltpu.VMEM((blocks, width, width), jnp.float32),
            pltpu.VMEM((blocks, width, width), jnp.float32),
            pltpu.VMEM((blocks, width, width), jnp.float32),
            pltpu.VMEM((blocks, width, width), jnp.float32),
            pltpu.VMEM((blocks, 2, 8, width), jnp.float32),
            pltpu.VMEM((blocks, HD, width), jnp.float32),
        ],
        compiler_params=pltpu.CompilerParams(vmem_limit_bytes=24 * 2**20),
        cost_estimate=pl.CostEstimate(
            flops=2 * 10**9, bytes_accessed=6 * 2**20, transcendentals=2 * 10**6
        ),
        name="attention_backward",
    )(my_recv, start, place, qg, *chunks)


def kv_pack_kernel(index_ref, kv_ref, out_ref):
    def body(slot, _):
        tile = index_ref[slot & 1, slot >> 1]
        piece = kv_ref[tile].reshape((2, 2, 2) + kv_ref.shape[2:])
        for half in range(2):
            out_ref[slot >> 1, half, slot & 1] = piece[:, half]
        return 0

    lax.fori_loop(0, 2 * index_ref.shape[1], body, 0, unroll=4)


def kv_unpack_kernel(recv_ref, place_ref, kv_ref, own_ref, other_ref):
    head = place_ref[0] >> 3

    def body(pair, _):
        low = recv_ref[PAIR * pair]
        high = recv_ref[PAIR * pair + 1]
        for half in range(2):
            for kind in range(2):
                for ref, which in ((own_ref, head), (other_ref, 1 - head)):
                    rows = [
                        kv_ref[slot >> 1, half, slot & 1, kind, which].astype(jnp.float32)
                        for slot in (low, high)
                    ]
                    ref[half, kind, pair] = jnp.concatenate(rows, axis=0).astype(jnp.bfloat16)
        return 0

    lax.fori_loop(0, recv_ref.shape[0] // PAIR, body, 0, unroll=4)


def kv_back_kernel(recv_ref, place_ref, *refs):
    own_refs, (across_ref, other_ref, out_ref) = refs[:NEAR], refs[NEAR:]
    head = place_ref[0] >> 3
    sliver = out_ref.shape[-2]

    def body(pair, _):
        slots = (recv_ref[PAIR * pair], recv_ref[PAIR * pair + 1])
        for half in range(2):
            for kind in range(2):
                own = across_ref[0, half, kind, pair].astype(jnp.float32)
                for ref in own_refs:
                    own += ref[0, half, kind, pair].astype(jnp.float32)
                for total, which in ((own, head), (other_ref[half, kind, pair], 1 - head)):
                    for order, slot in enumerate(slots):
                        rows = total[order * sliver : (order + 1) * sliver]
                        out_ref[slot >> 1, half, slot & 1, kind, which] = rows.astype(jnp.bfloat16)
        return 0

    lax.fori_loop(0, recv_ref.shape[0] // PAIR, body, 0, unroll=4)


def kv_final_kernel(anchor_ref, kv_ref, out_ref):
    def body(tile, _):
        slot = anchor_ref[tile]
        piece = kv_ref[slot >> 1, :, slot & 1]
        for half in range(2):
            for kind in range(2):
                for head in range(2):
                    out_ref[tile, kind * 4 + half * 2 + head] = piece[half, kind, head]
        return 0

    lax.fori_loop(0, anchor_ref.shape[0], body, 0, unroll=4)


def local_call(kernel, name, scalars, arrays, out_shape):
    vmem = pl.BlockSpec(memory_space=pltpu.VMEM)
    smem = pl.BlockSpec(memory_space=pltpu.SMEM)
    return pl.pallas_call(
        kernel,
        out_shape=out_shape,
        in_specs=[smem] * len(scalars) + [vmem] * len(arrays),
        out_specs=jax.tree.map(lambda _: vmem, out_shape),
        compiler_params=pltpu.CompilerParams(vmem_limit_bytes=16 * 2**20),
        name=name,
    )(*scalars, *arrays)


def far_swap(values, flip):
    return lax.ppermute(values, "z", [(place, place ^ flip) for place in range(16)])


def near_shift(values, step):
    pairs = [(place, (place & 12) | ((place + step) & 3)) for place in range(16)]
    return lax.ppermute(values, "z", pairs)


def near_gather(values):
    return [values] + [near_shift(values, step) for step in range(1, NEAR)]


def near_terms(terms):
    return [terms[0]] + [near_shift(terms[step], -step) for step in range(1, NEAR)]


def total(terms):
    return sum(term.astype(jnp.float32) for term in terms)


def on_device(queries, keys_values, grad_out, send_tiles, recv_slot, tile_seq):
    n_replicas = lax.axis_size("dp")
    replica = lax.axis_index("dp")
    tile_count, tile_rows, row_width = queries.shape
    sliver = keys_values.shape[1]
    slot_cap = send_tiles.shape[2]
    slots = n_replicas * slot_cap
    pairs = tile_count // PAIR
    my_send = send_tiles[0]
    outgoing = my_send.T
    my_recv = lax.dynamic_index_in_dim(recv_slot, replica, 0, keepdims=False)
    place = lax.axis_index("z").astype(jnp.int32).reshape(1)
    traveling = jax.ShapeDtypeStruct(
        (n_replicas, 2, slot_cap, 2, 2, sliver, HD), keys_values.dtype
    )
    half_shape = jax.ShapeDtypeStruct((2, 2, pairs, PAIR * sliver, HD), keys_values.dtype)

    def over_plane(values):
        return lax.all_to_all(
            values.reshape((2 * n_replicas,) + values.shape[2:]),
            PLANE, split_axis=0, concat_axis=0, tiled=True,
        ).reshape(values.shape)

    kv_blocks = keys_values.reshape(tile_count, sliver, 2 * KV, HD).transpose(0, 2, 1, 3)
    kv_arrived = over_plane(
        local_call(kv_pack_kernel, "kv_pack", [outgoing], [kv_blocks], traveling)
    )
    own, other = local_call(
        kv_unpack_kernel, "kv_unpack", [my_recv, place], [kv_arrived], (half_shape, half_shape)
    )
    qg_packed = pack(outgoing, queries, grad_out)
    qg_arrived = lax.all_to_all(
        qg_packed.reshape(n_replicas, slot_cap, 2, tile_rows, row_width),
        "dp", split_axis=0, concat_axis=0, tiled=True,
    ).reshape(slots, 2, tile_rows, row_width)
    far = jnp.stack(
        [far_swap(other, MIRROR), far_swap(own, ACROSS), far_swap(other, MIRROR ^ ACROSS)]
    )
    own_chunks = near_gather(own[None])
    far, own_chunks, qg_arrived = lax.optimization_barrier((far, own_chunks, qg_arrived))
    chunks = own_chunks + near_gather(far)

    seq = tile_seq[0]
    start = jnp.sum((seq[None, :] < seq[:, None]).astype(jnp.int32), axis=1)
    query_back, *terms = attention(my_recv, start, place, qg_arrived, chunks)
    query_returned = lax.all_to_all(
        query_back.reshape(n_replicas, slot_cap, tile_rows, row_width),
        "dp", split_axis=0, concat_axis=0, tiled=True,
    )
    own_terms, mirror_terms = terms[:NEAR], terms[NEAR : 2 * NEAR]
    across_terms = near_terms(terms[2 * NEAR :])
    own_terms, mirror_terms, across_terms = lax.optimization_barrier(
        (own_terms, mirror_terms, across_terms)
    )
    arrived = far_swap(total(across_terms).astype(jnp.bfloat16), ACROSS)
    base = lax.optimization_barrier(total([arrived[1:], mirror_terms[0]]))
    mirror_sum = total([base] + near_terms(mirror_terms)[1:])[0].astype(jnp.bfloat16)
    own_terms, mirror_sum = lax.optimization_barrier((own_terms, mirror_sum))
    other = lax.optimization_barrier(far_swap(mirror_sum, MIRROR).astype(jnp.float32))
    last = near_terms(own_terms) + [arrived, other]
    last, query_returned = lax.optimization_barrier((last, query_returned))
    kv_returned = over_plane(
        local_call(kv_back_kernel, "kv_back", [my_recv, place], last, traveling)
    )

    flat_slots = jnp.arange(slots)
    own_slots = replica * slot_cap + jnp.arange(slot_cap)
    slot_used = jnp.any(recv_slot[:, None, :] == own_slots[None, :, None], axis=2)
    matched = slot_used[:, :, None] & (my_send[:, :, None] == jnp.arange(tile_count)[None, None, :])
    anchor = jnp.sum(
        jnp.where(matched, flat_slots.reshape(n_replicas, slot_cap)[:, :, None], 0), axis=(0, 1)
    )
    grad_queries = query_returned.reshape(slots, tile_rows, row_width)[anchor]
    kv_final = local_call(
        kv_final_kernel, "kv_final", [anchor], [kv_returned],
        jax.ShapeDtypeStruct(kv_blocks.shape, keys_values.dtype),
    )
    grad_keys_values = kv_final.transpose(0, 2, 1, 3).reshape(keys_values.shape)
    return (grad_queries, grad_keys_values)


def solution(mesh):
    fine = Mesh(mesh.devices.reshape(mesh.devices.shape[0], 2, 16), ("dp", "xh", "z"))
    tensor = ("xh", "z")
    in_specs = (
        P("dp", None, tensor),
        P("dp", tensor, None),
        P("dp", None, tensor),
        P("dp", None, None),
        P(),
        P("dp", None),
    )
    out_specs = (P("dp", None, tensor), P("dp", tensor, None))
    return jax.shard_map(
        on_device, mesh=fine, in_specs=in_specs, out_specs=out_specs, check_vma=False
    )
```

```python
import functools

import jax
import jax.numpy as jnp
from jax import lax
from jax.experimental import pallas as pl
from jax.experimental.pallas import tpu as pltpu
from jax.sharding import Mesh
from jax.sharding import PartitionSpec as P

HD = 128
KV = 4
PAIR = 2
SCALING = HD ** (-0.5)
LOG2E = 1.4426950408889634
PLANE = ("dp", "xh")
MIRROR = 12
ACROSS = 7
NEAR = 4


def matmul(a, b, contract):
    return lax.dot_general(a, b, (contract, ((), ())), preferred_element_type=jnp.float32)


def pack_kernel(index_ref, q_ref, g_ref, out_ref):
    def body(slot, _):
        tile = index_ref[slot & 1, slot >> 1]
        out_ref[slot, 0] = q_ref[tile]
        out_ref[slot, 1] = g_ref[tile]
        return 0

    lax.fori_loop(0, out_ref.shape[0], body, 0, unroll=2)


def pack(index, queries, grad_out):
    slots = index.size
    return pl.pallas_call(
        pack_kernel,
        out_shape=jax.ShapeDtypeStruct((slots, 2) + queries.shape[1:], queries.dtype),
        in_specs=[
            pl.BlockSpec(memory_space=pltpu.SMEM),
            pl.BlockSpec(memory_space=pltpu.VMEM),
            pl.BlockSpec(memory_space=pltpu.VMEM),
        ],
        out_specs=pl.BlockSpec(memory_space=pltpu.VMEM),
        compiler_params=pltpu.CompilerParams(vmem_limit_bytes=24 * 2**20),
        name="pack_rows",
    )(index, queries, grad_out)


def attention_kernel(
    recv_ref, start_ref, place_ref, qg_ref, *refs
):
    kv_refs, dq_ref, dkv_refs = refs[: 2 * NEAR], refs[2 * NEAR], refs[2 * NEAR + 1 : 4 * NEAR + 1]
    k_all, kt_all, v_all, dk_all, dv_all, *rest = refs[4 * NEAR + 1 :]
    scores, dprobs, diagonal_scores, diagonal_dprobs, stats, dqt = rest
    blocks = k_all.shape[0]
    width = k_all.shape[1]
    tile_rows = width // PAIR
    part = width // NEAR
    factor = SCALING * LOG2E

    def rows_of(slot, first_part):
        begin = (slot % NEAR) * part
        if slot < NEAR:
            return slice(begin, begin + first_part)
        return slice(begin + first_part, begin + part)

    def stage(block, _):
        for slot, ref in enumerate(kv_refs):
            rows = rows_of(slot, part // 4)
            count = rows.stop - rows.start
            key = ref[:, :, 0, block].astype(jnp.float32).reshape(count, HD)
            value = ref[:, :, 1, block].astype(jnp.float32).reshape(count, HD)
            k_all[block, rows] = key.astype(jnp.bfloat16)
            v_all[block, rows] = value.astype(jnp.bfloat16)
        kt_all[block] = k_all[block].astype(jnp.float32).T.astype(jnp.bfloat16)
        return 0

    lax.fori_loop(0, blocks, stage, 0, unroll=2)

    row = lax.broadcasted_iota(jnp.int32, (width, 1), 0)
    holder = (place_ref[0] & 12) | ((place_ref[0] - (row >> 6)) & 3)
    source = holder ^ (((row >> 4) & 1) * MIRROR) ^ (((row >> 5) & 1) * ACROSS)
    key_offset = (
        ((row >> 2) & 1) * tile_rows + ((row >> 3) & 1) * 64 + source * 4 + (row & 3)
    )
    lane = lax.broadcasted_iota(jnp.int32, (1, width), 1)

    def operands(block):
        first = recv_ref[PAIR * block]
        second = recv_ref[PAIR * block + 1]
        query = jnp.concatenate([qg_ref[first, 0], qg_ref[second, 0]], axis=0)
        grad = jnp.concatenate([qg_ref[first, 1], qg_ref[second, 1]], axis=0)
        return query, grad

    def first_row(block):
        low, high = start_ref[PAIR * block], start_ref[PAIR * block + 1]
        return jnp.where(lane < tile_rows, low, high) * tile_rows

    def terms(weights, dprob, key_t, query, grad, inverse, delta):
        probs = weights * inverse
        dscores = (probs * (dprob - delta)).astype(jnp.bfloat16)
        grad_value = matmul(probs.astype(jnp.bfloat16), grad, ((1,), (0,)))
        grad_key = matmul(dscores, query, ((1,), (0,)))
        grad_query = matmul(key_t, dscores, ((1,), (0,)))
        return grad_key, grad_value, grad_query

    def diagonal_products(block, _):
        query, grad = operands(block)
        score = matmul(k_all[block], query, ((1,), (1,)))
        allowed = (key_offset >= first_row(block) - block * width) & (key_offset <= lane)
        score = jnp.where(allowed, score, -jnp.inf)
        diagonal_scores[block] = score
        diagonal_dprobs[block] = matmul(v_all[block], grad, ((1,), (1,)))
        peak = jnp.max(score, axis=0, keepdims=True)
        stats[block, 0] = jnp.broadcast_to(peak, stats.shape[2:])
        dk_all[block] = jnp.zeros_like(dk_all[block])
        dv_all[block] = jnp.zeros_like(dv_all[block])
        dqt[block] = jnp.zeros_like(dqt[block])
        return 0

    lax.fori_loop(0, blocks, diagonal_products, 0, unroll=4)

    def sweep(begin, end, step, state):
        twice = (end - begin) >> 1

        def two(index, state):
            return step(begin + 2 * index + 1, step(begin + 2 * index, state))

        state = lax.fori_loop(0, twice, two, state)
        return lax.fori_loop(begin + 2 * twice, end, step, state)

    def query_block(block, _):
        query, grad = operands(block)
        row_start = first_row(block)
        lowest = start_ref[PAIR * block] // PAIR

        def products(other, peak):
            score = matmul(k_all[other], query, ((1,), (1,)))
            score = jnp.where(key_offset >= row_start - other * width, score, -jnp.inf)
            scores[other] = score
            dprobs[other] = matmul(v_all[other], grad, ((1,), (1,)))
            return jnp.maximum(peak, jnp.max(score, axis=0, keepdims=True))

        peak = sweep(lowest, block, products, stats[block, 0][:1])
        shift = peak * factor

        def sums(other, totals):
            weights = jnp.exp2(scores[other] * factor - shift)
            scores[other] = weights
            return (
                totals[0] + jnp.sum(weights, axis=0, keepdims=True),
                totals[1] + jnp.sum(weights * dprobs[other], axis=0, keepdims=True),
            )

        weights = jnp.exp2(diagonal_scores[block] * factor - shift)
        diagonal_scores[block] = weights
        totals = (
            jnp.sum(weights, axis=0, keepdims=True),
            jnp.sum(weights * diagonal_dprobs[block], axis=0, keepdims=True),
        )
        total, weighted = sweep(lowest, block, sums, totals)
        inverse = 1.0 / total
        delta = weighted * inverse
        stats[block, 0] = jnp.broadcast_to(inverse, stats.shape[2:])
        stats[block, 1] = jnp.broadcast_to(delta, stats.shape[2:])

        def earlier(other, _):
            grad_key, grad_value, grad_query = terms(
                scores[other], dprobs[other], kt_all[other], query, grad, inverse, delta
            )
            dk_all[other] += grad_key
            dv_all[other] += grad_value
            dqt[block] += grad_query
            return 0

        sweep(lowest, block, earlier, 0)
        return 0

    lax.fori_loop(0, blocks, query_block, 0)

    def diagonal_terms(block, _):
        query, grad = operands(block)
        grad_key, grad_value, grad_query = terms(
            diagonal_scores[block], diagonal_dprobs[block], kt_all[block], query, grad,
            stats[block, 0][:1], stats[block, 1][:1],
        )
        dk_all[block] += grad_key
        dv_all[block] += grad_value
        result = ((dqt[block] + grad_query) * SCALING).T.astype(jnp.bfloat16)
        dq_ref[recv_ref[PAIR * block]] = result[:tile_rows]
        dq_ref[recv_ref[PAIR * block + 1]] = result[tile_rows:]
        return 0

    lax.fori_loop(0, blocks, diagonal_terms, 0, unroll=4)

    def unstage(block, _):
        for slot, ref in enumerate(dkv_refs):
            rows = rows_of(slot, part // 2)
            shape = ref.shape[:2] + ref.shape[4:]
            ref[:, :, 0, block] = (dk_all[block, rows] * SCALING).reshape(shape).astype(jnp.bfloat16)
            ref[:, :, 1, block] = dv_all[block, rows].reshape(shape).astype(jnp.bfloat16)
        return 0

    lax.fori_loop(0, blocks, unstage, 0, unroll=2)


def attention(my_recv, start, place, qg, chunks):
    slots, _, tile_rows, _ = qg.shape
    blocks = my_recv.shape[0] // PAIR
    width = PAIR * tile_rows
    vmem = pl.BlockSpec(memory_space=pltpu.VMEM)
    smem = pl.BlockSpec(memory_space=pltpu.SMEM)
    return pl.pallas_call(
        attention_kernel,
        out_shape=(jax.ShapeDtypeStruct((slots, tile_rows, HD), jnp.bfloat16),)
        + (jax.ShapeDtypeStruct((2,) + chunks[0].shape[1:], jnp.bfloat16),) * (2 * NEAR),
        in_specs=[smem] * 3 + [vmem] * (1 + 2 * NEAR),
        out_specs=(vmem,) * (1 + 2 * NEAR),
        scratch_shapes=[
            pltpu.VMEM((blocks, width, HD), jnp.bfloat16),
            pltpu.VMEM((blocks, HD, width), jnp.bfloat16),
            pltpu.VMEM((blocks, width, HD), jnp.bfloat16),
            pltpu.VMEM((blocks, width, HD), jnp.float32),
            pltpu.VMEM((blocks, width, HD), jnp.float32),
            pltpu.VMEM((blocks, width, width), jnp.float32),
            pltpu.VMEM((blocks, width, width), jnp.float32),
            pltpu.VMEM((blocks, width, width), jnp.float32),
            pltpu.VMEM((blocks, width, width), jnp.float32),
            pltpu.VMEM((blocks, 2, 8, width), jnp.float32),
            pltpu.VMEM((blocks, HD, width), jnp.float32),
        ],
        compiler_params=pltpu.CompilerParams(vmem_limit_bytes=24 * 2**20),
        cost_estimate=pl.CostEstimate(
            flops=2 * 10**9, bytes_accessed=6 * 2**20, transcendentals=2 * 10**6
        ),
        name="attention_backward",
    )(my_recv, start, place, qg, *chunks)


def kv_pack_kernel(index_ref, kv_ref, out_ref):
    def body(slot, _):
        tile = index_ref[slot & 1, slot >> 1]
        piece = kv_ref[tile].reshape((2, 2, 2) + kv_ref.shape[2:])
        for half in range(2):
            out_ref[slot >> 1, half, slot & 1] = piece[:, half]
        return 0

    lax.fori_loop(0, 2 * index_ref.shape[1], body, 0, unroll=4)


def kv_unpack_kernel(recv_ref, place_ref, kv_ref, own_ref, other_ref):
    head = place_ref[0] >> 3

    def body(pair, _):
        low = recv_ref[PAIR * pair]
        high = recv_ref[PAIR * pair + 1]
        for half in range(2):
            for kind in range(2):
                for ref, which in ((own_ref, head), (other_ref, 1 - head)):
                    rows = [
                        kv_ref[slot >> 1, half, slot & 1, kind, which].astype(jnp.float32)
                        for slot in (low, high)
                    ]
                    ref[half, kind, pair] = jnp.concatenate(rows, axis=0).astype(jnp.bfloat16)
        return 0

    lax.fori_loop(0, recv_ref.shape[0] // PAIR, body, 0, unroll=4)


def kv_back_kernel(recv_ref, place_ref, own_ref, other_ref, out_ref):
    head = place_ref[0] >> 3
    sliver = out_ref.shape[-2]

    def body(pair, _):
        slots = (recv_ref[PAIR * pair], recv_ref[PAIR * pair + 1])
        for half in range(2):
            for kind in range(2):
                for ref, which in ((own_ref, head), (other_ref, 1 - head)):
                    total = ref[half, kind, pair].astype(jnp.float32)
                    for order, slot in enumerate(slots):
                        rows = total[order * sliver : (order + 1) * sliver]
                        out_ref[slot >> 1, half, slot & 1, kind, which] = rows.astype(jnp.bfloat16)
        return 0

    lax.fori_loop(0, recv_ref.shape[0] // PAIR, body, 0, unroll=4)


def kv_final_kernel(anchor_ref, kv_ref, out_ref):
    def body(tile, _):
        slot = anchor_ref[tile]
        piece = kv_ref[slot >> 1, :, slot & 1]
        for half in range(2):
            for kind in range(2):
                for head in range(2):
                    out_ref[tile, kind * 4 + half * 2 + head] = piece[half, kind, head]
        return 0

    lax.fori_loop(0, anchor_ref.shape[0], body, 0, unroll=4)


def local_call(kernel, name, scalars, arrays, out_shape):
    vmem = pl.BlockSpec(memory_space=pltpu.VMEM)
    smem = pl.BlockSpec(memory_space=pltpu.SMEM)
    return pl.pallas_call(
        kernel,
        out_shape=out_shape,
        in_specs=[smem] * len(scalars) + [vmem] * len(arrays),
        out_specs=jax.tree.map(lambda _: vmem, out_shape),
        compiler_params=pltpu.CompilerParams(vmem_limit_bytes=16 * 2**20),
        name=name,
    )(*scalars, *arrays)


def far_swap(values, flip):
    return lax.ppermute(values, "z", [(place, place ^ flip) for place in range(16)])


def near_shift(values, step):
    pairs = [(place, (place & 12) | ((place + step) & 3)) for place in range(16)]
    return lax.ppermute(values, "z", pairs)


def near_gather(values):
    return [values] + [near_shift(values, step) for step in range(1, NEAR)]


def near_terms(terms):
    return [terms[0]] + [near_shift(terms[step], -step) for step in range(1, NEAR)]


def total(terms):
    return sum(term.astype(jnp.float32) for term in terms)


def on_device(queries, keys_values, grad_out, send_tiles, recv_slot, tile_seq):
    n_replicas = lax.axis_size("dp")
    replica = lax.axis_index("dp")
    tile_count, tile_rows, row_width = queries.shape
    sliver = keys_values.shape[1]
    slot_cap = send_tiles.shape[2]
    slots = n_replicas * slot_cap
    pairs = tile_count // PAIR
    my_send = send_tiles[0]
    outgoing = my_send.T
    my_recv = lax.dynamic_index_in_dim(recv_slot, replica, 0, keepdims=False)
    place = lax.axis_index("z").astype(jnp.int32).reshape(1)
    traveling = jax.ShapeDtypeStruct(
        (n_replicas, 2, slot_cap, 2, 2, sliver, HD), keys_values.dtype
    )
    half_shape = jax.ShapeDtypeStruct((2, 2, pairs, PAIR * sliver, HD), keys_values.dtype)

    def over_plane(values):
        return lax.all_to_all(
            values.reshape((2 * n_replicas,) + values.shape[2:]),
            PLANE, split_axis=0, concat_axis=0, tiled=True,
        ).reshape(values.shape)

    kv_blocks = keys_values.reshape(tile_count, sliver, 2 * KV, HD).transpose(0, 2, 1, 3)
    kv_arrived = over_plane(
        local_call(kv_pack_kernel, "kv_pack", [outgoing], [kv_blocks], traveling)
    )
    own, other = local_call(
        kv_unpack_kernel, "kv_unpack", [my_recv, place], [kv_arrived], (half_shape, half_shape)
    )
    qg_packed = pack(outgoing, queries, grad_out)
    qg_arrived = lax.all_to_all(
        qg_packed.reshape(n_replicas, slot_cap, 2, tile_rows, row_width),
        "dp", split_axis=0, concat_axis=0, tiled=True,
    ).reshape(slots, 2, tile_rows, row_width)
    far = jnp.stack(
        [far_swap(other, MIRROR), far_swap(own, ACROSS), far_swap(other, MIRROR ^ ACROSS)]
    )
    own_chunks = near_gather(own[None])
    far, own_chunks, qg_arrived = lax.optimization_barrier((far, own_chunks, qg_arrived))
    chunks = own_chunks + near_gather(far)

    seq = tile_seq[0]
    start = jnp.sum((seq[None, :] < seq[:, None]).astype(jnp.int32), axis=1)
    query_back, *terms = attention(my_recv, start, place, qg_arrived, chunks)
    query_returned = lax.all_to_all(
        query_back.reshape(n_replicas, slot_cap, tile_rows, row_width),
        "dp", split_axis=0, concat_axis=0, tiled=True,
    )
    across_terms = near_terms(terms[NEAR:])
    own_terms, across_terms = lax.optimization_barrier((terms[:NEAR], across_terms))
    arrived = far_swap(total(across_terms).astype(jnp.bfloat16), ACROSS)
    base = lax.optimization_barrier(total([arrived, own_terms[0]]))
    summed = total([base] + near_terms(own_terms)[1:]).astype(jnp.bfloat16)
    swapped = [summed[0], far_swap(summed[1], MIRROR)]
    swapped, query_returned = lax.optimization_barrier((swapped, query_returned))
    kv_returned = over_plane(
        local_call(kv_back_kernel, "kv_back", [my_recv, place], swapped, traveling)
    )

    flat_slots = jnp.arange(slots)
    own_slots = replica * slot_cap + jnp.arange(slot_cap)
    slot_used = jnp.any(recv_slot[:, None, :] == own_slots[None, :, None], axis=2)
    matched = slot_used[:, :, None] & (my_send[:, :, None] == jnp.arange(tile_count)[None, None, :])
    anchor = jnp.sum(
        jnp.where(matched, flat_slots.reshape(n_replicas, slot_cap)[:, :, None], 0), axis=(0, 1)
    )
    grad_queries = query_returned.reshape(slots, tile_rows, row_width)[anchor]
    kv_final = local_call(
        kv_final_kernel, "kv_final", [anchor], [kv_returned],
        jax.ShapeDtypeStruct(kv_blocks.shape, keys_values.dtype),
    )
    grad_keys_values = kv_final.transpose(0, 2, 1, 3).reshape(keys_values.shape)
    return (grad_queries, grad_keys_values)


def solution(mesh):
    fine = Mesh(mesh.devices.reshape(mesh.devices.shape[0], 2, 16), ("dp", "xh", "z"))
    tensor = ("xh", "z")
    in_specs = (
        P("dp", None, tensor),
        P("dp", tensor, None),
        P("dp", None, tensor),
        P("dp", None, None),
        P(),
        P("dp", None),
    )
    out_specs = (P("dp", None, tensor), P("dp", tensor, None))
    return jax.shard_map(
        on_device, mesh=fine, in_specs=in_specs, out_specs=out_specs, check_vma=False
    )
```

```python
import functools

import jax
import jax.numpy as jnp
from jax import lax
from jax.experimental import pallas as pl
from jax.experimental.pallas import tpu as pltpu
from jax.sharding import Mesh
from jax.sharding import PartitionSpec as P

HD = 128
KV = 4
PAIR = 2
SCALING = HD ** (-0.5)
LOG2E = 1.4426950408889634
PLANE = ("dp", "xh")
MIRROR = 12
ACROSS = 6
NEAR = 4


def matmul(a, b, contract):
    return lax.dot_general(a, b, (contract, ((), ())), preferred_element_type=jnp.float32)


def pack_kernel(index_ref, q_ref, g_ref, out_ref):
    def body(slot, _):
        tile = index_ref[slot & 1, slot >> 1]
        out_ref[slot, 0] = q_ref[tile]
        out_ref[slot, 1] = g_ref[tile]
        return 0

    lax.fori_loop(0, out_ref.shape[0], body, 0, unroll=2)


def pack(index, queries, grad_out):
    slots = index.size
    return pl.pallas_call(
        pack_kernel,
        out_shape=jax.ShapeDtypeStruct((slots, 2) + queries.shape[1:], queries.dtype),
        in_specs=[
            pl.BlockSpec(memory_space=pltpu.SMEM),
            pl.BlockSpec(memory_space=pltpu.VMEM),
            pl.BlockSpec(memory_space=pltpu.VMEM),
        ],
        out_specs=pl.BlockSpec(memory_space=pltpu.VMEM),
        compiler_params=pltpu.CompilerParams(vmem_limit_bytes=24 * 2**20),
        name="pack_rows",
    )(index, queries, grad_out)


def attention_kernel(
    recv_ref, start_ref, place_ref, qg_ref, *refs
):
    kv_refs, dq_ref, dkv_refs = refs[: 2 * NEAR], refs[2 * NEAR], refs[2 * NEAR + 1 : 4 * NEAR + 1]
    k_all, kt_all, v_all, dk_all, dv_all, *rest = refs[4 * NEAR + 1 :]
    scores, dprobs, diagonal_scores, diagonal_dprobs, stats, dqt = rest
    blocks = k_all.shape[0]
    width = k_all.shape[1]
    tile_rows = width // PAIR
    part = width // NEAR
    factor = SCALING * LOG2E

    def rows_of(slot, first_part):
        begin = (slot % NEAR) * part
        if slot < NEAR:
            return slice(begin, begin + first_part)
        return slice(begin + first_part, begin + part)

    def stage(block, _):
        for slot, ref in enumerate(kv_refs):
            rows = rows_of(slot, part // 4)
            count = rows.stop - rows.start
            key = ref[:, :, 0, block].astype(jnp.float32).reshape(count, HD)
            value = ref[:, :, 1, block].astype(jnp.float32).reshape(count, HD)
            k_all[block, rows] = key.astype(jnp.bfloat16)
            v_all[block, rows] = value.astype(jnp.bfloat16)
        kt_all[block] = k_all[block].astype(jnp.float32).T.astype(jnp.bfloat16)
        return 0

    lax.fori_loop(0, blocks, stage, 0, unroll=4)

    row = lax.broadcasted_iota(jnp.int32, (width, 1), 0)
    holder = (place_ref[0] & 12) | ((place_ref[0] - (row >> 6)) & 3)
    source = holder ^ (((row >> 4) & 1) * MIRROR) ^ (((row >> 5) & 1) * ACROSS)
    key_offset = (
        ((row >> 2) & 1) * tile_rows + ((row >> 3) & 1) * 64 + source * 4 + (row & 3)
    )
    lane = lax.broadcasted_iota(jnp.int32, (1, width), 1)

    def operands(block):
        first = recv_ref[PAIR * block]
        second = recv_ref[PAIR * block + 1]
        query = jnp.concatenate([qg_ref[first, 0], qg_ref[second, 0]], axis=0)
        grad = jnp.concatenate([qg_ref[first, 1], qg_ref[second, 1]], axis=0)
        return query, grad

    def first_row(block):
        low, high = start_ref[PAIR * block], start_ref[PAIR * block + 1]
        return jnp.where(lane < tile_rows, low, high) * tile_rows

    def terms(weights, dprob, key_t, query, grad, inverse, delta):
        probs = weights * inverse
        dscores = (probs * (dprob - delta)).astype(jnp.bfloat16)
        grad_value = matmul(probs.astype(jnp.bfloat16), grad, ((1,), (0,)))
        grad_key = matmul(dscores, query, ((1,), (0,)))
        grad_query = matmul(key_t, dscores, ((1,), (0,)))
        return grad_key, grad_value, grad_query

    def diagonal_products(block, _):
        query, grad = operands(block)
        score = matmul(k_all[block], query, ((1,), (1,)))
        allowed = (key_offset >= first_row(block) - block * width) & (key_offset <= lane)
        score = jnp.where(allowed, score, -jnp.inf)
        diagonal_scores[block] = score
        diagonal_dprobs[block] = matmul(v_all[block], grad, ((1,), (1,)))
        peak = jnp.max(score, axis=0, keepdims=True)
        stats[block, 0] = jnp.broadcast_to(peak, stats.shape[2:])
        dk_all[block] = jnp.zeros_like(dk_all[block])
        dv_all[block] = jnp.zeros_like(dv_all[block])
        dqt[block] = jnp.zeros_like(dqt[block])
        return 0

    lax.fori_loop(0, blocks, diagonal_products, 0, unroll=4)

    def sweep(begin, end, step, state):
        twice = (end - begin) >> 1

        def two(index, state):
            return step(begin + 2 * index + 1, step(begin + 2 * index, state))

        state = lax.fori_loop(0, twice, two, state)
        return lax.fori_loop(begin + 2 * twice, end, step, state)

    def query_block(block, _):
        query, grad = operands(block)
        row_start = first_row(block)
        lowest = start_ref[PAIR * block] // PAIR

        def products(other, peak):
            score = matmul(k_all[other], query, ((1,), (1,)))
            score = jnp.where(key_offset >= row_start - other * width, score, -jnp.inf)
            scores[other] = score
            dprobs[other] = matmul(v_all[other], grad, ((1,), (1,)))
            return jnp.maximum(peak, jnp.max(score, axis=0, keepdims=True))

        peak = sweep(lowest, block, products, stats[block, 0][:1])
        shift = peak * factor

        def sums(other, totals):
            weights = jnp.exp2(scores[other] * factor - shift)
            scores[other] = weights
            return (
                totals[0] + jnp.sum(weights, axis=0, keepdims=True),
                totals[1] + jnp.sum(weights * dprobs[other], axis=0, keepdims=True),
            )

        weights = jnp.exp2(diagonal_scores[block] * factor - shift)
        diagonal_scores[block] = weights
        totals = (
            jnp.sum(weights, axis=0, keepdims=True),
            jnp.sum(weights * diagonal_dprobs[block], axis=0, keepdims=True),
        )
        total, weighted = sweep(lowest, block, sums, totals)
        inverse = 1.0 / total
        delta = weighted * inverse
        stats[block, 0] = jnp.broadcast_to(inverse, stats.shape[2:])
        stats[block, 1] = jnp.broadcast_to(delta, stats.shape[2:])

        def earlier(other, _):
            grad_key, grad_value, grad_query = terms(
                scores[other], dprobs[other], kt_all[other], query, grad, inverse, delta
            )
            dk_all[other] += grad_key
            dv_all[other] += grad_value
            dqt[block] += grad_query
            return 0

        sweep(lowest, block, earlier, 0)
        return 0

    lax.fori_loop(0, blocks, query_block, 0)

    def diagonal_terms(block, _):
        query, grad = operands(block)
        grad_key, grad_value, grad_query = terms(
            diagonal_scores[block], diagonal_dprobs[block], kt_all[block], query, grad,
            stats[block, 0][:1], stats[block, 1][:1],
        )
        dk_all[block] += grad_key
        dv_all[block] += grad_value
        result = ((dqt[block] + grad_query) * SCALING).T.astype(jnp.bfloat16)
        dq_ref[recv_ref[PAIR * block]] = result[:tile_rows]
        dq_ref[recv_ref[PAIR * block + 1]] = result[tile_rows:]
        return 0

    lax.fori_loop(0, blocks, diagonal_terms, 0, unroll=4)

    def unstage(block, _):
        for slot, ref in enumerate(dkv_refs):
            rows = rows_of(slot, part // 2)
            shape = ref.shape[:2] + ref.shape[4:]
            ref[:, :, 0, block] = (dk_all[block, rows] * SCALING).reshape(shape).astype(jnp.bfloat16)
            ref[:, :, 1, block] = dv_all[block, rows].reshape(shape).astype(jnp.bfloat16)
        return 0

    lax.fori_loop(0, blocks, unstage, 0, unroll=4)


def attention(my_recv, start, place, qg, chunks):
    slots, _, tile_rows, _ = qg.shape
    blocks = my_recv.shape[0] // PAIR
    width = PAIR * tile_rows
    vmem = pl.BlockSpec(memory_space=pltpu.VMEM)
    smem = pl.BlockSpec(memory_space=pltpu.SMEM)
    return pl.pallas_call(
        attention_kernel,
        out_shape=(jax.ShapeDtypeStruct((slots, tile_rows, HD), jnp.bfloat16),)
        + (jax.ShapeDtypeStruct((2,) + chunks[0].shape[1:], jnp.bfloat16),) * (2 * NEAR),
        in_specs=[smem] * 3 + [vmem] * (1 + 2 * NEAR),
        out_specs=(vmem,) * (1 + 2 * NEAR),
        scratch_shapes=[
            pltpu.VMEM((blocks, width, HD), jnp.bfloat16),
            pltpu.VMEM((blocks, HD, width), jnp.bfloat16),
            pltpu.VMEM((blocks, width, HD), jnp.bfloat16),
            pltpu.VMEM((blocks, width, HD), jnp.float32),
            pltpu.VMEM((blocks, width, HD), jnp.float32),
            pltpu.VMEM((blocks, width, width), jnp.float32),
            pltpu.VMEM((blocks, width, width), jnp.float32),
            pltpu.VMEM((blocks, width, width), jnp.float32),
            pltpu.VMEM((blocks, width, width), jnp.float32),
            pltpu.VMEM((blocks, 2, 8, width), jnp.float32),
            pltpu.VMEM((blocks, HD, width), jnp.float32),
        ],
        compiler_params=pltpu.CompilerParams(vmem_limit_bytes=24 * 2**20),
        cost_estimate=pl.CostEstimate(
            flops=2 * 10**9, bytes_accessed=6 * 2**20, transcendentals=2 * 10**6
        ),
        name="attention_backward",
    )(my_recv, start, place, qg, *chunks)


def kv_pack_kernel(index_ref, kv_ref, out_ref):
    def body(slot, _):
        tile = index_ref[slot & 1, slot >> 1]
        piece = kv_ref[tile].reshape((2, 2, 2) + kv_ref.shape[2:])
        for half in range(2):
            out_ref[slot >> 1, half, slot & 1] = piece[:, half]
        return 0

    lax.fori_loop(0, 2 * index_ref.shape[1], body, 0, unroll=4)


def kv_unpack_kernel(recv_ref, place_ref, kv_ref, own_ref, other_ref):
    head = place_ref[0] >> 3

    def body(pair, _):
        low = recv_ref[PAIR * pair]
        high = recv_ref[PAIR * pair + 1]
        for half in range(2):
            for kind in range(2):
                for ref, which in ((own_ref, head), (other_ref, 1 - head)):
                    rows = [
                        kv_ref[slot >> 1, half, slot & 1, kind, which].astype(jnp.float32)
                        for slot in (low, high)
                    ]
                    ref[half, kind, pair] = jnp.concatenate(rows, axis=0).astype(jnp.bfloat16)
        return 0

    lax.fori_loop(0, recv_ref.shape[0] // PAIR, body, 0, unroll=4)


def kv_back_kernel(recv_ref, place_ref, own_ref, other_ref, out_ref):
    head = place_ref[0] >> 3
    sliver = out_ref.shape[-2]

    def body(pair, _):
        slots = (recv_ref[PAIR * pair], recv_ref[PAIR * pair + 1])
        for half in range(2):
            for kind in range(2):
                for ref, which in ((own_ref, head), (other_ref, 1 - head)):
                    total = ref[half, kind, pair].astype(jnp.float32)
                    for order, slot in enumerate(slots):
                        rows = total[order * sliver : (order + 1) * sliver]
                        out_ref[slot >> 1, half, slot & 1, kind, which] = rows.astype(jnp.bfloat16)
        return 0

    lax.fori_loop(0, recv_ref.shape[0] // PAIR, body, 0, unroll=4)


def kv_final_kernel(anchor_ref, kv_ref, out_ref):
    def body(tile, _):
        slot = anchor_ref[tile]
        piece = kv_ref[slot >> 1, :, slot & 1]
        for half in range(2):
            for kind in range(2):
                for head in range(2):
                    out_ref[tile, kind * 4 + half * 2 + head] = piece[half, kind, head]
        return 0

    lax.fori_loop(0, anchor_ref.shape[0], body, 0, unroll=4)


def local_call(kernel, name, scalars, arrays, out_shape):
    vmem = pl.BlockSpec(memory_space=pltpu.VMEM)
    smem = pl.BlockSpec(memory_space=pltpu.SMEM)
    return pl.pallas_call(
        kernel,
        out_shape=out_shape,
        in_specs=[smem] * len(scalars) + [vmem] * len(arrays),
        out_specs=jax.tree.map(lambda _: vmem, out_shape),
        compiler_params=pltpu.CompilerParams(vmem_limit_bytes=16 * 2**20),
        name=name,
    )(*scalars, *arrays)


def far_swap(values, flip):
    return lax.ppermute(values, "z", [(place, place ^ flip) for place in range(16)])


def near_shift(values, step):
    pairs = [(place, (place & 12) | ((place + step) & 3)) for place in range(16)]
    return lax.ppermute(values, "z", pairs)


def near_gather(values):
    return [values] + [near_shift(values, step) for step in range(1, NEAR)]


def near_terms(terms):
    return [terms[0]] + [near_shift(terms[step], -step) for step in range(1, NEAR)]


def total(terms):
    return sum(term.astype(jnp.float32) for term in terms)


def on_device(queries, keys_values, grad_out, send_tiles, recv_slot, tile_seq):
    n_replicas = lax.axis_size("dp")
    replica = lax.axis_index("dp")
    tile_count, tile_rows, row_width = queries.shape
    sliver = keys_values.shape[1]
    slot_cap = send_tiles.shape[2]
    slots = n_replicas * slot_cap
    pairs = tile_count // PAIR
    my_send = send_tiles[0]
    outgoing = my_send.T
    my_recv = lax.dynamic_index_in_dim(recv_slot, replica, 0, keepdims=False)
    place = lax.axis_index("z").astype(jnp.int32).reshape(1)
    traveling = jax.ShapeDtypeStruct(
        (n_replicas, 2, slot_cap, 2, 2, sliver, HD), keys_values.dtype
    )
    half_shape = jax.ShapeDtypeStruct((2, 2, pairs, PAIR * sliver, HD), keys_values.dtype)

    def over_plane(values):
        return lax.all_to_all(
            values.reshape((2 * n_replicas,) + values.shape[2:]),
            PLANE, split_axis=0, concat_axis=0, tiled=True,
        ).reshape(values.shape)

    kv_blocks = keys_values.reshape(tile_count, sliver, 2 * KV, HD).transpose(0, 2, 1, 3)
    kv_arrived = over_plane(
        local_call(kv_pack_kernel, "kv_pack", [outgoing], [kv_blocks], traveling)
    )
    own, other = local_call(
        kv_unpack_kernel, "kv_unpack", [my_recv, place], [kv_arrived], (half_shape, half_shape)
    )
    qg_packed = pack(outgoing, queries, grad_out)
    qg_arrived = lax.all_to_all(
        qg_packed.reshape(n_replicas, slot_cap, 2, tile_rows, row_width),
        "dp", split_axis=0, concat_axis=0, tiled=True,
    ).reshape(slots, 2, tile_rows, row_width)
    far = jnp.stack(
        [far_swap(other, MIRROR), far_swap(own, ACROSS), far_swap(other, MIRROR ^ ACROSS)]
    )
    own_chunks = near_gather(own[None])
    far, own_chunks, qg_arrived = lax.optimization_barrier((far, own_chunks, qg_arrived))
    chunks = own_chunks + near_gather(far)

    seq = tile_seq[0]
    start = jnp.sum((seq[None, :] < seq[:, None]).astype(jnp.int32), axis=1)
    query_back, *terms = attention(my_recv, start, place, qg_arrived, chunks)
    query_returned = lax.all_to_all(
        query_back.reshape(n_replicas, slot_cap, tile_rows, row_width),
        "dp", split_axis=0, concat_axis=0, tiled=True,
    )
    across_terms = near_terms(terms[NEAR:])
    own_terms, across_terms = lax.optimization_barrier((terms[:NEAR], across_terms))
    arrived = far_swap(total(across_terms).astype(jnp.bfloat16), ACROSS)
    base = lax.optimization_barrier(total([arrived, own_terms[0]]))
    summed = total([base] + near_terms(own_terms)[1:]).astype(jnp.bfloat16)
    swapped = [summed[0], far_swap(summed[1], MIRROR)]
    swapped, query_returned = lax.optimization_barrier((swapped, query_returned))
    kv_returned = over_plane(
        local_call(kv_back_kernel, "kv_back", [my_recv, place], swapped, traveling)
    )

    flat_slots = jnp.arange(slots)
    own_slots = replica * slot_cap + jnp.arange(slot_cap)
    slot_used = jnp.any(recv_slot[:, None, :] == own_slots[None, :, None], axis=2)
    matched = slot_used[:, :, None] & (my_send[:, :, None] == jnp.arange(tile_count)[None, None, :])
    anchor = jnp.sum(
        jnp.where(matched, flat_slots.reshape(n_replicas, slot_cap)[:, :, None], 0), axis=(0, 1)
    )
    grad_queries = query_returned.reshape(slots, tile_rows, row_width)[anchor]
    kv_final = local_call(
        kv_final_kernel, "kv_final", [anchor], [kv_returned],
        jax.ShapeDtypeStruct(kv_blocks.shape, keys_values.dtype),
    )
    grad_keys_values = kv_final.transpose(0, 2, 1, 3).reshape(keys_values.shape)
    return (grad_queries, grad_keys_values)


def solution(mesh):
    fine = Mesh(mesh.devices.reshape(mesh.devices.shape[0], 2, 16), ("dp", "xh", "z"))
    tensor = ("xh", "z")
    in_specs = (
        P("dp", None, tensor),
        P("dp", tensor, None),
        P("dp", None, tensor),
        P("dp", None, None),
        P(),
        P("dp", None),
    )
    out_specs = (P("dp", None, tensor), P("dp", tensor, None))
    return jax.shard_map(
        on_device, mesh=fine, in_specs=in_specs, out_specs=out_specs, check_vma=False
    )
```

```python
import functools

import jax
import jax.numpy as jnp
from jax import lax
from jax.experimental import pallas as pl
from jax.experimental.pallas import tpu as pltpu
from jax.sharding import Mesh
from jax.sharding import PartitionSpec as P

HD = 128
KV = 4
PAIR = 2
SCALING = HD ** (-0.5)
LOG2E = 1.4426950408889634
PLANE = ("dp", "xh")
MIRROR = 12
ACROSS = 6
NEAR = 4


def matmul(a, b, contract):
    return lax.dot_general(a, b, (contract, ((), ())), preferred_element_type=jnp.float32)


def pack_kernel(index_ref, q_ref, g_ref, out_ref):
    def body(slot, _):
        tile = index_ref[slot & 1, slot >> 1]
        out_ref[slot, 0] = q_ref[tile]
        out_ref[slot, 1] = g_ref[tile]
        return 0

    lax.fori_loop(0, out_ref.shape[0], body, 0, unroll=2)


def pack(index, queries, grad_out):
    slots = index.size
    return pl.pallas_call(
        pack_kernel,
        out_shape=jax.ShapeDtypeStruct((slots, 2) + queries.shape[1:], queries.dtype),
        in_specs=[
            pl.BlockSpec(memory_space=pltpu.SMEM),
            pl.BlockSpec(memory_space=pltpu.VMEM),
            pl.BlockSpec(memory_space=pltpu.VMEM),
        ],
        out_specs=pl.BlockSpec(memory_space=pltpu.VMEM),
        compiler_params=pltpu.CompilerParams(vmem_limit_bytes=24 * 2**20),
        name="pack_rows",
    )(index, queries, grad_out)


def attention_kernel(
    recv_ref, start_ref, place_ref, qg_ref, *refs
):
    kv_refs, dq_ref, dkv_refs = refs[: 2 * NEAR], refs[2 * NEAR], refs[2 * NEAR + 1 : 4 * NEAR + 1]
    k_all, kt_all, v_all, dk_all, dv_all, *rest = refs[4 * NEAR + 1 :]
    scores, dprobs, diagonal_scores, diagonal_dprobs, stats, dqt = rest
    blocks = k_all.shape[0]
    width = k_all.shape[1]
    tile_rows = width // PAIR
    part = width // NEAR
    factor = SCALING * LOG2E

    def rows_of(slot, first_part):
        begin = (slot % NEAR) * part
        if slot < NEAR:
            return slice(begin, begin + first_part)
        return slice(begin + first_part, begin + part)

    def stage(block, _):
        for slot, ref in enumerate(kv_refs):
            rows = rows_of(slot, part // 4)
            count = rows.stop - rows.start
            key = ref[:, :, 0, block].astype(jnp.float32).reshape(count, HD)
            value = ref[:, :, 1, block].astype(jnp.float32).reshape(count, HD)
            k_all[block, rows] = key.astype(jnp.bfloat16)
            v_all[block, rows] = value.astype(jnp.bfloat16)
        kt_all[block] = k_all[block].astype(jnp.float32).T.astype(jnp.bfloat16)
        return 0

    lax.fori_loop(0, blocks, stage, 0, unroll=4)

    row = lax.broadcasted_iota(jnp.int32, (width, 1), 0)
    holder = (place_ref[0] & 12) | ((place_ref[0] - (row >> 6)) & 3)
    source = holder ^ (((row >> 4) & 1) * MIRROR) ^ (((row >> 5) & 1) * ACROSS)
    key_offset = (
        ((row >> 2) & 1) * tile_rows + ((row >> 3) & 1) * 64 + source * 4 + (row & 3)
    )
    lane = lax.broadcasted_iota(jnp.int32, (1, width), 1)

    def operands(block):
        first = recv_ref[PAIR * block]
        second = recv_ref[PAIR * block + 1]
        query = jnp.concatenate([qg_ref[first, 0], qg_ref[second, 0]], axis=0)
        grad = jnp.concatenate([qg_ref[first, 1], qg_ref[second, 1]], axis=0)
        return query, grad

    def first_row(block):
        low, high = start_ref[PAIR * block], start_ref[PAIR * block + 1]
        return jnp.where(lane < tile_rows, low, high) * tile_rows

    def terms(weights, dprob, key_t, query, grad, inverse, delta):
        probs = weights * inverse
        dscores = (probs * (dprob - delta)).astype(jnp.bfloat16)
        grad_value = matmul(probs.astype(jnp.bfloat16), grad, ((1,), (0,)))
        grad_key = matmul(dscores, query, ((1,), (0,)))
        grad_query = matmul(key_t, dscores, ((1,), (0,)))
        return grad_key, grad_value, grad_query

    def diagonal_products(block, _):
        query, grad = operands(block)
        score = matmul(k_all[block], query, ((1,), (1,)))
        allowed = (key_offset >= first_row(block) - block * width) & (key_offset <= lane)
        score = jnp.where(allowed, score, -jnp.inf)
        diagonal_scores[block] = score
        diagonal_dprobs[block] = matmul(v_all[block], grad, ((1,), (1,)))
        peak = jnp.max(score, axis=0, keepdims=True)
        stats[block, 0] = jnp.broadcast_to(peak, stats.shape[2:])
        dk_all[block] = jnp.zeros_like(dk_all[block])
        dv_all[block] = jnp.zeros_like(dv_all[block])
        dqt[block] = jnp.zeros_like(dqt[block])
        return 0

    lax.fori_loop(0, blocks, diagonal_products, 0, unroll=4)

    def sweep(begin, end, step, state):
        twice = (end - begin) >> 1

        def two(index, state):
            return step(begin + 2 * index + 1, step(begin + 2 * index, state))

        state = lax.fori_loop(0, twice, two, state)
        return lax.fori_loop(begin + 2 * twice, end, step, state)

    def query_block(block, _):
        query, grad = operands(block)
        row_start = first_row(block)
        lowest = start_ref[PAIR * block] // PAIR

        def products(other, peak):
            score = matmul(k_all[other], query, ((1,), (1,)))
            score = jnp.where(key_offset >= row_start - other * width, score, -jnp.inf)
            scores[other] = score
            dprobs[other] = matmul(v_all[other], grad, ((1,), (1,)))
            return jnp.maximum(peak, jnp.max(score, axis=0, keepdims=True))

        peak = sweep(lowest, block, products, stats[block, 0][:1])
        shift = peak * factor

        def sums(other, totals):
            weights = jnp.exp2(scores[other] * factor - shift)
            scores[other] = weights
            return (
                totals[0] + jnp.sum(weights, axis=0, keepdims=True),
                totals[1] + jnp.sum(weights * dprobs[other], axis=0, keepdims=True),
            )

        weights = jnp.exp2(diagonal_scores[block] * factor - shift)
        diagonal_scores[block] = weights
        totals = (
            jnp.sum(weights, axis=0, keepdims=True),
            jnp.sum(weights * diagonal_dprobs[block], axis=0, keepdims=True),
        )
        total, weighted = sweep(lowest, block, sums, totals)
        inverse = 1.0 / total
        delta = weighted * inverse
        stats[block, 0] = jnp.broadcast_to(inverse, stats.shape[2:])
        stats[block, 1] = jnp.broadcast_to(delta, stats.shape[2:])

        def earlier(other, _):
            grad_key, grad_value, grad_query = terms(
                scores[other], dprobs[other], kt_all[other], query, grad, inverse, delta
            )
            dk_all[other] += grad_key
            dv_all[other] += grad_value
            dqt[block] += grad_query
            return 0

        sweep(lowest, block, earlier, 0)
        return 0

    lax.fori_loop(0, blocks, query_block, 0)

    def diagonal_terms(block, _):
        query, grad = operands(block)
        grad_key, grad_value, grad_query = terms(
            diagonal_scores[block], diagonal_dprobs[block], kt_all[block], query, grad,
            stats[block, 0][:1], stats[block, 1][:1],
        )
        dk_all[block] += grad_key
        dv_all[block] += grad_value
        result = ((dqt[block] + grad_query) * SCALING).T.astype(jnp.bfloat16)
        dq_ref[recv_ref[PAIR * block]] = result[:tile_rows]
        dq_ref[recv_ref[PAIR * block + 1]] = result[tile_rows:]
        return 0

    lax.fori_loop(0, blocks, diagonal_terms, 0, unroll=4)

    def unstage(block, _):
        for slot, ref in enumerate(dkv_refs):
            rows = rows_of(slot, part // 4)
            shape = ref.shape[:2] + ref.shape[4:]
            ref[:, :, 0, block] = (dk_all[block, rows] * SCALING).reshape(shape).astype(jnp.bfloat16)
            ref[:, :, 1, block] = dv_all[block, rows].reshape(shape).astype(jnp.bfloat16)
        return 0

    lax.fori_loop(0, blocks, unstage, 0, unroll=4)


def attention(my_recv, start, place, qg, chunks):
    slots, _, tile_rows, _ = qg.shape
    blocks = my_recv.shape[0] // PAIR
    width = PAIR * tile_rows
    vmem = pl.BlockSpec(memory_space=pltpu.VMEM)
    smem = pl.BlockSpec(memory_space=pltpu.SMEM)
    return pl.pallas_call(
        attention_kernel,
        out_shape=(jax.ShapeDtypeStruct((slots, tile_rows, HD), jnp.bfloat16),)
        + tuple(jax.ShapeDtypeStruct(chunk.shape, jnp.bfloat16) for chunk in chunks),
        in_specs=[smem] * 3 + [vmem] * (1 + 2 * NEAR),
        out_specs=(vmem,) * (1 + 2 * NEAR),
        scratch_shapes=[
            pltpu.VMEM((blocks, width, HD), jnp.bfloat16),
            pltpu.VMEM((blocks, HD, width), jnp.bfloat16),
            pltpu.VMEM((blocks, width, HD), jnp.bfloat16),
            pltpu.VMEM((blocks, width, HD), jnp.float32),
            pltpu.VMEM((blocks, width, HD), jnp.float32),
            pltpu.VMEM((blocks, width, width), jnp.float32),
            pltpu.VMEM((blocks, width, width), jnp.float32),
            pltpu.VMEM((blocks, width, width), jnp.float32),
            pltpu.VMEM((blocks, width, width), jnp.float32),
            pltpu.VMEM((blocks, 2, 8, width), jnp.float32),
            pltpu.VMEM((blocks, HD, width), jnp.float32),
        ],
        compiler_params=pltpu.CompilerParams(vmem_limit_bytes=24 * 2**20),
        cost_estimate=pl.CostEstimate(
            flops=2 * 10**9, bytes_accessed=6 * 2**20, transcendentals=2 * 10**6
        ),
        name="attention_backward",
    )(my_recv, start, place, qg, *chunks)


def kv_pack_kernel(index_ref, kv_ref, out_ref):
    def body(slot, _):
        tile = index_ref[slot & 1, slot >> 1]
        piece = kv_ref[tile].reshape((2, 2, 2) + kv_ref.shape[2:])
        for half in range(2):
            out_ref[slot >> 1, half, slot & 1] = piece[:, half]
        return 0

    lax.fori_loop(0, 2 * index_ref.shape[1], body, 0, unroll=4)


def kv_unpack_kernel(recv_ref, place_ref, kv_ref, own_ref, other_ref):
    head = place_ref[0] >> 3

    def body(pair, _):
        low = recv_ref[PAIR * pair]
        high = recv_ref[PAIR * pair + 1]
        for half in range(2):
            for kind in range(2):
                for ref, which in ((own_ref, head), (other_ref, 1 - head)):
                    rows = [
                        kv_ref[slot >> 1, half, slot & 1, kind, which].astype(jnp.float32)
                        for slot in (low, high)
                    ]
                    ref[half, kind, pair] = jnp.concatenate(rows, axis=0).astype(jnp.bfloat16)
        return 0

    lax.fori_loop(0, recv_ref.shape[0] // PAIR, body, 0, unroll=4)


def kv_back_kernel(recv_ref, place_ref, own_ref, other_ref, out_ref):
    head = place_ref[0] >> 3
    sliver = out_ref.shape[-2]

    def body(pair, _):
        slots = (recv_ref[PAIR * pair], recv_ref[PAIR * pair + 1])
        for half in range(2):
            for kind in range(2):
                for ref, which in ((own_ref, head), (other_ref, 1 - head)):
                    total = ref[half, kind, pair].astype(jnp.float32)
                    for order, slot in enumerate(slots):
                        rows = total[order * sliver : (order + 1) * sliver]
                        out_ref[slot >> 1, half, slot & 1, kind, which] = rows.astype(jnp.bfloat16)
        return 0

    lax.fori_loop(0, recv_ref.shape[0] // PAIR, body, 0, unroll=4)


def kv_final_kernel(anchor_ref, kv_ref, out_ref):
    def body(tile, _):
        slot = anchor_ref[tile]
        piece = kv_ref[slot >> 1, :, slot & 1]
        for half in range(2):
            for kind in range(2):
                for head in range(2):
                    out_ref[tile, kind * 4 + half * 2 + head] = piece[half, kind, head]
        return 0

    lax.fori_loop(0, anchor_ref.shape[0], body, 0, unroll=4)


def local_call(kernel, name, scalars, arrays, out_shape):
    vmem = pl.BlockSpec(memory_space=pltpu.VMEM)
    smem = pl.BlockSpec(memory_space=pltpu.SMEM)
    return pl.pallas_call(
        kernel,
        out_shape=out_shape,
        in_specs=[smem] * len(scalars) + [vmem] * len(arrays),
        out_specs=jax.tree.map(lambda _: vmem, out_shape),
        compiler_params=pltpu.CompilerParams(vmem_limit_bytes=16 * 2**20),
        name=name,
    )(*scalars, *arrays)


def far_swap(values, flip):
    return lax.ppermute(values, "z", [(place, place ^ flip) for place in range(16)])


def near_shift(values, step):
    pairs = [(place, (place & 12) | ((place + step) & 3)) for place in range(16)]
    return lax.ppermute(values, "z", pairs)


def near_gather(values):
    return [values] + [near_shift(values, step) for step in range(1, NEAR)]


def near_terms(terms):
    return [terms[0]] + [near_shift(terms[step], -step) for step in range(1, NEAR)]


def total(terms):
    return sum(term.astype(jnp.float32) for term in terms)


def on_device(queries, keys_values, grad_out, send_tiles, recv_slot, tile_seq):
    n_replicas = lax.axis_size("dp")
    replica = lax.axis_index("dp")
    tile_count, tile_rows, row_width = queries.shape
    sliver = keys_values.shape[1]
    slot_cap = send_tiles.shape[2]
    slots = n_replicas * slot_cap
    pairs = tile_count // PAIR
    my_send = send_tiles[0]
    outgoing = my_send.T
    my_recv = lax.dynamic_index_in_dim(recv_slot, replica, 0, keepdims=False)
    place = lax.axis_index("z").astype(jnp.int32).reshape(1)
    traveling = jax.ShapeDtypeStruct(
        (n_replicas, 2, slot_cap, 2, 2, sliver, HD), keys_values.dtype
    )
    half_shape = jax.ShapeDtypeStruct((2, 2, pairs, PAIR * sliver, HD), keys_values.dtype)

    def over_plane(values):
        return lax.all_to_all(
            values.reshape((2 * n_replicas,) + values.shape[2:]),
            PLANE, split_axis=0, concat_axis=0, tiled=True,
        ).reshape(values.shape)

    kv_blocks = keys_values.reshape(tile_count, sliver, 2 * KV, HD).transpose(0, 2, 1, 3)
    kv_arrived = over_plane(
        local_call(kv_pack_kernel, "kv_pack", [outgoing], [kv_blocks], traveling)
    )
    own, other = local_call(
        kv_unpack_kernel, "kv_unpack", [my_recv, place], [kv_arrived], (half_shape, half_shape)
    )
    qg_packed = pack(outgoing, queries, grad_out)
    qg_arrived = lax.all_to_all(
        qg_packed.reshape(n_replicas, slot_cap, 2, tile_rows, row_width),
        "dp", split_axis=0, concat_axis=0, tiled=True,
    ).reshape(slots, 2, tile_rows, row_width)
    far = jnp.stack(
        [far_swap(other, MIRROR), far_swap(own, ACROSS), far_swap(other, MIRROR ^ ACROSS)]
    )
    own_chunks = near_gather(own[None])
    far, own_chunks, qg_arrived = lax.optimization_barrier((far, own_chunks, qg_arrived))
    chunks = own_chunks + near_gather(far)

    seq = tile_seq[0]
    start = jnp.sum((seq[None, :] < seq[:, None]).astype(jnp.int32), axis=1)
    query_back, *terms = attention(my_recv, start, place, qg_arrived, chunks)
    query_returned = lax.all_to_all(
        query_back.reshape(n_replicas, slot_cap, tile_rows, row_width),
        "dp", split_axis=0, concat_axis=0, tiled=True,
    )
    far_terms = near_terms(terms[NEAR:])
    own_terms, far_terms = lax.optimization_barrier((terms[:NEAR], far_terms))
    across = total([term[1:] for term in far_terms]).astype(jnp.bfloat16)
    arrived = far_swap(across, ACROSS)
    crossing = total([term[0] for term in far_terms] + [arrived[1]]).astype(jnp.bfloat16)
    own_sum = total([term[0] for term in near_terms(own_terms)] + [arrived[0]]).astype(jnp.bfloat16)
    swapped = [own_sum, far_swap(crossing, MIRROR)]
    swapped, query_returned = lax.optimization_barrier((swapped, query_returned))
    kv_returned = over_plane(
        local_call(kv_back_kernel, "kv_back", [my_recv, place], swapped, traveling)
    )

    flat_slots = jnp.arange(slots)
    own_slots = replica * slot_cap + jnp.arange(slot_cap)
    slot_used = jnp.any(recv_slot[:, None, :] == own_slots[None, :, None], axis=2)
    matched = slot_used[:, :, None] & (my_send[:, :, None] == jnp.arange(tile_count)[None, None, :])
    anchor = jnp.sum(
        jnp.where(matched, flat_slots.reshape(n_replicas, slot_cap)[:, :, None], 0), axis=(0, 1)
    )
    grad_queries = query_returned.reshape(slots, tile_rows, row_width)[anchor]
    kv_final = local_call(
        kv_final_kernel, "kv_final", [anchor], [kv_returned],
        jax.ShapeDtypeStruct(kv_blocks.shape, keys_values.dtype),
    )
    grad_keys_values = kv_final.transpose(0, 2, 1, 3).reshape(keys_values.shape)
    return (grad_queries, grad_keys_values)


def solution(mesh):
    fine = Mesh(mesh.devices.reshape(mesh.devices.shape[0], 2, 16), ("dp", "xh", "z"))
    tensor = ("xh", "z")
    in_specs = (
        P("dp", None, tensor),
        P("dp", tensor, None),
        P("dp", None, tensor),
        P("dp", None, None),
        P(),
        P("dp", None),
    )
    out_specs = (P("dp", None, tensor), P("dp", tensor, None))
    return jax.shard_map(
        on_device, mesh=fine, in_specs=in_specs, out_specs=out_specs, check_vma=False
    )
```

```python
import functools

import jax
import jax.numpy as jnp
from jax import lax
from jax.experimental import pallas as pl
from jax.experimental.pallas import tpu as pltpu
from jax.sharding import Mesh
from jax.sharding import PartitionSpec as P

HD = 128
KV = 4
PAIR = 2
SCALING = HD ** (-0.5)
LOG2E = 1.4426950408889634
PLANE = ("dp", "xh")
MIRROR = 12
ACROSS = 6
NEAR = 4


def matmul(a, b, contract):
    return lax.dot_general(a, b, (contract, ((), ())), preferred_element_type=jnp.float32)


def pack_kernel(index_ref, q_ref, g_ref, out_ref):
    def body(slot, _):
        tile = index_ref[slot & 1, slot >> 1]
        out_ref[slot, 0] = q_ref[tile]
        out_ref[slot, 1] = g_ref[tile]
        return 0

    lax.fori_loop(0, out_ref.shape[0], body, 0, unroll=2)


def pack(index, queries, grad_out):
    slots = index.size
    return pl.pallas_call(
        pack_kernel,
        out_shape=jax.ShapeDtypeStruct((slots, 2) + queries.shape[1:], queries.dtype),
        in_specs=[
            pl.BlockSpec(memory_space=pltpu.SMEM),
            pl.BlockSpec(memory_space=pltpu.VMEM),
            pl.BlockSpec(memory_space=pltpu.VMEM),
        ],
        out_specs=pl.BlockSpec(memory_space=pltpu.VMEM),
        compiler_params=pltpu.CompilerParams(vmem_limit_bytes=24 * 2**20),
        name="pack_rows",
    )(index, queries, grad_out)


def attention_kernel(
    recv_ref, start_ref, place_ref, qg_ref, *refs
):
    kv_refs, dq_ref, dkv_refs = refs[: 2 * NEAR], refs[2 * NEAR], refs[2 * NEAR + 1 : 4 * NEAR + 1]
    k_all, kt_all, v_all, dk_all, dv_all, *rest = refs[4 * NEAR + 1 :]
    scores, dprobs, diagonal_scores, diagonal_dprobs, stats, dqt = rest
    blocks = k_all.shape[0]
    width = k_all.shape[1]
    tile_rows = width // PAIR
    part = width // NEAR
    factor = SCALING * LOG2E

    def rows_of(slot, first_part):
        begin = (slot % NEAR) * part
        if slot < NEAR:
            return slice(begin, begin + first_part)
        return slice(begin + first_part, begin + part)

    def stage(block, _):
        for slot, ref in enumerate(kv_refs):
            rows = rows_of(slot, part // 4)
            count = rows.stop - rows.start
            key = ref[:, :, 0, block].astype(jnp.float32).reshape(count, HD)
            value = ref[:, :, 1, block].astype(jnp.float32).reshape(count, HD)
            k_all[block, rows] = key.astype(jnp.bfloat16)
            v_all[block, rows] = value.astype(jnp.bfloat16)
        kt_all[block] = k_all[block].astype(jnp.float32).T.astype(jnp.bfloat16)
        return 0

    lax.fori_loop(0, blocks, stage, 0, unroll=4)

    row = lax.broadcasted_iota(jnp.int32, (width, 1), 0)
    holder = (place_ref[0] & 12) | ((place_ref[0] - (row >> 6)) & 3)
    source = holder ^ (((row >> 4) & 1) * MIRROR) ^ (((row >> 5) & 1) * ACROSS)
    key_offset = (
        ((row >> 2) & 1) * tile_rows + ((row >> 3) & 1) * 64 + source * 4 + (row & 3)
    )
    lane = lax.broadcasted_iota(jnp.int32, (1, width), 1)

    def operands(block):
        first = recv_ref[PAIR * block]
        second = recv_ref[PAIR * block + 1]
        query = jnp.concatenate([qg_ref[first, 0], qg_ref[second, 0]], axis=0)
        grad = jnp.concatenate([qg_ref[first, 1], qg_ref[second, 1]], axis=0)
        return query, grad

    def first_row(block):
        low, high = start_ref[PAIR * block], start_ref[PAIR * block + 1]
        return jnp.where(lane < tile_rows, low, high) * tile_rows

    def terms(weights, dprob, key_t, query, grad, inverse, delta):
        probs = weights * inverse
        dscores = (probs * (dprob - delta)).astype(jnp.bfloat16)
        grad_value = matmul(probs.astype(jnp.bfloat16), grad, ((1,), (0,)))
        grad_key = matmul(dscores, query, ((1,), (0,)))
        grad_query = matmul(key_t, dscores, ((1,), (0,)))
        return grad_key, grad_value, grad_query

    def diagonal_products(block, _):
        query, grad = operands(block)
        score = matmul(k_all[block], query, ((1,), (1,)))
        allowed = (key_offset >= first_row(block) - block * width) & (key_offset <= lane)
        score = jnp.where(allowed, score, -jnp.inf)
        diagonal_scores[block] = score
        diagonal_dprobs[block] = matmul(v_all[block], grad, ((1,), (1,)))
        peak = jnp.max(score, axis=0, keepdims=True)
        stats[block, 0] = jnp.broadcast_to(peak, stats.shape[2:])
        dk_all[block] = jnp.zeros_like(dk_all[block])
        dv_all[block] = jnp.zeros_like(dv_all[block])
        dqt[block] = jnp.zeros_like(dqt[block])
        return 0

    lax.fori_loop(0, blocks, diagonal_products, 0, unroll=4)

    def sweep(begin, end, step, state):
        twice = (end - begin) >> 1

        def two(index, state):
            return step(begin + 2 * index + 1, step(begin + 2 * index, state))

        state = lax.fori_loop(0, twice, two, state)
        return lax.fori_loop(begin + 2 * twice, end, step, state)

    def query_block(block, _):
        query, grad = operands(block)
        row_start = first_row(block)
        lowest = start_ref[PAIR * block] // PAIR

        def products(other, peak):
            score = matmul(k_all[other], query, ((1,), (1,)))
            score = jnp.where(key_offset >= row_start - other * width, score, -jnp.inf)
            scores[other] = score
            dprobs[other] = matmul(v_all[other], grad, ((1,), (1,)))
            return jnp.maximum(peak, jnp.max(score, axis=0, keepdims=True))

        peak = sweep(lowest, block, products, stats[block, 0][:1])
        shift = peak * factor

        def sums(other, totals):
            weights = jnp.exp2(scores[other] * factor - shift)
            scores[other] = weights
            return (
                totals[0] + jnp.sum(weights, axis=0, keepdims=True),
                totals[1] + jnp.sum(weights * dprobs[other], axis=0, keepdims=True),
            )

        weights = jnp.exp2(diagonal_scores[block] * factor - shift)
        diagonal_scores[block] = weights
        totals = (
            jnp.sum(weights, axis=0, keepdims=True),
            jnp.sum(weights * diagonal_dprobs[block], axis=0, keepdims=True),
        )
        total, weighted = sweep(lowest, block, sums, totals)
        inverse = 1.0 / total
        delta = weighted * inverse
        stats[block, 0] = jnp.broadcast_to(inverse, stats.shape[2:])
        stats[block, 1] = jnp.broadcast_to(delta, stats.shape[2:])

        def earlier(other, _):
            grad_key, grad_value, grad_query = terms(
                scores[other], dprobs[other], kt_all[other], query, grad, inverse, delta
            )
            dk_all[other] += grad_key
            dv_all[other] += grad_value
            dqt[block] += grad_query
            return 0

        sweep(lowest, block, earlier, 0)
        return 0

    lax.fori_loop(0, blocks, query_block, 0)

    def diagonal_terms(block, _):
        query, grad = operands(block)
        grad_key, grad_value, grad_query = terms(
            diagonal_scores[block], diagonal_dprobs[block], kt_all[block], query, grad,
            stats[block, 0][:1], stats[block, 1][:1],
        )
        dk_all[block] += grad_key
        dv_all[block] += grad_value
        result = ((dqt[block] + grad_query) * SCALING).T.astype(jnp.bfloat16)
        dq_ref[recv_ref[PAIR * block]] = result[:tile_rows]
        dq_ref[recv_ref[PAIR * block + 1]] = result[tile_rows:]
        return 0

    lax.fori_loop(0, blocks, diagonal_terms, 0, unroll=4)

    def unstage(block, _):
        for slot, ref in enumerate(dkv_refs):
            rows = rows_of(slot, part // 4)
            shape = ref.shape[:2] + ref.shape[4:]
            ref[:, :, 0, block] = (dk_all[block, rows] * SCALING).reshape(shape).astype(jnp.bfloat16)
            ref[:, :, 1, block] = dv_all[block, rows].reshape(shape).astype(jnp.bfloat16)
        return 0

    lax.fori_loop(0, blocks, unstage, 0, unroll=4)


def attention(my_recv, start, place, qg, chunks):
    slots, _, tile_rows, _ = qg.shape
    blocks = my_recv.shape[0] // PAIR
    width = PAIR * tile_rows
    vmem = pl.BlockSpec(memory_space=pltpu.VMEM)
    smem = pl.BlockSpec(memory_space=pltpu.SMEM)
    return pl.pallas_call(
        attention_kernel,
        out_shape=(jax.ShapeDtypeStruct((slots, tile_rows, HD), jnp.bfloat16),)
        + tuple(jax.ShapeDtypeStruct(chunk.shape, jnp.bfloat16) for chunk in chunks),
        in_specs=[smem] * 3 + [vmem] * (1 + 2 * NEAR),
        out_specs=(vmem,) * (1 + 2 * NEAR),
        scratch_shapes=[
            pltpu.VMEM((blocks, width, HD), jnp.bfloat16),
            pltpu.VMEM((blocks, HD, width), jnp.bfloat16),
            pltpu.VMEM((blocks, width, HD), jnp.bfloat16),
            pltpu.VMEM((blocks, width, HD), jnp.float32),
            pltpu.VMEM((blocks, width, HD), jnp.float32),
            pltpu.VMEM((blocks, width, width), jnp.float32),
            pltpu.VMEM((blocks, width, width), jnp.float32),
            pltpu.VMEM((blocks, width, width), jnp.float32),
            pltpu.VMEM((blocks, width, width), jnp.float32),
            pltpu.VMEM((blocks, 2, 8, width), jnp.float32),
            pltpu.VMEM((blocks, HD, width), jnp.float32),
        ],
        compiler_params=pltpu.CompilerParams(vmem_limit_bytes=24 * 2**20),
        cost_estimate=pl.CostEstimate(
            flops=2 * 10**9, bytes_accessed=6 * 2**20, transcendentals=2 * 10**6
        ),
        name="attention_backward",
    )(my_recv, start, place, qg, *chunks)


def kv_pack_kernel(index_ref, kv_ref, out_ref):
    def body(slot, _):
        tile = index_ref[slot & 1, slot >> 1]
        piece = kv_ref[tile].reshape((2, 2, 2) + kv_ref.shape[2:])
        for half in range(2):
            out_ref[slot >> 1, half, slot & 1] = piece[:, half]
        return 0

    lax.fori_loop(0, 2 * index_ref.shape[1], body, 0, unroll=4)


def kv_unpack_kernel(recv_ref, place_ref, kv_ref, own_ref, other_ref):
    head = place_ref[0] >> 3

    def body(pair, _):
        low = recv_ref[PAIR * pair]
        high = recv_ref[PAIR * pair + 1]
        for half in range(2):
            for kind in range(2):
                for ref, which in ((own_ref, head), (other_ref, 1 - head)):
                    rows = [
                        kv_ref[slot >> 1, half, slot & 1, kind, which].astype(jnp.float32)
                        for slot in (low, high)
                    ]
                    ref[half, kind, pair] = jnp.concatenate(rows, axis=0).astype(jnp.bfloat16)
        return 0

    lax.fori_loop(0, recv_ref.shape[0] // PAIR, body, 0, unroll=4)


def kv_back_kernel(recv_ref, place_ref, *refs):
    own_refs, (across_ref, other_ref, out_ref) = refs[:NEAR], refs[NEAR:]
    head = place_ref[0] >> 3
    sliver = out_ref.shape[-2]

    def body(pair, _):
        slots = (recv_ref[PAIR * pair], recv_ref[PAIR * pair + 1])
        for half in range(2):
            for kind in range(2):
                own = across_ref[0, half, kind, pair].astype(jnp.float32)
                for ref in own_refs:
                    own += ref[0, half, kind, pair].astype(jnp.float32)
                other = other_ref[half, kind, pair].astype(jnp.float32)
                for total, which in ((own, head), (other, 1 - head)):
                    for order, slot in enumerate(slots):
                        rows = total[order * sliver : (order + 1) * sliver]
                        out_ref[slot >> 1, half, slot & 1, kind, which] = rows.astype(jnp.bfloat16)
        return 0

    lax.fori_loop(0, recv_ref.shape[0] // PAIR, body, 0, unroll=4)


def kv_final_kernel(anchor_ref, kv_ref, out_ref):
    def body(tile, _):
        slot = anchor_ref[tile]
        piece = kv_ref[slot >> 1, :, slot & 1]
        for half in range(2):
            for kind in range(2):
                for head in range(2):
                    out_ref[tile, kind * 4 + half * 2 + head] = piece[half, kind, head]
        return 0

    lax.fori_loop(0, anchor_ref.shape[0], body, 0, unroll=4)


def local_call(kernel, name, scalars, arrays, out_shape):
    vmem = pl.BlockSpec(memory_space=pltpu.VMEM)
    smem = pl.BlockSpec(memory_space=pltpu.SMEM)
    return pl.pallas_call(
        kernel,
        out_shape=out_shape,
        in_specs=[smem] * len(scalars) + [vmem] * len(arrays),
        out_specs=jax.tree.map(lambda _: vmem, out_shape),
        compiler_params=pltpu.CompilerParams(vmem_limit_bytes=16 * 2**20),
        name=name,
    )(*scalars, *arrays)


def far_swap(values, flip):
    return lax.ppermute(values, "z", [(place, place ^ flip) for place in range(16)])


def near_shift(values, step):
    pairs = [(place, (place & 12) | ((place + step) & 3)) for place in range(16)]
    return lax.ppermute(values, "z", pairs)


def near_gather(values):
    return [values] + [near_shift(values, step) for step in range(1, NEAR)]


def near_terms(terms):
    return [terms[0]] + [near_shift(terms[step], -step) for step in range(1, NEAR)]


def total(terms):
    return sum(term.astype(jnp.float32) for term in terms)


def on_device(queries, keys_values, grad_out, send_tiles, recv_slot, tile_seq):
    n_replicas = lax.axis_size("dp")
    replica = lax.axis_index("dp")
    tile_count, tile_rows, row_width = queries.shape
    sliver = keys_values.shape[1]
    slot_cap = send_tiles.shape[2]
    slots = n_replicas * slot_cap
    pairs = tile_count // PAIR
    my_send = send_tiles[0]
    outgoing = my_send.T
    my_recv = lax.dynamic_index_in_dim(recv_slot, replica, 0, keepdims=False)
    place = lax.axis_index("z").astype(jnp.int32).reshape(1)
    traveling = jax.ShapeDtypeStruct(
        (n_replicas, 2, slot_cap, 2, 2, sliver, HD), keys_values.dtype
    )
    half_shape = jax.ShapeDtypeStruct((2, 2, pairs, PAIR * sliver, HD), keys_values.dtype)

    def over_plane(values):
        return lax.all_to_all(
            values.reshape((2 * n_replicas,) + values.shape[2:]),
            PLANE, split_axis=0, concat_axis=0, tiled=True,
        ).reshape(values.shape)

    kv_blocks = keys_values.reshape(tile_count, sliver, 2 * KV, HD).transpose(0, 2, 1, 3)
    kv_arrived = over_plane(
        local_call(kv_pack_kernel, "kv_pack", [outgoing], [kv_blocks], traveling)
    )
    own, other = local_call(
        kv_unpack_kernel, "kv_unpack", [my_recv, place], [kv_arrived], (half_shape, half_shape)
    )
    qg_packed = pack(outgoing, queries, grad_out)
    qg_arrived = lax.all_to_all(
        qg_packed.reshape(n_replicas, slot_cap, 2, tile_rows, row_width),
        "dp", split_axis=0, concat_axis=0, tiled=True,
    ).reshape(slots, 2, tile_rows, row_width)
    far = jnp.stack(
        [far_swap(other, MIRROR), far_swap(own, ACROSS), far_swap(other, MIRROR ^ ACROSS)]
    )
    own_chunks = near_gather(own[None])
    far, own_chunks, qg_arrived = lax.optimization_barrier((far, own_chunks, qg_arrived))
    chunks = own_chunks + near_gather(far)

    seq = tile_seq[0]
    start = jnp.sum((seq[None, :] < seq[:, None]).astype(jnp.int32), axis=1)
    query_back, *terms = attention(my_recv, start, place, qg_arrived, chunks)
    query_returned = lax.all_to_all(
        query_back.reshape(n_replicas, slot_cap, tile_rows, row_width),
        "dp", split_axis=0, concat_axis=0, tiled=True,
    )
    far_terms = near_terms(terms[NEAR:])
    own_terms, far_terms = lax.optimization_barrier((terms[:NEAR], far_terms))
    across = total([term[1:] for term in far_terms]).astype(jnp.bfloat16)
    arrived = far_swap(across, ACROSS)
    crossing = total([term[0] for term in far_terms] + [arrived[1]]).astype(jnp.bfloat16)
    other = far_swap(crossing, MIRROR)
    last = near_terms(own_terms) + [arrived, other]
    last, query_returned = lax.optimization_barrier((last, query_returned))
    kv_returned = over_plane(
        local_call(kv_back_kernel, "kv_back", [my_recv, place], last, traveling)
    )

    flat_slots = jnp.arange(slots)
    own_slots = replica * slot_cap + jnp.arange(slot_cap)
    slot_used = jnp.any(recv_slot[:, None, :] == own_slots[None, :, None], axis=2)
    matched = slot_used[:, :, None] & (my_send[:, :, None] == jnp.arange(tile_count)[None, None, :])
    anchor = jnp.sum(
        jnp.where(matched, flat_slots.reshape(n_replicas, slot_cap)[:, :, None], 0), axis=(0, 1)
    )
    grad_queries = query_returned.reshape(slots, tile_rows, row_width)[anchor]
    kv_final = local_call(
        kv_final_kernel, "kv_final", [anchor], [kv_returned],
        jax.ShapeDtypeStruct(kv_blocks.shape, keys_values.dtype),
    )
    grad_keys_values = kv_final.transpose(0, 2, 1, 3).reshape(keys_values.shape)
    return (grad_queries, grad_keys_values)


def solution(mesh):
    fine = Mesh(mesh.devices.reshape(mesh.devices.shape[0], 2, 16), ("dp", "xh", "z"))
    tensor = ("xh", "z")
    in_specs = (
        P("dp", None, tensor),
        P("dp", tensor, None),
        P("dp", None, tensor),
        P("dp", None, None),
        P(),
        P("dp", None),
    )
    out_specs = (P("dp", None, tensor), P("dp", tensor, None))
    return jax.shard_map(
        on_device, mesh=fine, in_specs=in_specs, out_specs=out_specs, check_vma=False
    )
```

```python
import functools

import jax
import jax.numpy as jnp
from jax import lax
from jax.experimental import pallas as pl
from jax.experimental.pallas import tpu as pltpu
from jax.sharding import Mesh
from jax.sharding import PartitionSpec as P

HD = 128
KV = 4
PAIR = 2
SCALING = HD ** (-0.5)
LOG2E = 1.4426950408889634
PLANE = ("dp", "xh")
MIRROR = 12
ACROSS = 6
NEAR = 4


def matmul(a, b, contract):
    return lax.dot_general(a, b, (contract, ((), ())), preferred_element_type=jnp.float32)


def pack_kernel(index_ref, q_ref, g_ref, out_ref):
    def body(slot, _):
        tile = index_ref[slot & 1, slot >> 1]
        out_ref[slot, 0] = q_ref[tile]
        out_ref[slot, 1] = g_ref[tile]
        return 0

    lax.fori_loop(0, out_ref.shape[0], body, 0, unroll=2)


def pack(index, queries, grad_out):
    slots = index.size
    return pl.pallas_call(
        pack_kernel,
        out_shape=jax.ShapeDtypeStruct((slots, 2) + queries.shape[1:], queries.dtype),
        in_specs=[
            pl.BlockSpec(memory_space=pltpu.SMEM),
            pl.BlockSpec(memory_space=pltpu.VMEM),
            pl.BlockSpec(memory_space=pltpu.VMEM),
        ],
        out_specs=pl.BlockSpec(memory_space=pltpu.VMEM),
        compiler_params=pltpu.CompilerParams(vmem_limit_bytes=24 * 2**20),
        name="pack_rows",
    )(index, queries, grad_out)


def attention_kernel(
    recv_ref, start_ref, place_ref, qg_ref, *refs
):
    kv_refs, dq_ref, dkv_refs = refs[: 2 * NEAR], refs[2 * NEAR], refs[2 * NEAR + 1 : 4 * NEAR + 1]
    k_all, kt_all, v_all, dk_all, dv_all, *rest = refs[4 * NEAR + 1 :]
    scores, dprobs, diagonal_scores, diagonal_dprobs, stats, dqt = rest
    blocks = k_all.shape[0]
    width = k_all.shape[1]
    tile_rows = width // PAIR
    part = width // NEAR
    factor = SCALING * LOG2E

    def rows_of(slot, first_part):
        begin = (slot % NEAR) * part
        if slot < NEAR:
            return slice(begin, begin + first_part)
        return slice(begin + first_part, begin + part)

    def stage(block, _):
        for slot, ref in enumerate(kv_refs):
            rows = rows_of(slot, part // 4)
            count = rows.stop - rows.start
            key = ref[:, :, 0, block].astype(jnp.float32).reshape(count, HD)
            value = ref[:, :, 1, block].astype(jnp.float32).reshape(count, HD)
            k_all[block, rows] = key.astype(jnp.bfloat16)
            v_all[block, rows] = value.astype(jnp.bfloat16)
        kt_all[block] = k_all[block].astype(jnp.float32).T.astype(jnp.bfloat16)
        return 0

    lax.fori_loop(0, blocks, stage, 0, unroll=4)

    row = lax.broadcasted_iota(jnp.int32, (width, 1), 0)
    holder = (place_ref[0] & 12) | ((place_ref[0] - (row >> 6)) & 3)
    source = holder ^ (((row >> 4) & 1) * MIRROR) ^ (((row >> 5) & 1) * ACROSS)
    key_offset = (
        ((row >> 2) & 1) * tile_rows + ((row >> 3) & 1) * 64 + source * 4 + (row & 3)
    )
    lane = lax.broadcasted_iota(jnp.int32, (1, width), 1)

    def operands(block):
        first = recv_ref[PAIR * block]
        second = recv_ref[PAIR * block + 1]
        query = jnp.concatenate([qg_ref[first, 0], qg_ref[second, 0]], axis=0)
        grad = jnp.concatenate([qg_ref[first, 1], qg_ref[second, 1]], axis=0)
        return query, grad

    def first_row(block):
        low, high = start_ref[PAIR * block], start_ref[PAIR * block + 1]
        return jnp.where(lane < tile_rows, low, high) * tile_rows

    def terms(weights, dprob, key_t, query, grad, inverse, delta):
        probs = weights * inverse
        dscores = (probs * (dprob - delta)).astype(jnp.bfloat16)
        grad_value = matmul(probs.astype(jnp.bfloat16), grad, ((1,), (0,)))
        grad_key = matmul(dscores, query, ((1,), (0,)))
        grad_query = matmul(key_t, dscores, ((1,), (0,)))
        return grad_key, grad_value, grad_query

    def diagonal_products(block, _):
        query, grad = operands(block)
        score = matmul(k_all[block], query, ((1,), (1,)))
        allowed = (key_offset >= first_row(block) - block * width) & (key_offset <= lane)
        score = jnp.where(allowed, score, -jnp.inf)
        diagonal_scores[block] = score
        diagonal_dprobs[block] = matmul(v_all[block], grad, ((1,), (1,)))
        peak = jnp.max(score, axis=0, keepdims=True)
        stats[block, 0] = jnp.broadcast_to(peak, stats.shape[2:])
        dk_all[block] = jnp.zeros_like(dk_all[block])
        dv_all[block] = jnp.zeros_like(dv_all[block])
        dqt[block] = jnp.zeros_like(dqt[block])
        return 0

    lax.fori_loop(0, blocks, diagonal_products, 0, unroll=8)

    def sweep(begin, end, step, state):
        twice = (end - begin) >> 1

        def two(index, state):
            return step(begin + 2 * index + 1, step(begin + 2 * index, state))

        state = lax.fori_loop(0, twice, two, state)
        return lax.fori_loop(begin + 2 * twice, end, step, state)

    def query_block(block, _):
        query, grad = operands(block)
        row_start = first_row(block)
        lowest = start_ref[PAIR * block] // PAIR

        def products(other, peak):
            score = matmul(k_all[other], query, ((1,), (1,)))
            score = jnp.where(key_offset >= row_start - other * width, score, -jnp.inf)
            scores[other] = score
            dprobs[other] = matmul(v_all[other], grad, ((1,), (1,)))
            return jnp.maximum(peak, jnp.max(score, axis=0, keepdims=True))

        peak = sweep(lowest, block, products, stats[block, 0][:1])
        shift = peak * factor

        def sums(other, totals):
            weights = jnp.exp2(scores[other] * factor - shift)
            scores[other] = weights
            return (
                totals[0] + jnp.sum(weights, axis=0, keepdims=True),
                totals[1] + jnp.sum(weights * dprobs[other], axis=0, keepdims=True),
            )

        weights = jnp.exp2(diagonal_scores[block] * factor - shift)
        diagonal_scores[block] = weights
        totals = (
            jnp.sum(weights, axis=0, keepdims=True),
            jnp.sum(weights * diagonal_dprobs[block], axis=0, keepdims=True),
        )
        total, weighted = sweep(lowest, block, sums, totals)
        inverse = 1.0 / total
        delta = weighted * inverse
        stats[block, 0] = jnp.broadcast_to(inverse, stats.shape[2:])
        stats[block, 1] = jnp.broadcast_to(delta, stats.shape[2:])

        def earlier(other, _):
            grad_key, grad_value, grad_query = terms(
                scores[other], dprobs[other], kt_all[other], query, grad, inverse, delta
            )
            dk_all[other] += grad_key
            dv_all[other] += grad_value
            dqt[block] += grad_query
            return 0

        sweep(lowest, block, earlier, 0)
        return 0

    lax.fori_loop(0, blocks, query_block, 0)

    def diagonal_terms(block, _):
        query, grad = operands(block)
        grad_key, grad_value, grad_query = terms(
            diagonal_scores[block], diagonal_dprobs[block], kt_all[block], query, grad,
            stats[block, 0][:1], stats[block, 1][:1],
        )
        dk_all[block] += grad_key
        dv_all[block] += grad_value
        result = ((dqt[block] + grad_query) * SCALING).T.astype(jnp.bfloat16)
        dq_ref[recv_ref[PAIR * block]] = result[:tile_rows]
        dq_ref[recv_ref[PAIR * block + 1]] = result[tile_rows:]
        return 0

    lax.fori_loop(0, blocks, diagonal_terms, 0, unroll=8)

    def unstage(block, _):
        for slot, ref in enumerate(dkv_refs):
            rows = rows_of(slot, part // 4)
            shape = ref.shape[:2] + ref.shape[4:]
            ref[:, :, 0, block] = (dk_all[block, rows] * SCALING).reshape(shape).astype(jnp.bfloat16)
            ref[:, :, 1, block] = dv_all[block, rows].reshape(shape).astype(jnp.bfloat16)
        return 0

    lax.fori_loop(0, blocks, unstage, 0, unroll=4)


def attention(my_recv, start, place, qg, chunks):
    slots, _, tile_rows, _ = qg.shape
    blocks = my_recv.shape[0] // PAIR
    width = PAIR * tile_rows
    vmem = pl.BlockSpec(memory_space=pltpu.VMEM)
    smem = pl.BlockSpec(memory_space=pltpu.SMEM)
    return pl.pallas_call(
        attention_kernel,
        out_shape=(jax.ShapeDtypeStruct((slots, tile_rows, HD), jnp.bfloat16),)
        + tuple(jax.ShapeDtypeStruct(chunk.shape, jnp.bfloat16) for chunk in chunks),
        in_specs=[smem] * 3 + [vmem] * (1 + 2 * NEAR),
        out_specs=(vmem,) * (1 + 2 * NEAR),
        scratch_shapes=[
            pltpu.VMEM((blocks, width, HD), jnp.bfloat16),
            pltpu.VMEM((blocks, HD, width), jnp.bfloat16),
            pltpu.VMEM((blocks, width, HD), jnp.bfloat16),
            pltpu.VMEM((blocks, width, HD), jnp.float32),
            pltpu.VMEM((blocks, width, HD), jnp.float32),
            pltpu.VMEM((blocks, width, width), jnp.float32),
            pltpu.VMEM((blocks, width, width), jnp.float32),
            pltpu.VMEM((blocks, width, width), jnp.float32),
            pltpu.VMEM((blocks, width, width), jnp.float32),
            pltpu.VMEM((blocks, 2, 8, width), jnp.float32),
            pltpu.VMEM((blocks, HD, width), jnp.float32),
        ],
        compiler_params=pltpu.CompilerParams(vmem_limit_bytes=20 * 2**20),
        cost_estimate=pl.CostEstimate(
            flops=2 * 10**9, bytes_accessed=6 * 2**20, transcendentals=2 * 10**6
        ),
        name="attention_backward",
    )(my_recv, start, place, qg, *chunks)


def kv_pack_kernel(index_ref, kv_ref, out_ref):
    def body(slot, _):
        tile = index_ref[slot & 1, slot >> 1]
        piece = kv_ref[tile].reshape((2, 2, 2) + kv_ref.shape[2:])
        for half in range(2):
            out_ref[slot >> 1, half, slot & 1] = piece[:, half]
        return 0

    lax.fori_loop(0, 2 * index_ref.shape[1], body, 0, unroll=4)


def kv_unpack_kernel(recv_ref, place_ref, kv_ref, own_ref, other_ref):
    head = place_ref[0] >> 3

    def body(pair, _):
        low = recv_ref[PAIR * pair]
        high = recv_ref[PAIR * pair + 1]
        for half in range(2):
            for kind in range(2):
                for ref, which in ((own_ref, head), (other_ref, 1 - head)):
                    rows = [
                        kv_ref[slot >> 1, half, slot & 1, kind, which].astype(jnp.float32)
                        for slot in (low, high)
                    ]
                    ref[half, kind, pair] = jnp.concatenate(rows, axis=0).astype(jnp.bfloat16)
        return 0

    lax.fori_loop(0, recv_ref.shape[0] // PAIR, body, 0, unroll=4)


def kv_back_kernel(recv_ref, place_ref, *refs):
    own_refs, (across_ref, other_ref, out_ref) = refs[:NEAR], refs[NEAR:]
    head = place_ref[0] >> 3
    sliver = out_ref.shape[-2]

    def body(pair, _):
        slots = (recv_ref[PAIR * pair], recv_ref[PAIR * pair + 1])
        for half in range(2):
            for kind in range(2):
                own = across_ref[0, half, kind, pair].astype(jnp.float32)
                for ref in own_refs:
                    own += ref[0, half, kind, pair].astype(jnp.float32)
                other = other_ref[half, kind, pair].astype(jnp.float32)
                for total, which in ((own, head), (other, 1 - head)):
                    for order, slot in enumerate(slots):
                        rows = total[order * sliver : (order + 1) * sliver]
                        out_ref[slot >> 1, half, slot & 1, kind, which] = rows.astype(jnp.bfloat16)
        return 0

    lax.fori_loop(0, recv_ref.shape[0] // PAIR, body, 0, unroll=4)


def kv_final_kernel(anchor_ref, kv_ref, out_ref):
    def body(tile, _):
        slot = anchor_ref[tile]
        piece = kv_ref[slot >> 1, :, slot & 1]
        for half in range(2):
            for kind in range(2):
                for head in range(2):
                    out_ref[tile, kind * 4 + half * 2 + head] = piece[half, kind, head]
        return 0

    lax.fori_loop(0, anchor_ref.shape[0], body, 0, unroll=4)


def local_call(kernel, name, scalars, arrays, out_shape):
    vmem = pl.BlockSpec(memory_space=pltpu.VMEM)
    smem = pl.BlockSpec(memory_space=pltpu.SMEM)
    return pl.pallas_call(
        kernel,
        out_shape=out_shape,
        in_specs=[smem] * len(scalars) + [vmem] * len(arrays),
        out_specs=jax.tree.map(lambda _: vmem, out_shape),
        compiler_params=pltpu.CompilerParams(vmem_limit_bytes=16 * 2**20),
        name=name,
    )(*scalars, *arrays)


def far_swap(values, flip):
    return lax.ppermute(values, "z", [(place, place ^ flip) for place in range(16)])


def near_shift(values, step):
    pairs = [(place, (place & 12) | ((place + step) & 3)) for place in range(16)]
    return lax.ppermute(values, "z", pairs)


def near_gather(values):
    return [values] + [near_shift(values, step) for step in range(1, NEAR)]


def near_terms(terms):
    return [terms[0]] + [near_shift(terms[step], -step) for step in range(1, NEAR)]


def total(terms):
    return sum(term.astype(jnp.float32) for term in terms)


def on_device(queries, keys_values, grad_out, send_tiles, recv_slot, tile_seq):
    n_replicas = lax.axis_size("dp")
    replica = lax.axis_index("dp")
    tile_count, tile_rows, row_width = queries.shape
    sliver = keys_values.shape[1]
    slot_cap = send_tiles.shape[2]
    slots = n_replicas * slot_cap
    pairs = tile_count // PAIR
    my_send = send_tiles[0]
    outgoing = my_send.T
    my_recv = lax.dynamic_index_in_dim(recv_slot, replica, 0, keepdims=False)
    place = lax.axis_index("z").astype(jnp.int32).reshape(1)
    traveling = jax.ShapeDtypeStruct(
        (n_replicas, 2, slot_cap, 2, 2, sliver, HD), keys_values.dtype
    )
    half_shape = jax.ShapeDtypeStruct((2, 2, pairs, PAIR * sliver, HD), keys_values.dtype)

    def over_plane(values):
        return lax.all_to_all(
            values.reshape((2 * n_replicas,) + values.shape[2:]),
            PLANE, split_axis=0, concat_axis=0, tiled=True,
        ).reshape(values.shape)

    kv_blocks = keys_values.reshape(tile_count, sliver, 2 * KV, HD).transpose(0, 2, 1, 3)
    kv_arrived = over_plane(
        local_call(kv_pack_kernel, "kv_pack", [outgoing], [kv_blocks], traveling)
    )
    own, other = local_call(
        kv_unpack_kernel, "kv_unpack", [my_recv, place], [kv_arrived], (half_shape, half_shape)
    )
    qg_packed = pack(outgoing, queries, grad_out)
    qg_arrived = lax.all_to_all(
        qg_packed.reshape(n_replicas, slot_cap, 2, tile_rows, row_width),
        "dp", split_axis=0, concat_axis=0, tiled=True,
    ).reshape(slots, 2, tile_rows, row_width)
    far = jnp.stack(
        [far_swap(other, MIRROR), far_swap(own, ACROSS), far_swap(other, MIRROR ^ ACROSS)]
    )
    own_chunks = near_gather(own[None])
    far, own_chunks, qg_arrived = lax.optimization_barrier((far, own_chunks, qg_arrived))
    chunks = own_chunks + near_gather(far)

    seq = tile_seq[0]
    start = jnp.sum((seq[None, :] < seq[:, None]).astype(jnp.int32), axis=1)
    query_back, *terms = attention(my_recv, start, place, qg_arrived, chunks)
    query_returned = lax.all_to_all(
        query_back.reshape(n_replicas, slot_cap, tile_rows, row_width),
        "dp", split_axis=0, concat_axis=0, tiled=True,
    )
    far_terms = near_terms(terms[NEAR:])
    own_terms, far_terms = lax.optimization_barrier((terms[:NEAR], far_terms))
    across = total([term[1:] for term in far_terms]).astype(jnp.bfloat16)
    arrived = far_swap(across, ACROSS)
    crossing = total([term[0] for term in far_terms] + [arrived[1]]).astype(jnp.bfloat16)
    other = far_swap(crossing, MIRROR)
    last = near_terms(own_terms) + [arrived, other]
    last, query_returned = lax.optimization_barrier((last, query_returned))
    kv_returned = over_plane(
        local_call(kv_back_kernel, "kv_back", [my_recv, place], last, traveling)
    )

    flat_slots = jnp.arange(slots)
    own_slots = replica * slot_cap + jnp.arange(slot_cap)
    slot_used = jnp.any(recv_slot[:, None, :] == own_slots[None, :, None], axis=2)
    matched = slot_used[:, :, None] & (my_send[:, :, None] == jnp.arange(tile_count)[None, None, :])
    anchor = jnp.sum(
        jnp.where(matched, flat_slots.reshape(n_replicas, slot_cap)[:, :, None], 0), axis=(0, 1)
    )
    grad_queries = query_returned.reshape(slots, tile_rows, row_width)[anchor]
    kv_final = local_call(
        kv_final_kernel, "kv_final", [anchor], [kv_returned],
        jax.ShapeDtypeStruct(kv_blocks.shape, keys_values.dtype),
    )
    grad_keys_values = kv_final.transpose(0, 2, 1, 3).reshape(keys_values.shape)
    return (grad_queries, grad_keys_values)


def solution(mesh):
    fine = Mesh(mesh.devices.reshape(mesh.devices.shape[0], 2, 16), ("dp", "xh", "z"))
    tensor = ("xh", "z")
    in_specs = (
        P("dp", None, tensor),
        P("dp", tensor, None),
        P("dp", None, tensor),
        P("dp", None, None),
        P(),
        P("dp", None),
    )
    out_specs = (P("dp", None, tensor), P("dp", tensor, None))
    return jax.shard_map(
        on_device, mesh=fine, in_specs=in_specs, out_specs=out_specs, check_vma=False
    )
```

```python
import functools

import jax
import jax.numpy as jnp
from jax import lax
from jax.experimental import pallas as pl
from jax.experimental.pallas import tpu as pltpu
from jax.sharding import Mesh
from jax.sharding import PartitionSpec as P

HD = 128
KV = 4
PAIR = 2
SCALING = HD ** (-0.5)
LOG2E = 1.4426950408889634
PLANE = ("dp", "xh")
MIRROR = 12
ACROSS = 7
NEAR = 4


def matmul(a, b, contract):
    return lax.dot_general(a, b, (contract, ((), ())), preferred_element_type=jnp.float32)


def pack_kernel(index_ref, q_ref, g_ref, out_ref):
    def body(slot, _):
        tile = index_ref[slot & 1, slot >> 1]
        out_ref[slot, 0] = q_ref[tile]
        out_ref[slot, 1] = g_ref[tile]
        return 0

    lax.fori_loop(0, out_ref.shape[0], body, 0, unroll=2)


def pack(index, queries, grad_out):
    slots = index.size
    return pl.pallas_call(
        pack_kernel,
        out_shape=jax.ShapeDtypeStruct((slots, 2) + queries.shape[1:], queries.dtype),
        in_specs=[
            pl.BlockSpec(memory_space=pltpu.SMEM),
            pl.BlockSpec(memory_space=pltpu.VMEM),
            pl.BlockSpec(memory_space=pltpu.VMEM),
        ],
        out_specs=pl.BlockSpec(memory_space=pltpu.VMEM),
        compiler_params=pltpu.CompilerParams(vmem_limit_bytes=24 * 2**20),
        name="pack_rows",
    )(index, queries, grad_out)


def attention_kernel(
    recv_ref, start_ref, place_ref, qg_ref, *refs
):
    kv_refs, dq_ref, dkv_refs = refs[: 2 * NEAR], refs[2 * NEAR], refs[2 * NEAR + 1 : 4 * NEAR + 1]
    k_all, kt_all, v_all, dk_all, dv_all, *rest = refs[4 * NEAR + 1 :]
    scores, dprobs, diagonal_scores, diagonal_dprobs, stats, dqt = rest
    blocks = k_all.shape[0]
    width = k_all.shape[1]
    tile_rows = width // PAIR
    part = width // NEAR
    factor = SCALING * LOG2E

    def rows_of(slot, first_part):
        begin = (slot % NEAR) * part
        if slot < NEAR:
            return slice(begin, begin + first_part)
        return slice(begin + first_part, begin + part)

    def stage(block, _):
        for slot, ref in enumerate(kv_refs):
            rows = rows_of(slot, part // 4)
            count = rows.stop - rows.start
            key = ref[:, :, 0, block].astype(jnp.float32).reshape(count, HD)
            value = ref[:, :, 1, block].astype(jnp.float32).reshape(count, HD)
            k_all[block, rows] = key.astype(jnp.bfloat16)
            v_all[block, rows] = value.astype(jnp.bfloat16)
        kt_all[block] = k_all[block].astype(jnp.float32).T.astype(jnp.bfloat16)
        return 0

    lax.fori_loop(0, blocks, stage, 0, unroll=4)

    row = lax.broadcasted_iota(jnp.int32, (width, 1), 0)
    holder = (place_ref[0] & 12) | ((place_ref[0] - (row >> 6)) & 3)
    source = holder ^ (((row >> 4) & 1) * MIRROR) ^ (((row >> 5) & 1) * ACROSS)
    key_offset = (
        ((row >> 2) & 1) * tile_rows + ((row >> 3) & 1) * 64 + source * 4 + (row & 3)
    )
    lane = lax.broadcasted_iota(jnp.int32, (1, width), 1)

    def operands(block):
        first = recv_ref[PAIR * block]
        second = recv_ref[PAIR * block + 1]
        query = jnp.concatenate([qg_ref[first, 0], qg_ref[second, 0]], axis=0)
        grad = jnp.concatenate([qg_ref[first, 1], qg_ref[second, 1]], axis=0)
        return query, grad

    def first_row(block):
        low, high = start_ref[PAIR * block], start_ref[PAIR * block + 1]
        return jnp.where(lane < tile_rows, low, high) * tile_rows

    def terms(weights, dprob, key_t, query, grad, inverse, delta):
        probs = weights * inverse
        dscores = (probs * (dprob - delta)).astype(jnp.bfloat16)
        grad_value = matmul(probs.astype(jnp.bfloat16), grad, ((1,), (0,)))
        grad_key = matmul(dscores, query, ((1,), (0,)))
        grad_query = matmul(key_t, dscores, ((1,), (0,)))
        return grad_key, grad_value, grad_query

    def diagonal_products(block, _):
        query, grad = operands(block)
        score = matmul(k_all[block], query, ((1,), (1,)))
        allowed = (key_offset >= first_row(block) - block * width) & (key_offset <= lane)
        score = jnp.where(allowed, score, -jnp.inf)
        diagonal_scores[block] = score
        diagonal_dprobs[block] = matmul(v_all[block], grad, ((1,), (1,)))
        peak = jnp.max(score, axis=0, keepdims=True)
        stats[block, 0] = jnp.broadcast_to(peak, stats.shape[2:])
        dk_all[block] = jnp.zeros_like(dk_all[block])
        dv_all[block] = jnp.zeros_like(dv_all[block])
        dqt[block] = jnp.zeros_like(dqt[block])
        return 0

    lax.fori_loop(0, blocks, diagonal_products, 0, unroll=8)

    def sweep(begin, end, step, state):
        twice = (end - begin) >> 1

        def two(index, state):
            return step(begin + 2 * index + 1, step(begin + 2 * index, state))

        state = lax.fori_loop(0, twice, two, state)
        return lax.fori_loop(begin + 2 * twice, end, step, state)

    def query_block(block, _):
        query, grad = operands(block)
        row_start = first_row(block)
        lowest = start_ref[PAIR * block] // PAIR

        def products(other, peak):
            score = matmul(k_all[other], query, ((1,), (1,)))
            score = jnp.where(key_offset >= row_start - other * width, score, -jnp.inf)
            scores[other] = score
            dprobs[other] = matmul(v_all[other], grad, ((1,), (1,)))
            return jnp.maximum(peak, jnp.max(score, axis=0, keepdims=True))

        peak = sweep(lowest, block, products, stats[block, 0][:1])
        shift = peak * factor

        def sums(other, totals):
            weights = jnp.exp2(scores[other] * factor - shift)
            scores[other] = weights
            return (
                totals[0] + jnp.sum(weights, axis=0, keepdims=True),
                totals[1] + jnp.sum(weights * dprobs[other], axis=0, keepdims=True),
            )

        weights = jnp.exp2(diagonal_scores[block] * factor - shift)
        diagonal_scores[block] = weights
        totals = (
            jnp.sum(weights, axis=0, keepdims=True),
            jnp.sum(weights * diagonal_dprobs[block], axis=0, keepdims=True),
        )
        total, weighted = sweep(lowest, block, sums, totals)
        inverse = 1.0 / total
        delta = weighted * inverse
        stats[block, 0] = jnp.broadcast_to(inverse, stats.shape[2:])
        stats[block, 1] = jnp.broadcast_to(delta, stats.shape[2:])

        def earlier(other, _):
            grad_key, grad_value, grad_query = terms(
                scores[other], dprobs[other], kt_all[other], query, grad, inverse, delta
            )
            dk_all[other] += grad_key
            dv_all[other] += grad_value
            dqt[block] += grad_query
            return 0

        sweep(lowest, block, earlier, 0)
        return 0

    lax.fori_loop(0, blocks, query_block, 0)

    def diagonal_terms(block, _):
        query, grad = operands(block)
        grad_key, grad_value, grad_query = terms(
            diagonal_scores[block], diagonal_dprobs[block], kt_all[block], query, grad,
            stats[block, 0][:1], stats[block, 1][:1],
        )
        dk_all[block] += grad_key
        dv_all[block] += grad_value
        result = ((dqt[block] + grad_query) * SCALING).T.astype(jnp.bfloat16)
        dq_ref[recv_ref[PAIR * block]] = result[:tile_rows]
        dq_ref[recv_ref[PAIR * block + 1]] = result[tile_rows:]
        return 0

    lax.fori_loop(0, blocks, diagonal_terms, 0, unroll=8)

    def unstage(block, _):
        for slot, ref in enumerate(dkv_refs):
            rows = rows_of(slot, part // 4)
            shape = ref.shape[:2] + ref.shape[4:]
            ref[:, :, 0, block] = (dk_all[block, rows] * SCALING).reshape(shape).astype(jnp.bfloat16)
            ref[:, :, 1, block] = dv_all[block, rows].reshape(shape).astype(jnp.bfloat16)
        return 0

    lax.fori_loop(0, blocks, unstage, 0, unroll=4)


def attention(my_recv, start, place, qg, chunks):
    slots, _, tile_rows, _ = qg.shape
    blocks = my_recv.shape[0] // PAIR
    width = PAIR * tile_rows
    vmem = pl.BlockSpec(memory_space=pltpu.VMEM)
    smem = pl.BlockSpec(memory_space=pltpu.SMEM)
    return pl.pallas_call(
        attention_kernel,
        out_shape=(jax.ShapeDtypeStruct((slots, tile_rows, HD), jnp.bfloat16),)
        + tuple(jax.ShapeDtypeStruct(chunk.shape, jnp.bfloat16) for chunk in chunks),
        in_specs=[smem] * 3 + [vmem] * (1 + 2 * NEAR),
        out_specs=(vmem,) * (1 + 2 * NEAR),
        scratch_shapes=[
            pltpu.VMEM((blocks, width, HD), jnp.bfloat16),
            pltpu.VMEM((blocks, HD, width), jnp.bfloat16),
            pltpu.VMEM((blocks, width, HD), jnp.bfloat16),
            pltpu.VMEM((blocks, width, HD), jnp.float32),
            pltpu.VMEM((blocks, width, HD), jnp.float32),
            pltpu.VMEM((blocks, width, width), jnp.float32),
            pltpu.VMEM((blocks, width, width), jnp.float32),
            pltpu.VMEM((blocks, width, width), jnp.float32),
            pltpu.VMEM((blocks, width, width), jnp.float32),
            pltpu.VMEM((blocks, 2, 8, width), jnp.float32),
            pltpu.VMEM((blocks, HD, width), jnp.float32),
        ],
        compiler_params=pltpu.CompilerParams(vmem_limit_bytes=20 * 2**20),
        cost_estimate=pl.CostEstimate(
            flops=2 * 10**9, bytes_accessed=6 * 2**20, transcendentals=2 * 10**6
        ),
        name="attention_backward",
    )(my_recv, start, place, qg, *chunks)


def kv_pack_kernel(index_ref, kv_ref, out_ref):
    def body(slot, _):
        tile = index_ref[slot & 1, slot >> 1]
        piece = kv_ref[tile].reshape((2, 2, 2) + kv_ref.shape[2:])
        for half in range(2):
            out_ref[slot >> 1, half, slot & 1] = piece[:, half]
        return 0

    lax.fori_loop(0, 2 * index_ref.shape[1], body, 0, unroll=4)


def kv_unpack_kernel(recv_ref, place_ref, kv_ref, own_ref, other_ref):
    head = place_ref[0] >> 3

    def body(pair, _):
        low = recv_ref[PAIR * pair]
        high = recv_ref[PAIR * pair + 1]
        for half in range(2):
            for kind in range(2):
                for ref, which in ((own_ref, head), (other_ref, 1 - head)):
                    rows = [
                        kv_ref[slot >> 1, half, slot & 1, kind, which].astype(jnp.float32)
                        for slot in (low, high)
                    ]
                    ref[half, kind, pair] = jnp.concatenate(rows, axis=0).astype(jnp.bfloat16)
        return 0

    lax.fori_loop(0, recv_ref.shape[0] // PAIR, body, 0, unroll=4)


def kv_back_kernel(recv_ref, place_ref, *refs):
    own_refs, (across_ref, other_ref, out_ref) = refs[:NEAR], refs[NEAR:]
    head = place_ref[0] >> 3
    sliver = out_ref.shape[-2]

    def body(pair, _):
        slots = (recv_ref[PAIR * pair], recv_ref[PAIR * pair + 1])
        for half in range(2):
            for kind in range(2):
                own = across_ref[0, half, kind, pair].astype(jnp.float32)
                for ref in own_refs:
                    own += ref[0, half, kind, pair].astype(jnp.float32)
                other = other_ref[half, kind, pair].astype(jnp.float32)
                for total, which in ((own, head), (other, 1 - head)):
                    for order, slot in enumerate(slots):
                        rows = total[order * sliver : (order + 1) * sliver]
                        out_ref[slot >> 1, half, slot & 1, kind, which] = rows.astype(jnp.bfloat16)
        return 0

    lax.fori_loop(0, recv_ref.shape[0] // PAIR, body, 0, unroll=4)


def kv_final_kernel(anchor_ref, kv_ref, out_ref):
    def body(tile, _):
        slot = anchor_ref[tile]
        piece = kv_ref[slot >> 1, :, slot & 1]
        for half in range(2):
            for kind in range(2):
                for head in range(2):
                    out_ref[tile, kind * 4 + half * 2 + head] = piece[half, kind, head]
        return 0

    lax.fori_loop(0, anchor_ref.shape[0], body, 0, unroll=4)


def local_call(kernel, name, scalars, arrays, out_shape):
    vmem = pl.BlockSpec(memory_space=pltpu.VMEM)
    smem = pl.BlockSpec(memory_space=pltpu.SMEM)
    return pl.pallas_call(
        kernel,
        out_shape=out_shape,
        in_specs=[smem] * len(scalars) + [vmem] * len(arrays),
        out_specs=jax.tree.map(lambda _: vmem, out_shape),
        compiler_params=pltpu.CompilerParams(vmem_limit_bytes=16 * 2**20),
        name=name,
    )(*scalars, *arrays)


def far_swap(values, flip):
    return lax.ppermute(values, "z", [(place, place ^ flip) for place in range(16)])


def near_shift(values, step):
    pairs = [(place, (place & 12) | ((place + step) & 3)) for place in range(16)]
    return lax.ppermute(values, "z", pairs)


def near_gather(values):
    return [values] + [near_shift(values, step) for step in range(1, NEAR)]


def near_terms(terms):
    return [terms[0]] + [near_shift(terms[step], -step) for step in range(1, NEAR)]


def total(terms):
    return sum(term.astype(jnp.float32) for term in terms)


def on_device(queries, keys_values, grad_out, send_tiles, recv_slot, tile_seq):
    n_replicas = lax.axis_size("dp")
    replica = lax.axis_index("dp")
    tile_count, tile_rows, row_width = queries.shape
    sliver = keys_values.shape[1]
    slot_cap = send_tiles.shape[2]
    slots = n_replicas * slot_cap
    pairs = tile_count // PAIR
    my_send = send_tiles[0]
    outgoing = my_send.T
    my_recv = lax.dynamic_index_in_dim(recv_slot, replica, 0, keepdims=False)
    place = lax.axis_index("z").astype(jnp.int32).reshape(1)
    traveling = jax.ShapeDtypeStruct(
        (n_replicas, 2, slot_cap, 2, 2, sliver, HD), keys_values.dtype
    )
    half_shape = jax.ShapeDtypeStruct((2, 2, pairs, PAIR * sliver, HD), keys_values.dtype)

    def over_plane(values):
        return lax.all_to_all(
            values.reshape((2 * n_replicas,) + values.shape[2:]),
            PLANE, split_axis=0, concat_axis=0, tiled=True,
        ).reshape(values.shape)

    kv_blocks = keys_values.reshape(tile_count, sliver, 2 * KV, HD).transpose(0, 2, 1, 3)
    kv_arrived = over_plane(
        local_call(kv_pack_kernel, "kv_pack", [outgoing], [kv_blocks], traveling)
    )
    own, other = local_call(
        kv_unpack_kernel, "kv_unpack", [my_recv, place], [kv_arrived], (half_shape, half_shape)
    )
    qg_packed = pack(outgoing, queries, grad_out)
    qg_arrived = lax.all_to_all(
        qg_packed.reshape(n_replicas, slot_cap, 2, tile_rows, row_width),
        "dp", split_axis=0, concat_axis=0, tiled=True,
    ).reshape(slots, 2, tile_rows, row_width)
    far = jnp.stack(
        [far_swap(other, MIRROR), far_swap(own, ACROSS), far_swap(other, MIRROR ^ ACROSS)]
    )
    own_chunks = near_gather(own[None])
    far, own_chunks, qg_arrived = lax.optimization_barrier((far, own_chunks, qg_arrived))
    chunks = own_chunks + near_gather(far)

    seq = tile_seq[0]
    start = jnp.sum((seq[None, :] < seq[:, None]).astype(jnp.int32), axis=1)
    query_back, *terms = attention(my_recv, start, place, qg_arrived, chunks)
    query_returned = lax.all_to_all(
        query_back.reshape(n_replicas, slot_cap, tile_rows, row_width),
        "dp", split_axis=0, concat_axis=0, tiled=True,
    )
    far_terms = near_terms(terms[NEAR:])
    own_terms, far_terms = lax.optimization_barrier((terms[:NEAR], far_terms))
    across = total([term[1:] for term in far_terms]).astype(jnp.bfloat16)
    arrived = far_swap(across, ACROSS)
    crossing = total([term[0] for term in far_terms] + [arrived[1]]).astype(jnp.bfloat16)
    other = far_swap(crossing, MIRROR)
    last = near_terms(own_terms) + [arrived, other]
    last, query_returned = lax.optimization_barrier((last, query_returned))
    kv_returned = over_plane(
        local_call(kv_back_kernel, "kv_back", [my_recv, place], last, traveling)
    )

    flat_slots = jnp.arange(slots)
    own_slots = replica * slot_cap + jnp.arange(slot_cap)
    slot_used = jnp.any(recv_slot[:, None, :] == own_slots[None, :, None], axis=2)
    matched = slot_used[:, :, None] & (my_send[:, :, None] == jnp.arange(tile_count)[None, None, :])
    anchor = jnp.sum(
        jnp.where(matched, flat_slots.reshape(n_replicas, slot_cap)[:, :, None], 0), axis=(0, 1)
    )
    grad_queries = query_returned.reshape(slots, tile_rows, row_width)[anchor]
    kv_final = local_call(
        kv_final_kernel, "kv_final", [anchor], [kv_returned],
        jax.ShapeDtypeStruct(kv_blocks.shape, keys_values.dtype),
    )
    grad_keys_values = kv_final.transpose(0, 2, 1, 3).reshape(keys_values.shape)
    return (grad_queries, grad_keys_values)


def solution(mesh):
    fine = Mesh(mesh.devices.reshape(mesh.devices.shape[0], 2, 16), ("dp", "xh", "z"))
    tensor = ("xh", "z")
    in_specs = (
        P("dp", None, tensor),
        P("dp", tensor, None),
        P("dp", None, tensor),
        P("dp", None, None),
        P(),
        P("dp", None),
    )
    out_specs = (P("dp", None, tensor), P("dp", tensor, None))
    return jax.shard_map(
        on_device, mesh=fine, in_specs=in_specs, out_specs=out_specs, check_vma=False
    )
```
